32 devices in a mesh: fsdp: 4 (over z), ctx: 8 (over y, x, core).
Axes of the slice: x: 2, y: 2, z: 4, core: 2. Of those that a mesh axis runs over, the one named last changes fastest.
Arguments:
- tokens: bfloat16 [4, 1024, 2048], P('fsdp', 'ctx'), may hold values from -6 to 6
- positions: int32 [4, 1024], P('fsdp', 'ctx'), may hold values from 0 to 1023, as said below
- attn_gain: bfloat16 [2048], P(('fsdp', 'ctx')), may hold values from 0.5 to 1.5
- w_query: bfloat16 [2048, 2048], P(('fsdp', 'ctx')), may hold values from -0.125 to 0.125
- w_key: bfloat16 [2048, 512], P(('fsdp', 'ctx')), may hold values from -0.125 to 0.125
- w_value: bfloat16 [2048, 512], P(('fsdp', 'ctx')), may hold values from -0.125 to 0.125
- w_out: bfloat16 [2048, 2048], P(('fsdp', 'ctx')), may hold values from -2 to 2
- mlp_gain: bfloat16 [2048], P(('fsdp', 'ctx')), may hold values from 0.5 to 1.5
- w_gate: bfloat16 [2048, 8192], P(('fsdp', 'ctx')), may hold values from -0.125 to 0.125
- w_up: bfloat16 [2048, 8192], P(('fsdp', 'ctx')), may hold values from -0.125 to 0.125
- w_down: bfloat16 [8192, 2048], P(('fsdp', 'ctx')), may hold values from -0.125 to 0.125
- cotangent: bfloat16 [4, 1024, 2048], P('fsdp', 'ctx'), may hold values from -6 to 6
Outputs:
- output: bfloat16 [4, 1024, 2048], P('fsdp', 'ctx')
- input_grad: bfloat16 [4, 1024, 2048], P('fsdp', 'ctx')
- attn_gain_grad: float32 [2048], P(('fsdp', 'ctx'))
- query_grad: float32 [2048, 2048], P(('fsdp', 'ctx'))
- key_grad: float32 [2048, 512], P(('fsdp', 'ctx'))
- value_grad: float32 [2048, 512], P(('fsdp', 'ctx'))
- out_grad: float32 [2048, 2048], P(('fsdp', 'ctx'))
- mlp_gain_grad: float32 [2048], P(('fsdp', 'ctx'))
- gate_grad: float32 [2048, 8192], P(('fsdp', 'ctx'))
- up_grad: float32 [2048, 8192], P(('fsdp', 'ctx'))
- down_grad: float32 [8192, 2048], P(('fsdp', 'ctx'))
The draws below stay inside these ranges and needn't reach their ends.
Inputs may be any that keep to these rules, and one draw needn't show every extreme that they name: In each sequence the positions are a permutation of 0 to 1023 made of runs of 64 consecutive rising positions; the order of the runs is drawn afresh for every sequence.
All inputs are finite; a program needn't handle non-finite values.
Results may differ from the reference program's by a relative error of at most 0.023.
Values may be sent and summed in bfloat16 or wider, within the bound.
No kernel may reach another device: no remote copies, remote signals or barrier semaphores. Data moves between devices by JAX's collectives and lax.ppermute only.
A program may use at most 384 MiB of HBM per device.

```python
import jax
import jax.numpy as jnp
from jax import lax

D = 2048
HEADS = 32
KV_HEADS = 8
HEAD_DIM = 64
FF = 8192
TOK_DEV = 128
LENGTH = 1024
SEQS = 4


def draw_positions(key, part):
    key = jax.random.fold_in(key, 11)
    run_length = TOK_DEV // 2
    run_count = LENGTH // run_length
    seq_keys = jax.random.split(key, SEQS)
    orders = jax.vmap(lambda single: jax.random.permutation(single, run_count))(seq_keys).astype(jnp.int32)
    offsets = jnp.arange(run_length, dtype=jnp.int32)
    return (orders[:, :, None] * run_length + offsets[None, None, :]).reshape(SEQS, LENGTH)


def shard_levels(own_key, dims, shards, smallest, high):
    gain = 1.0
    for dim, parts in shards:
        steps = jax.random.uniform(jax.random.fold_in(jax.random.fold_in(own_key, 6), dim), (parts,), jnp.float32, smallest / len(shards), high / len(shards))
        gain = gain * jnp.repeat(jnp.exp(steps), dims[dim] // parts).reshape((-1,) + (1,) * (len(dims) - 1 - dim))
    return gain


def scatter_about(stream_key, extent, deviation, bound, cuts=(), held_as=jnp.bfloat16):
    entries = jax.random.normal(stream_key, extent, jnp.float32) * deviation
    if len(cuts) > 0:
        entries = shard_levels(stream_key, extent, cuts, -0.22, 0.18) * entries
    return jnp.clip(entries, min=-bound, max=bound).astype(held_as)


def setup_inputs(seed: int = 0) -> dict:
    key_list = jax.random.split(jax.random.key(seed), 13)
    return {
        "tokens": scatter_about(key_list[0], (SEQS, LENGTH, D), 1.0, 6.0, ((0, 4), (1, 8))),
        "positions": draw_positions(jax.random.fold_in(key_list[12], 71), 0),
        "attn_gain": jnp.clip(1.0 + 0.1 * jax.random.normal(key_list[2], (D,), jnp.float32), 0.5, 1.5).astype(jnp.bfloat16),
        "w_query": scatter_about(key_list[3], (D, HEADS * HEAD_DIM), D ** -0.5, 0.125, ((0, 32),)),
        "w_key": scatter_about(key_list[4], (D, KV_HEADS * HEAD_DIM), D ** -0.5, 0.125, ((0, 32),)),
        "w_value": scatter_about(key_list[5], (D, KV_HEADS * HEAD_DIM), D ** -0.5, 0.125, ((0, 32),)),
        "w_out": scatter_about(key_list[6], (HEADS * HEAD_DIM, D), (max(1, 4 * D // LENGTH)) ** -0.5, 2.0, ((0, 32),)),
        "mlp_gain": jnp.clip(1.0 + 0.1 * jax.random.normal(key_list[7], (D,), jnp.float32), 0.5, 1.5).astype(jnp.bfloat16),
        "w_gate": scatter_about(key_list[8], (D, FF), D ** -0.5, 0.125, ((0, 32),)),
        "w_up": scatter_about(key_list[9], (D, FF), D ** -0.5, 0.125, ((0, 32),)),
        "w_down": scatter_about(key_list[10], (FF, D), (FF // 4) ** -0.5, 0.125, ((0, 32),)),
        "cotangent": scatter_about(key_list[11], (SEQS, LENGTH, D), 1.0, 6.0, ((0, 4), (1, 8))),
    }


EPSILON = 1e-05
ROPE_BASE = 500000.0
HIGHEST_PREC = lax.Precision.HIGHEST

@jax.custom_vjp
def low(v):
    return lax.optimization_barrier(v.astype(jnp.bfloat16)).astype(jnp.float32)

@jax.custom_vjp
def low_back(v):
    return v

def low_keep(v):
    return (low(v), None)

def low_pass(kept, grad):
    return (grad,)

def back_keep(v):
    return (v, None)

def back_low(kept, grad):
    return (low(grad),)
low.defvjp(low_keep, low_pass)
low_back.defvjp(back_keep, back_low)

def rotate(features, places, direction):
    half_dim = features.shape[-1] // 2
    frequency = jnp.power(ROPE_BASE, -2.0 * jnp.arange(half_dim, dtype=jnp.float32) / features.shape[-1])
    angles = places.astype(jnp.float32)[:, None] * frequency[None, :]
    cosine = jnp.cos(angles)[:, None, :]
    sine_part = direction * jnp.sin(angles)[:, None, :]
    first_half = features[..., :half_dim]
    second_half = features[..., half_dim:]
    return jnp.concatenate([first_half * cosine - second_half * sine_part, second_half * cosine + first_half * sine_part], axis=-1)

def attend_block(query_block, query_places, key_rot, value_heads, key_places):
    scores = low_back(jnp.einsum('bkgd,lkd->kgbl', query_block, key_rot, precision=HIGHEST_PREC) * HEAD_DIM ** (-0.5))
    visible = key_places[None, :] <= query_places[:, None]
    probs_block = jax.nn.softmax(jnp.where(visible, scores, -1e+30), axis=-1)
    mixed_block = jnp.einsum('kgbl,lkd->bkgd', low(probs_block), value_heads, precision=HIGHEST_PREC)
    return mixed_block.reshape(query_block.shape[0], HEADS * HEAD_DIM)

def layer_forward(features, places, params):
    attn_gain, w_query, w_key, w_value, w_out, mlp_gain, w_gate, w_up, w_down = params
    length = features.shape[0]
    group_size = HEADS // KV_HEADS
    inv_first = lax.rsqrt(lax.optimization_barrier(jnp.mean(features * features, axis=-1, keepdims=True)) + EPSILON)
    normed = low(features * inv_first * attn_gain)
    query_proj = low_back(jnp.dot(normed, w_query, precision=HIGHEST_PREC))
    key_proj = low_back(jnp.dot(normed, w_key, precision=HIGHEST_PREC))
    value_proj = low_back(low(jnp.dot(normed, w_value, precision=HIGHEST_PREC)))
    query_rot = low(rotate(query_proj.reshape(length, HEADS, HEAD_DIM), places, 1.0))
    query_rot = query_rot.reshape(length, KV_HEADS, group_size, HEAD_DIM)
    key_rot = low(rotate(key_proj.reshape(length, KV_HEADS, HEAD_DIM), places, 1.0))
    value_heads = value_proj.reshape(length, KV_HEADS, HEAD_DIM)
    blocks = length // TOK_DEV
    mapped = lax.map(jax.checkpoint(lambda paired: attend_block(paired[0], paired[1], key_rot, value_heads, places)), (query_rot.reshape(blocks, TOK_DEV, KV_HEADS, group_size, HEAD_DIM), places.reshape(blocks, TOK_DEV)))
    attn_mixed = low_back(low(mapped.reshape(length, HEADS * HEAD_DIM)))
    hidden = features + low_back(jnp.dot(attn_mixed, w_out, precision=HIGHEST_PREC))
    inv_second = lax.rsqrt(lax.optimization_barrier(jnp.mean(hidden * hidden, axis=-1, keepdims=True)) + EPSILON)
    normed_second = low(hidden * inv_second * mlp_gain)
    gate_proj = low_back(jnp.dot(normed_second, w_gate, precision=HIGHEST_PREC))
    up_proj = low_back(jnp.dot(normed_second, w_up, precision=HIGHEST_PREC))
    activated = low(jax.nn.silu(gate_proj) * up_proj)
    return hidden + jnp.dot(activated, w_down, precision=HIGHEST_PREC)

def reference(tokens, positions, attn_gain, w_query, w_key, w_value, w_out, mlp_gain, w_gate, w_up, w_down, cotangent):
    params = (attn_gain.astype(jnp.float32), w_query.astype(jnp.float32), w_key.astype(jnp.float32), w_value.astype(jnp.float32), w_out.astype(jnp.float32), mlp_gain.astype(jnp.float32), w_gate.astype(jnp.float32), w_up.astype(jnp.float32), w_down.astype(jnp.float32))
    all_tokens = tokens.astype(jnp.float32)

    def forward(inputs, weights):
        return lax.map(jax.checkpoint(lambda paired: layer_forward(paired[0], paired[1], weights)), (inputs, positions))
    result, pullback = jax.vjp(forward, all_tokens, params)
    input_grad, grads = pullback(cotangent.astype(jnp.float32))
    return (result.astype(jnp.bfloat16), input_grad.astype(jnp.bfloat16), grads[0], grads[1], grads[2], grads[3], grads[4], grads[5], grads[6], grads[7], grads[8])
```

```python
import functools

import jax
import jax.numpy as jnp
from jax import lax
from jax.experimental import pallas as pl
from jax.experimental.pallas import tpu as pltpu
from jax.sharding import PartitionSpec as P

HEADS = 32
KV_HEADS = 8
HEAD_DIM = 64
EPSILON = 1e-05
ROPE_BASE = 500000.0
LOW = jnp.bfloat16
WIDE = jnp.float32


def dot(left, right, dims=((1,), (0,)), out=WIDE):
    return lax.dot_general(left, right, (dims, ((), ())), preferred_element_type=WIDE).astype(out)


def swap(block, axis, mask):
    count = lax.axis_size(axis)
    return lax.ppermute(block, axis, [(i, i ^ mask) for i in range(count)])


def pick(stack, index):
    return lax.dynamic_index_in_dim(stack, index, 0, keepdims=False)


def in_order(pieces, base):
    out = jnp.zeros((len(pieces),) + pieces[0].shape, pieces[0].dtype)
    for r, piece in enumerate(pieces):
        out = lax.dynamic_update_index_in_dim(out, piece, base ^ r, 0)
    return out


def ctx_order(count):
    order = [0]
    bit = 2
    while bit < count:
        order = order + [k ^ bit for k in order]
        bit *= 2
    return order + [k ^ 1 for k in order]


def gather_ctx(block):
    count = lax.axis_size("ctx")
    if count == 8:
        near_x, near_y = swap(block, "ctx", 2), swap(block, "ctx", 4)
        half = block.shape[0] // 2
        far_top = swap(near_y[:half], "ctx", 2)
        far_low = swap(near_x[half:], "ctx", 4)
        quad = jnp.concatenate([block, near_x, near_y, far_top, far_low], axis=0)
    else:
        quad = block
        bit = 2
        while bit < count:
            quad = jnp.concatenate([quad, swap(quad, "ctx", bit)], axis=0)
            bit *= 2
    return jnp.concatenate([quad, swap(quad, "ctx", 1)], axis=0)


def scatter_ctx(partial):
    count = lax.axis_size("ctx")
    middle = partial.shape[0] // 2
    quad = partial[:middle].astype(WIDE) + swap(partial[middle:], "ctx", 1).astype(WIDE)
    rows = partial.shape[0] // count
    if count == 8:
        half = rows // 2
        quad = quad.astype(LOW)
        own, to_x, to_y, far = (quad[j * rows : (j + 1) * rows] for j in range(4))
        by_x = swap(jnp.concatenate([to_x[half:], far[half:]], axis=0), "ctx", 2)
        by_y = swap(jnp.concatenate([to_y[:half], far[:half]], axis=0), "ctx", 4)
        last_x = swap((to_x[:half].astype(WIDE) + by_y[half:].astype(WIDE)).astype(LOW), "ctx", 2)
        last_y = swap((to_y[half:].astype(WIDE) + by_x[half:].astype(WIDE)).astype(LOW), "ctx", 4)
        top = own[:half].astype(WIDE) + last_x.astype(WIDE) + by_y[:half].astype(WIDE)
        low = own[half:].astype(WIDE) + by_x[:half].astype(WIDE) + last_y.astype(WIDE)
        return jnp.concatenate([top, low], axis=0)
    bit = count // 2
    while bit >= 2:
        middle = quad.shape[0] // 2
        quad = quad[:middle] + swap(quad[middle:].astype(LOW), "ctx", bit).astype(WIDE)
        bit //= 2
    return quad


def exchange_ctx(stack):
    return lax.all_to_all(stack, "ctx", 0, 0, tiled=True)


def gather_fsdp(block, base):
    count = lax.axis_size("fsdp")
    return in_order([block] + [swap(block, "fsdp", r) for r in range(1, count)], base)


def scatter_fsdp(stack, base):
    count = lax.axis_size("fsdp")
    total = pick(stack, base).astype(WIDE)
    for r in range(1, count):
        total = total + swap(pick(stack, base ^ r), "fsdp", r).astype(WIDE)
    return total


def turned(block, cosine, sine):
    lane = lax.broadcasted_iota(jnp.int32, block.shape, 1)
    first = (lane % HEAD_DIM) < HEAD_DIM // 2
    width = block.shape[1]
    other = jnp.where(
        first, pltpu.roll(block, width - HEAD_DIM // 2, 1), pltpu.roll(block, HEAD_DIM // 2, 1)
    )
    return block * cosine + other * sine


def forward_kernel(
    heads, q_ref, kv_ref, cos_ref, sin_ref, cosk_ref, sink_ref, row_ref, col_ref,
    mixed_ref, lse_ref, qs_ref, kr_ref, vl_ref, vt_ref,
):
    @pl.when(pl.program_id(0) == 0)
    def _():
        keys = turned(kv_ref[...], cosk_ref[...], sink_ref[...])
        kr_ref[...] = keys[:, :HEAD_DIM].astype(LOW)
        values = kv_ref[...][:, HEAD_DIM:].astype(LOW)
        vl_ref[...] = values
        vt_ref[...] = values.astype(WIDE).T.astype(LOW)

    cosine, sine = cos_ref[...], sin_ref[...]
    keys = kr_ref[...]
    values_t = vt_ref[...]
    visible = col_ref[...] <= row_ref[...]
    scale = HEAD_DIM ** (-0.5)
    mixed, totals = [], []
    for pair in range(heads // 2):
        both = turned(q_ref[:, pair * 128 : pair * 128 + 128], cosine, sine)
        both = (both.astype(LOW).astype(WIDE) * scale).astype(LOW)
        qs_ref[:, pair * 128 : pair * 128 + 128] = both
        for side in range(2):
            query = both[:, side * HEAD_DIM : (side + 1) * HEAD_DIM]
            scores = jnp.where(visible, dot(keys, query, ((1,), (1,))), -1e30)
            top = jnp.max(scores, axis=0, keepdims=True)
            weights = jnp.exp(scores - top)
            total = jnp.sum(weights, axis=0, keepdims=True)
            out = dot(values_t, weights.astype(LOW)) / total
            mixed.append(out)
            totals.append(top + jnp.log(total))
    mixed_ref[...] = jnp.concatenate(mixed, axis=0).T.astype(LOW)
    pad = [jnp.zeros_like(totals[0])] * (8 - heads)
    lse_ref[...] = jnp.concatenate(totals + pad, axis=0)


def backward_kernel(
    heads, steps, q_ref, k_ref, v_ref, do_ref, lse_ref, cos_ref, sin_ref, cosk_ref, sink_ref,
    row_ref, col_ref, dq_ref, dkv_ref, kt_ref, dk_ref, dv_ref,
):
    @pl.when(pl.program_id(0) == 0)
    def _():
        kt_ref[...] = k_ref[...].astype(WIDE).T.astype(LOW)
        dk_ref[...] = jnp.zeros_like(dk_ref)
        dv_ref[...] = jnp.zeros_like(dv_ref)

    keys, values, keys_t = k_ref[...], v_ref[...], kt_ref[...]
    visible = col_ref[...] <= row_ref[...]
    scale = HEAD_DIM ** (-0.5)
    grads = []
    for head in range(heads):
        lanes = slice(head * HEAD_DIM, (head + 1) * HEAD_DIM)
        query, grad_out = q_ref[:, lanes], do_ref[:, lanes]
        scores = dot(keys, query, ((1,), (1,)))
        probs = jnp.where(visible, jnp.exp(scores - lse_ref[head : head + 1, :]), 0.0)
        grad_probs = dot(values, grad_out, ((1,), (1,)))
        product = probs * grad_probs
        delta = jnp.sum(product, axis=0, keepdims=True)
        grad_scores = (product - probs * delta).astype(LOW)
        dv_ref[...] += dot(probs.astype(LOW), grad_out)
        dk_ref[...] += dot(grad_scores, query)
        grads.append(dot(keys_t, grad_scores) * scale)
    grad_q = jnp.concatenate(grads, axis=0).T
    cosine, sine = cos_ref[...], sin_ref[...]
    for pair in range(heads // 2):
        lanes = slice(pair * 128, pair * 128 + 128)
        dq_ref[:, lanes] = turned(grad_q[:, lanes], cosine, -sine).astype(LOW)

    @pl.when(pl.program_id(0) == steps - 1)
    def _():
        both = jnp.concatenate([dk_ref[...], dv_ref[...]], axis=1)
        back = turned(both, cosk_ref[...], -sink_ref[...])
        lane = lax.broadcasted_iota(jnp.int32, both.shape, 1)
        dkv_ref[...] = jnp.where(lane < HEAD_DIM, back, both).astype(LOW)


VMEM_LIMIT = 56 * 1024 * 1024


def attention_forward(qkv, cosine, sine, places, heads):
    length = qkv.shape[0]
    width = heads * HEAD_DIM
    block = min(256, length)
    whole = lambda shape: pl.BlockSpec(shape, lambda i: (0,) * len(shape))
    rows = lambda columns: pl.BlockSpec((block, columns), lambda i: (i, 0))
    flops = 4 * heads * length * length * HEAD_DIM
    return pl.pallas_call(
        functools.partial(forward_kernel, heads),
        grid=(length // block,),
        in_specs=[
            rows(width),
            pl.BlockSpec((length, 128), lambda i: (0, width // 128)),
            rows(128), rows(128), whole((length, 128)), whole((length, 128)),
            pl.BlockSpec((1, block), lambda i: (0, i)), whole((length, 1)),
        ],
        out_specs=[
            rows(width), pl.BlockSpec((8, block), lambda i: (0, i)), rows(width),
            whole((length, HEAD_DIM)), whole((length, HEAD_DIM)),
        ],
        out_shape=[
            jax.ShapeDtypeStruct((length, width), LOW),
            jax.ShapeDtypeStruct((8, length), WIDE),
            jax.ShapeDtypeStruct((length, width), LOW),
            jax.ShapeDtypeStruct((length, HEAD_DIM), LOW),
            jax.ShapeDtypeStruct((length, HEAD_DIM), LOW),
        ],
        scratch_shapes=[pltpu.VMEM((HEAD_DIM, length), LOW)],
        compiler_params=pltpu.CompilerParams(
            dimension_semantics=("arbitrary",), vmem_limit_bytes=VMEM_LIMIT
        ),
        cost_estimate=pl.CostEstimate(
            flops=flops * 2, bytes_accessed=8 * length * width, transcendentals=heads * length * length
        ),
        name="attention_forward",
    )(qkv, qkv, cosine, sine, cosine, sine, places[None, :], places[:, None])


def attention_backward(q_scaled, k_rot, v_low, grad_mixed, lse, cosine, sine, places, heads):
    length = q_scaled.shape[0]
    width = heads * HEAD_DIM
    block = min(256, length)
    steps = length // block
    whole = lambda shape: pl.BlockSpec(shape, lambda i: (0,) * len(shape))
    rows = lambda columns: pl.BlockSpec((block, columns), lambda i: (i, 0))
    flops = 10 * heads * length * length * HEAD_DIM
    return pl.pallas_call(
        functools.partial(backward_kernel, heads, steps),
        grid=(steps,),
        in_specs=[
            rows(width), whole((length, HEAD_DIM)), whole((length, HEAD_DIM)), rows(width),
            pl.BlockSpec((8, block), lambda i: (0, i)),
            rows(128), rows(128), whole((length, 128)), whole((length, 128)),
            pl.BlockSpec((1, block), lambda i: (0, i)), whole((length, 1)),
        ],
        out_specs=[rows(width), whole((length, 128))],
        out_shape=[
            jax.ShapeDtypeStruct((length, width), LOW),
            jax.ShapeDtypeStruct((length, 128), LOW),
        ],
        scratch_shapes=[
            pltpu.VMEM((HEAD_DIM, length), LOW),
            pltpu.VMEM((length, HEAD_DIM), WIDE),
            pltpu.VMEM((length, HEAD_DIM), WIDE),
        ],
        compiler_params=pltpu.CompilerParams(
            dimension_semantics=("arbitrary",), vmem_limit_bytes=VMEM_LIMIT
        ),
        cost_estimate=pl.CostEstimate(
            flops=flops * 2, bytes_accessed=8 * length * width, transcendentals=heads * length * length
        ),
        name="attention_backward",
    )(
        q_scaled, k_rot, v_low, grad_mixed, lse, cosine, sine, cosine, sine,
        places[None, :], places[:, None],
    )


def inverse_rms(rows):
    return lax.rsqrt(jnp.mean(rows * rows, axis=-1, keepdims=True) + EPSILON)


def norm_back(grad_hat, hat_rows, inv_rms):
    return inv_rms * (grad_hat - hat_rows * jnp.mean(grad_hat * hat_rows, axis=-1, keepdims=True))


def per_device(
    tokens, positions, attn_gain, w_query, w_key, w_value, w_out,
    mlp_gain, w_gate, w_up, w_down, cotangent,
):
    f_count, c_count = lax.axis_size("fsdp"), lax.axis_size("ctx")
    f_index, c_index = lax.axis_index("fsdp"), lax.axis_index("ctx")
    f_side, f_high = f_index % 2, f_index // 2
    groups = f_count // 2
    own_tokens, own_cot = tokens[0], cotangent[0]
    tok_rows, width = own_tokens.shape
    piece = w_query.shape[0]
    heads = HEADS // c_count
    q_width = heads * HEAD_DIM
    qkv_width = q_width + 2 * HEAD_DIM
    kv_share = max(1, c_count // KV_HEADS)
    ff_width = w_gate.shape[1]
    ff_block = w_down.shape[0]

    gains = jnp.concatenate([attn_gain, mlp_gain]).astype(WIDE)
    gains = gather_fsdp(gains, f_index).reshape(-1)
    small = lax.all_gather(
        jnp.concatenate([gains, positions[0].astype(WIDE)])[None], "ctx", axis=0, tiled=True
    )
    both_gains = small[:, : gains.shape[0]].reshape(c_count, f_count, 2, piece)
    both_gains = both_gains.transpose(2, 1, 0, 3).reshape(2, width)
    gain_first, gain_second = both_gains[0], both_gains[1]
    order = jnp.array(ctx_order(c_count), jnp.int32) ^ c_index
    places = jnp.take(small[:, gains.shape[0] :], order, axis=0).reshape(-1)
    length = places.shape[0]
    half_dim = HEAD_DIM // 2
    frequency = jnp.power(ROPE_BASE, -2.0 * jnp.arange(half_dim, dtype=WIDE) / HEAD_DIM)
    angles = places[:, None] * frequency[None, :]
    cosine, sine = jnp.cos(angles), jnp.sin(angles)
    cosine = jnp.concatenate([cosine] * 4, axis=1)
    sine = jnp.concatenate([-sine, sine, -sine, sine], axis=1)
    int_places = places.astype(jnp.int32)

    shares = [
        w_query.reshape(piece, c_count, q_width),
        jnp.repeat(w_key.reshape(piece, KV_HEADS, HEAD_DIM), kv_share, axis=1),
        jnp.repeat(w_value.reshape(piece, KV_HEADS, HEAD_DIM), kv_share, axis=1),
    ]
    qkv_piece = jnp.concatenate(shares, axis=2).transpose(1, 0, 2)
    qkv_piece = exchange_ctx(qkv_piece).reshape(c_count * piece, qkv_width)
    w_qkv = gather_fsdp(qkv_piece, f_index).reshape(width, qkv_width)
    devices = f_count * c_count
    out_route = [(f_count * c + j, j * c_count + c) for c in range(c_count) for j in range(f_count)]
    out_piece = lax.ppermute(w_out, ("fsdp", "ctx"), out_route)
    w_out_rows = gather_fsdp(out_piece, f_index).reshape(q_width, width)

    all_tokens = gather_ctx(own_tokens)
    wide_tokens = all_tokens.astype(WIDE)
    normed_first = (wide_tokens * inverse_rms(wide_tokens) * gain_first).astype(LOW)
    qkv = dot(normed_first, w_qkv)
    mixed, lse, q_scaled, k_rot, v_low = attention_forward(qkv, cosine, sine, int_places, heads)
    inputs = own_tokens.astype(WIDE)
    inv_first = inverse_rms(inputs)
    hat_first = inputs * inv_first
    hidden = inputs + scatter_ctx(dot(mixed, w_out_rows, out=LOW))
    inv_second = inverse_rms(hidden)
    hat_second = hidden * inv_second
    normed_own = (hat_second * gain_second).astype(LOW)

    def my_columns(weight):
        split = weight.reshape(piece, groups, 2, c_count, ff_block).transpose(2, 3, 0, 1, 4)
        mine = pick(split, f_side)
        theirs = swap(pick(split, 1 - f_side), "fsdp", 1)
        return jnp.stack([mine, theirs], axis=1)

    gate_up = jnp.stack([my_columns(w_gate), my_columns(w_up)], axis=3)
    gate_up = exchange_ctx(gate_up)
    gate_up = gate_up.transpose(1, 0, 2, 3, 4, 5)
    local = groups * ff_block
    gate_up = gate_up.reshape(2, c_count * piece, 2 * local)
    gate_up = [gate_up] + [swap(gate_up, "fsdp", 2 * r) for r in range(1, groups)]
    gate_up = in_order([g[s] for g in gate_up for s in range(2)], f_index)
    gate_up = gate_up.reshape(width, 2 * local)
    down_rows = [w_down] + [swap(w_down, "fsdp", 2 * r) for r in range(1, groups)]
    down_rows = in_order(down_rows, f_high).reshape(local, width)

    def gather_pair(block):
        return gather_ctx(block), gather_ctx(swap(block, "fsdp", 1))

    def scatter_pair(first, second):
        return scatter_ctx(first) + swap(scatter_ctx(second).astype(LOW), "fsdp", 1).astype(WIDE)

    cots = gather_pair(own_cot)
    norms = gather_pair(normed_own)
    down_terms, norm_terms, acts, lows = [], [], [], []
    for cot, normed in zip(cots, norms):
        grad_act = dot(cot, down_rows, ((1,), (1,)))
        projected = dot(normed, gate_up)
        gate, up = projected[:, :local], projected[:, local:]
        sig = jax.nn.sigmoid(gate)
        acts.append((gate * sig * up).astype(LOW))
        gate_low = grad_act * up * sig * (1.0 + gate * (1.0 - sig))
        up_low = grad_act * gate * sig
        lows.append(jnp.concatenate([gate_low, up_low], axis=1).astype(LOW))
        norm_terms.append(dot(lows[-1], gate_up, ((1,), (1,)), LOW))
        down_terms.append(dot(acts[-1], down_rows, out=LOW))
    grad_normed = scatter_pair(*norm_terms)
    output = hidden + scatter_pair(*down_terms)
    down_part = dot(acts[0], cots[0], ((0,), (0,))) + dot(acts[1], cots[1], ((0,), (0,)))
    gate_up_part = dot(norms[0], lows[0], ((0,), (0,))) + dot(norms[1], lows[1], ((0,), (0,)))

    down_part = down_part.astype(LOW).reshape(groups, ff_block, width)
    down_grad = pick(down_part, f_high).astype(WIDE)
    for r in range(1, groups):
        down_grad = down_grad + swap(pick(down_part, f_high ^ r), "fsdp", 2 * r).astype(WIDE)
    gate_up_part = gate_up_part.astype(LOW).reshape(groups, 2, c_count * piece, 2 * local)
    gate_up_sum = pick(gate_up_part, f_high).astype(WIDE)
    for r in range(1, groups):
        gate_up_sum = gate_up_sum + swap(pick(gate_up_part, f_high ^ r), "fsdp", 2 * r).astype(WIDE)
    gate_up_sum = gate_up_sum.astype(LOW)
    gate_up_sum = gate_up_sum.reshape(2, c_count, piece, 2 * local).transpose(1, 0, 2, 3)
    gate_up_sum = exchange_ctx(gate_up_sum).transpose(1, 0, 2, 3)
    sides = in_order([pick(gate_up_sum, f_side), swap(pick(gate_up_sum, 1 - f_side), "fsdp", 1)], f_side)
    sides = sides.reshape(2, c_count, piece, 2, groups, ff_block).transpose(3, 2, 4, 0, 1, 5)
    sides = sides.reshape(2, piece, ff_width).astype(WIDE)
    gate_grad, up_grad = sides[0], sides[1]
    mlp_gain_grad = jnp.sum(
        gate_grad * w_gate.astype(WIDE) + up_grad * w_up.astype(WIDE), axis=1
    ) / mlp_gain.astype(WIDE)

    grad_hidden = own_cot.astype(WIDE) + norm_back(grad_normed * gain_second, hat_second, inv_second)
    all_hidden = gather_ctx(grad_hidden.astype(LOW))
    grad_mixed = dot(all_hidden, w_out_rows, ((1,), (1,)), LOW)
    out_part = dot(mixed, all_hidden, ((0,), (0,)), LOW).reshape(f_count, piece, width)
    grad_q, grad_kv = attention_backward(
        q_scaled, k_rot, v_low, grad_mixed, lse, cosine, sine, int_places, heads
    )
    grad_qkv = jnp.concatenate([grad_q, grad_kv], axis=1)
    grad_normed = scatter_ctx(dot(grad_qkv, w_qkv, ((1,), (1,)), LOW))
    input_grad = grad_hidden + norm_back(grad_normed * gain_first, hat_first, inv_first)

    out_sum = scatter_fsdp(out_part, f_index).astype(LOW)
    out_grad = lax.ppermute(out_sum, ("fsdp", "ctx"), [(d, s) for s, d in out_route]).astype(WIDE)
    qkv_part = dot(normed_first, grad_qkv, ((0,), (0,)), LOW)
    qkv_sum = scatter_fsdp(qkv_part.reshape(f_count, c_count * piece, qkv_width), f_index)
    qkv_sum = exchange_ctx(qkv_sum.astype(LOW).reshape(c_count, piece, qkv_width))
    qkv_sum = qkv_sum.astype(WIDE)
    query_grad = qkv_sum[:, :, :q_width].transpose(1, 0, 2).reshape(piece, -1)
    kv_sum = qkv_sum[:, :, q_width:].reshape(KV_HEADS, kv_share, piece, 2, HEAD_DIM).sum(axis=1)
    key_grad = kv_sum[:, :, 0].transpose(1, 0, 2).reshape(piece, -1)
    value_grad = kv_sum[:, :, 1].transpose(1, 0, 2).reshape(piece, -1)
    attn_gain_grad = (
        jnp.sum(query_grad * w_query.astype(WIDE), axis=1)
        + jnp.sum(key_grad * w_key.astype(WIDE), axis=1)
        + jnp.sum(value_grad * w_value.astype(WIDE), axis=1)
    ) / attn_gain.astype(WIDE)

    return (
        output.astype(LOW)[None],
        input_grad.astype(LOW)[None],
        attn_gain_grad,
        query_grad,
        key_grad,
        value_grad,
        out_grad,
        mlp_gain_grad,
        gate_grad,
        up_grad,
        down_grad,
    )


def solution(mesh):
    rows = P(("fsdp", "ctx"), None)
    vector = P(("fsdp", "ctx"))
    tokens = P("fsdp", "ctx", None)
    in_specs = (
        tokens, P("fsdp", "ctx"), vector, rows, rows, rows, rows, vector, rows, rows, rows, tokens,
    )
    out_specs = (
        tokens, tokens, vector, rows, rows, rows, rows, vector, rows, rows, rows,
    )
    return jax.shard_map(
        per_device, mesh=mesh, in_specs=in_specs, out_specs=out_specs, check_vma=False
    )
```

```python
import functools

import jax
import jax.numpy as jnp
from jax import lax
from jax.experimental import pallas as pl
from jax.experimental.pallas import tpu as pltpu
from jax.sharding import PartitionSpec as P

HEADS = 32
KV_HEADS = 8
HEAD_DIM = 64
EPSILON = 1e-05
ROPE_BASE = 500000.0
VMEM_LIMIT = 56 * 1024 * 1024
LOW = jnp.bfloat16
WIDE = jnp.float32


def dot(left, right, dims=((1,), (0,)), out=WIDE):
    return lax.dot_general(left, right, (dims, ((), ())), preferred_element_type=WIDE).astype(out)


def tie(*values):
    return lax.optimization_barrier(values)


def swap(block, axis, mask):
    count = lax.axis_size(axis)
    return lax.ppermute(block, axis, [(i, i ^ mask) for i in range(count)])


def pick(stack, index):
    return lax.dynamic_index_in_dim(stack, index, 0, keepdims=False)


def in_order(pieces, base):
    out = jnp.zeros((len(pieces),) + pieces[0].shape, pieces[0].dtype)
    for r, piece in enumerate(pieces):
        out = lax.dynamic_update_index_in_dim(out, piece, base ^ r, 0)
    return out


def ctx_order(count):
    order = [0]
    bit = 2
    while bit < count:
        order = order + [k ^ bit for k in order]
        bit *= 2
    return order + [k ^ 1 for k in order]


def gather_near(block):
    count = lax.axis_size("ctx")
    return (swap(block, "ctx", 2), swap(block, "ctx", 4)) if count == 8 else ()


def gather_far(block, near):
    count = lax.axis_size("ctx")
    if count == 8:
        near_x, near_y = near
        half = block.shape[0] // 2
        return block, near_x, near_y, swap(near_y[:half], "ctx", 2), swap(near_x[half:], "ctx", 4)
    even, bit = (block,), 2
    while bit < count:
        even = even + tuple(swap(part, "ctx", bit) for part in even)
        bit *= 2
    return even


def gather_core(even):
    quad = jnp.concatenate(even, axis=0)
    return quad, swap(quad, "ctx", 1)


def scatter_core(odd):
    return swap(odd, "ctx", 1)


def scatter_far(even, odd):
    count = lax.axis_size("ctx")
    quad = even.astype(WIDE) + odd.astype(WIDE)
    if count != 8:
        return (quad,)
    quad = quad.astype(LOW)
    rows = quad.shape[0] // 4
    half = rows // 2
    own, to_x, to_y, far = (quad[j * rows : (j + 1) * rows] for j in range(4))
    far_x, far_y = swap(far[half:], "ctx", 2), swap(far[:half], "ctx", 4)
    by_x, by_y = swap(to_x[half:], "ctx", 2), swap(to_y[:half], "ctx", 4)
    return own, to_x[:half], to_y[half:], by_x, by_y, far_x, far_y


def scatter_near(state):
    count = lax.axis_size("ctx")
    if count != 8:
        (quad,) = state
        bit = count // 2
        while bit >= 2:
            middle = quad.shape[0] // 2
            quad = quad[:middle] + swap(quad[middle:].astype(LOW), "ctx", bit).astype(WIDE)
            bit //= 2
        return (quad,)
    own, to_x, to_y, by_x, by_y, far_x, far_y = state
    last_x = swap((to_x.astype(WIDE) + far_y.astype(WIDE)).astype(LOW), "ctx", 2)
    last_y = swap((to_y.astype(WIDE) + far_x.astype(WIDE)).astype(LOW), "ctx", 4)
    return own, by_x, by_y, last_x, last_y


def scatter_end(state):
    if len(state) == 1:
        return state[0]
    own, by_x, by_y, last_x, last_y = state
    half = last_x.shape[0]
    top = own[:half].astype(WIDE) + last_x.astype(WIDE) + by_y.astype(WIDE)
    low = own[half:].astype(WIDE) + by_x.astype(WIDE) + last_y.astype(WIDE)
    return jnp.concatenate([top, low], axis=0)


def exchange_ctx(stack):
    return lax.all_to_all(stack, "ctx", 0, 0, tiled=True)


def double_fsdp(stack, first, last):
    bits, bit = [], first
    while bit >= last:
        bits.append(bit)
        bit //= 2
    for bit in bits:
        stack = jnp.concatenate([stack, swap(stack, "fsdp", bit)], axis=0)
    return stack


def xor_order(first, last):
    order, bit = [0], first
    while bit >= last:
        order = order + [k ^ bit for k in order]
        bit //= 2
    return order


def place_kernel(spots, rows, base_ref, *refs):
    out_ref = refs[-1]
    for (mask, offset), part in zip(spots, refs[:-1]):
        start = pl.multiple_of((base_ref[0] ^ mask) * rows + offset, 16)
        out_ref[pl.ds(start, part.shape[0]), :] = part[...]


def place(parts, base, count):
    columns = parts[0][2].shape[1]
    total = sum(part.shape[0] for _, _, part in parts)
    whole = pl.BlockSpec(memory_space=pltpu.VMEM)
    return pl.pallas_call(
        functools.partial(place_kernel, [(m, o) for m, o, _ in parts], total // count),
        in_specs=[pl.BlockSpec(memory_space=pltpu.SMEM)] + [whole] * len(parts),
        out_specs=whole,
        out_shape=jax.ShapeDtypeStruct((total, columns), parts[0][2].dtype),
        compiler_params=pltpu.CompilerParams(vmem_limit_bytes=VMEM_LIMIT),
        cost_estimate=pl.CostEstimate(flops=0, bytes_accessed=total * columns * 2, transcendentals=0),
        name="place",
    )(base.reshape(1), *[part for _, _, part in parts])


def halve_fsdp(stack, base, first, last):
    bit = first
    while bit >= last:
        low = stack.shape[0] // 2
        side = (base // bit) % 2
        pair = stack.reshape((2, low) + stack.shape[1:])
        mine, theirs = pick(pair, side), pick(pair, 1 - side)
        stack = (mine.astype(WIDE) + swap(theirs, "fsdp", bit).astype(WIDE)).astype(LOW)
        bit //= 2
    return stack if stack.shape[0] > 1 else stack[0]


def halve_near(stack, base):
    pair = stack.reshape((stack.shape[0] // 2, 2) + stack.shape[1:]).swapaxes(0, 1)
    mine, theirs = pick(pair, base % 2), pick(pair, 1 - base % 2)
    return (mine.astype(WIDE) + swap(theirs, "fsdp", 1).astype(WIDE)).astype(LOW)


def halve_far(stack, base, first):
    return halve_fsdp(stack, base, first, 2)


def turned(block, cosine, sine):
    lane = lax.broadcasted_iota(jnp.int32, block.shape, 1)
    first = (lane % HEAD_DIM) < HEAD_DIM // 2
    width = block.shape[1]
    other = jnp.where(
        first, pltpu.roll(block, width - HEAD_DIM // 2, 1), pltpu.roll(block, HEAD_DIM // 2, 1)
    )
    return block * cosine + other * sine


def forward_kernel(
    heads, q_ref, kv_ref, cos_ref, sin_ref, cosk_ref, sink_ref, row_ref, col_ref,
    mixed_ref, lse_ref, qs_ref, kr_ref, vl_ref, vt_ref,
):
    @pl.when(pl.program_id(0) == 0)
    def _():
        keys = turned(kv_ref[...], cosk_ref[...], sink_ref[...])
        kr_ref[...] = keys[:, :HEAD_DIM].astype(LOW)
        values = kv_ref[...][:, HEAD_DIM:].astype(LOW)
        vl_ref[...] = values
        vt_ref[...] = values.astype(WIDE).T.astype(LOW)

    cosine, sine = cos_ref[...], sin_ref[...]
    keys = kr_ref[...]
    values_t = vt_ref[...]
    visible = col_ref[...] <= row_ref[...]
    scale = HEAD_DIM ** (-0.5)
    mixed, totals = [], []
    for pair in range(heads // 2):
        both = turned(q_ref[:, pair * 128 : pair * 128 + 128], cosine, sine)
        both = (both.astype(LOW).astype(WIDE) * scale).astype(LOW)
        qs_ref[:, pair * 128 : pair * 128 + 128] = both
        for side in range(2):
            query = both[:, side * HEAD_DIM : (side + 1) * HEAD_DIM]
            scores = jnp.where(visible, dot(keys, query, ((1,), (1,))), -1e30)
            top = jnp.max(scores, axis=0, keepdims=True)
            weights = jnp.exp(scores - top)
            total = jnp.sum(weights, axis=0, keepdims=True)
            out = dot(values_t, weights.astype(LOW)) / total
            mixed.append(out)
            totals.append(top + jnp.log(total))
    mixed_ref[...] = jnp.concatenate(mixed, axis=0).T.astype(LOW)
    pad = [jnp.zeros_like(totals[0])] * (8 - heads)
    lse_ref[...] = jnp.concatenate(totals + pad, axis=0)


def backward_kernel(
    heads, steps, q_ref, k_ref, v_ref, do_ref, lse_ref, cos_ref, sin_ref, cosk_ref, sink_ref,
    row_ref, col_ref, dq_ref, dkv_ref, kt_ref, dk_ref, dv_ref,
):
    @pl.when(pl.program_id(0) == 0)
    def _():
        kt_ref[...] = k_ref[...].astype(WIDE).T.astype(LOW)
        dk_ref[...] = jnp.zeros_like(dk_ref)
        dv_ref[...] = jnp.zeros_like(dv_ref)

    keys, values, keys_t = k_ref[...], v_ref[...], kt_ref[...]
    visible = col_ref[...] <= row_ref[...]
    scale = HEAD_DIM ** (-0.5)
    grads = []
    for head in range(heads):
        lanes = slice(head * HEAD_DIM, (head + 1) * HEAD_DIM)
        query, grad_out = q_ref[:, lanes], do_ref[:, lanes]
        scores = dot(keys, query, ((1,), (1,)))
        probs = jnp.where(visible, jnp.exp(scores - lse_ref[head : head + 1, :]), 0.0)
        grad_probs = dot(values, grad_out, ((1,), (1,)))
        product = probs * grad_probs
        delta = jnp.sum(product, axis=0, keepdims=True)
        grad_scores = (product - probs * delta).astype(LOW)
        dv_ref[...] += dot(probs.astype(LOW), grad_out)
        dk_ref[...] += dot(grad_scores, query)
        grads.append(dot(keys_t, grad_scores) * scale)
    grad_q = jnp.concatenate(grads, axis=0).T
    cosine, sine = cos_ref[...], sin_ref[...]
    for pair in range(heads // 2):
        lanes = slice(pair * 128, pair * 128 + 128)
        dq_ref[:, lanes] = turned(grad_q[:, lanes], cosine, -sine).astype(LOW)

    @pl.when(pl.program_id(0) == steps - 1)
    def _():
        both = jnp.concatenate([dk_ref[...], dv_ref[...]], axis=1)
        back = turned(both, cosk_ref[...], -sink_ref[...])
        lane = lax.broadcasted_iota(jnp.int32, both.shape, 1)
        dkv_ref[...] = jnp.where(lane < HEAD_DIM, back, both).astype(LOW)


def attention_forward(qkv, cosine, sine, places, heads):
    length = qkv.shape[0]
    width = heads * HEAD_DIM
    block = min(256, length)
    whole = lambda shape: pl.BlockSpec(shape, lambda i: (0,) * len(shape))
    rows = lambda columns: pl.BlockSpec((block, columns), lambda i: (i, 0))
    return pl.pallas_call(
        functools.partial(forward_kernel, heads),
        grid=(length // block,),
        in_specs=[
            rows(width),
            pl.BlockSpec((length, 128), lambda i: (0, width // 128)),
            rows(128), rows(128), whole((length, 128)), whole((length, 128)),
            pl.BlockSpec((1, block), lambda i: (0, i)), whole((length, 1)),
        ],
        out_specs=[
            rows(width), pl.BlockSpec((8, block), lambda i: (0, i)), rows(width),
            whole((length, HEAD_DIM)), whole((length, HEAD_DIM)),
        ],
        out_shape=[
            jax.ShapeDtypeStruct((length, width), LOW),
            jax.ShapeDtypeStruct((8, length), WIDE),
            jax.ShapeDtypeStruct((length, width), LOW),
            jax.ShapeDtypeStruct((length, HEAD_DIM), LOW),
            jax.ShapeDtypeStruct((length, HEAD_DIM), LOW),
        ],
        scratch_shapes=[pltpu.VMEM((HEAD_DIM, length), LOW)],
        compiler_params=pltpu.CompilerParams(
            dimension_semantics=("arbitrary",), vmem_limit_bytes=VMEM_LIMIT
        ),
        cost_estimate=pl.CostEstimate(
            flops=0, bytes_accessed=8 * length * width, transcendentals=0
        ),
        name="attention_forward",
    )(qkv, qkv, cosine, sine, cosine, sine, places[None, :], places[:, None])


def attention_backward(q_scaled, k_rot, v_low, grad_mixed, lse, cosine, sine, places, heads):
    length = q_scaled.shape[0]
    width = heads * HEAD_DIM
    block = min(256, length)
    steps = length // block
    whole = lambda shape: pl.BlockSpec(shape, lambda i: (0,) * len(shape))
    rows = lambda columns: pl.BlockSpec((block, columns), lambda i: (i, 0))
    return pl.pallas_call(
        functools.partial(backward_kernel, heads, steps),
        grid=(steps,),
        in_specs=[
            rows(width), whole((length, HEAD_DIM)), whole((length, HEAD_DIM)), rows(width),
            pl.BlockSpec((8, block), lambda i: (0, i)),
            rows(128), rows(128), whole((length, 128)), whole((length, 128)),
            pl.BlockSpec((1, block), lambda i: (0, i)), whole((length, 1)),
        ],
        out_specs=[rows(width), whole((length, 128))],
        out_shape=[
            jax.ShapeDtypeStruct((length, width), LOW),
            jax.ShapeDtypeStruct((length, 128), LOW),
        ],
        scratch_shapes=[
            pltpu.VMEM((HEAD_DIM, length), LOW),
            pltpu.VMEM((length, HEAD_DIM), WIDE),
            pltpu.VMEM((length, HEAD_DIM), WIDE),
        ],
        compiler_params=pltpu.CompilerParams(
            dimension_semantics=("arbitrary",), vmem_limit_bytes=VMEM_LIMIT
        ),
        cost_estimate=pl.CostEstimate(
            flops=0, bytes_accessed=8 * length * width, transcendentals=0
        ),
        name="attention_backward",
    )(
        q_scaled, k_rot, v_low, grad_mixed, lse, cosine, sine, cosine, sine,
        places[None, :], places[:, None],
    )


def columns_kernel(block, gate_ref, up_ref, scale_ref, out_ref):
    scale = scale_ref[...]
    for j in range(out_ref.shape[0]):
        lanes = slice(j * block, (j + 1) * block)
        out_ref[j, :, :block] = (gate_ref[:, lanes].astype(WIDE) * scale).astype(LOW)
        out_ref[j, :, block:] = (up_ref[:, lanes].astype(WIDE) * scale).astype(LOW)


def columns_by_device(w_gate, w_up, scale, block):
    rows, ff_width = w_gate.shape
    devices = ff_width // block
    if block % 128:
        split = [(w.astype(WIDE) * scale).astype(LOW).reshape(rows, devices, block) for w in (w_gate, w_up)]
        return jnp.concatenate(split, axis=2).transpose(1, 0, 2)
    some = 8
    part = pl.BlockSpec((rows, some * block), lambda d: (0, d))
    return pl.pallas_call(
        functools.partial(columns_kernel, block),
        grid=(devices // some,),
        in_specs=[part, part, pl.BlockSpec((rows, 1), lambda d: (0, 0))],
        out_specs=pl.BlockSpec((some, rows, 2 * block), lambda d: (d, 0, 0)),
        out_shape=jax.ShapeDtypeStruct((devices, rows, 2 * block), LOW),
        cost_estimate=pl.CostEstimate(flops=0, bytes_accessed=2 << 20, transcendentals=0),
        name="columns_by_device",
    )(w_gate, w_up, scale)


def assemble_kernel(part_ref, gate_ref, up_ref, scale_ref, gate_out, up_out, gain_out):
    @pl.when(pl.program_id(0) == 0)
    def _():
        gain_out[...] = jnp.zeros_like(gain_out)

    scale = scale_ref[...]
    block = gate_ref.shape[1] // part_ref.shape[0]
    total = jnp.zeros_like(gain_out)
    for j in range(part_ref.shape[0]):
        lanes = slice(j * block, (j + 1) * block)
        gate = part_ref[j, :, :block].astype(WIDE)
        up = part_ref[j, :, block:].astype(WIDE)
        gate_out[:, lanes] = gate * scale
        up_out[:, lanes] = up * scale
        products = gate * gate_ref[:, lanes].astype(WIDE) + up * up_ref[:, lanes].astype(WIDE)
        total = total + jnp.sum(products, axis=1, keepdims=True)
    gain_out[...] += total


def assemble_columns(parts, w_gate, w_up, scale):
    devices, rows, both = parts.shape
    block = both // 2
    ff_width = w_gate.shape[1]
    if block % 128:
        sides = parts.reshape(devices, rows, 2, block).transpose(2, 1, 0, 3).reshape(2, rows, ff_width)
        sides = sides.astype(WIDE)
        products = sides[0] * w_gate.astype(WIDE) + sides[1] * w_up.astype(WIDE)
        return sides[0] * scale, sides[1] * scale, jnp.sum(products, axis=1, keepdims=True)
    some = 8
    columns = pl.BlockSpec((rows, some * block), lambda d: (0, d))
    one = pl.BlockSpec((rows, 1), lambda d: (0, 0))
    return pl.pallas_call(
        assemble_kernel,
        grid=(devices // some,),
        in_specs=[pl.BlockSpec((some, rows, both), lambda d: (d, 0, 0)), columns, columns, one],
        out_specs=[columns, columns, one],
        out_shape=[
            jax.ShapeDtypeStruct((rows, ff_width), WIDE),
            jax.ShapeDtypeStruct((rows, ff_width), WIDE),
            jax.ShapeDtypeStruct((rows, 1), WIDE),
        ],
        compiler_params=pltpu.CompilerParams(
            dimension_semantics=("arbitrary",), vmem_limit_bytes=VMEM_LIMIT
        ),
        cost_estimate=pl.CostEstimate(flops=0, bytes_accessed=8 << 20, transcendentals=0),
        name="assemble_columns",
    )(parts, w_gate, w_up, scale)


def feed_kernel(blocks, steps, per_step, table_ref, *refs):
    even_ref, odd_ref = refs[:2]
    cot_refs = refs[2 : 2 + per_step]
    weights = refs[2 + per_step : 2 + per_step + blocks]
    downs = refs[2 + per_step + blocks : 2 + per_step + 2 * blocks]
    norm_out, cot_out, act_out, low_out, even_out, odd_out = refs[-6:]
    step = pl.program_id(0)
    norm = jnp.where(step < steps // 2, even_ref[...], odd_ref[...])
    norm_out[...] = norm
    cot = jnp.concatenate([ref[0, 0] for ref in cot_refs], axis=0)
    cot_out[...] = cot
    term = None
    for j in range(blocks):
        rows = dot(norm, weights[j][...])
        grad_act = dot(cot, downs[j][...], ((1,), (1,)))
        width = rows.shape[1] // 2
        gate, up = rows[:, :width], rows[:, width:]
        sig = 1.0 / (1.0 + jnp.exp(-gate))
        gate_sig = gate * sig
        act_out[:, j * width : (j + 1) * width] = (gate_sig * up).astype(LOW)
        grad_up = grad_act * gate_sig
        grad_gate = grad_act * up * (sig + gate_sig * (1.0 - sig))
        low = jnp.concatenate([grad_gate, grad_up], axis=1).astype(LOW)
        low_out[j] = low
        more = dot(low, weights[j][...], ((1,), (1,)))
        term = more if term is None else term + more
    term = term.astype(LOW)

    @pl.when(step < steps // 2)
    def _():
        even_out[...] = term

    @pl.when(step >= steps // 2)
    def _():
        odd_out[...] = term


def feed_forward(which, even, odd, cots, table, weights, downs, earlier):
    half, width = even.shape
    _, c_count, tok_rows, _ = cots.shape
    blocks = len(weights)
    both = weights[0].shape[1]
    block = both // 2
    steps = 4
    rows = 2 * half // steps
    per_step = rows // tok_rows
    total = 4 * half
    first = which * steps
    even_at = lambda i, t: (jnp.minimum(i, steps // 2 - 1), 0)
    odd_at = lambda i, t: (jnp.maximum(i - steps // 2, 0), 0)
    cot_spec = lambda j: pl.BlockSpec(
        (1, 1, tok_rows, width), lambda i, t, j=j: (which, t[i * per_step + j], 0, 0)
    )
    fixed = lambda shape: pl.BlockSpec(shape, lambda i, t: (0,) * len(shape))
    at = lambda i, t: (first + i, 0)
    out_shape = [
        jax.ShapeDtypeStruct((total, width), LOW),
        jax.ShapeDtypeStruct((total, width), LOW),
        jax.ShapeDtypeStruct((total, blocks * block), LOW),
        jax.ShapeDtypeStruct((blocks, total, both), LOW),
        jax.ShapeDtypeStruct((half, width), LOW),
        jax.ShapeDtypeStruct((half, width), LOW),
    ]
    inputs = [even, odd] + [cots] * per_step + list(weights) + list(downs) + list(earlier)
    in_specs = (
        [pl.BlockSpec((rows, width), even_at), pl.BlockSpec((rows, width), odd_at)]
        + [cot_spec(j) for j in range(per_step)]
        + [fixed(w.shape) for w in weights]
        + [fixed(d.shape) for d in downs]
        + [pl.BlockSpec(memory_space=pl.ANY)] * len(earlier)
    )
    aliases = {1 + len(inputs) - len(earlier) + j: j for j in range(len(earlier))}
    return pl.pallas_call(
        functools.partial(feed_kernel, blocks, steps, per_step),
        grid_spec=pltpu.PrefetchScalarGridSpec(
            num_scalar_prefetch=1,
            grid=(steps,),
            in_specs=in_specs,
            out_specs=[
                pl.BlockSpec((rows, width), at),
                pl.BlockSpec((rows, width), at),
                pl.BlockSpec((rows, blocks * block), at),
                pl.BlockSpec((blocks, rows, both), lambda i, t: (0, first + i, 0)),
                pl.BlockSpec((rows, width), even_at),
                pl.BlockSpec((rows, width), odd_at),
            ],
        ),
        out_shape=out_shape,
        input_output_aliases=aliases,
        compiler_params=pltpu.CompilerParams(
            dimension_semantics=("arbitrary",), vmem_limit_bytes=VMEM_LIMIT
        ),
        cost_estimate=pl.CostEstimate(flops=0, bytes_accessed=8 << 20, transcendentals=0),
        name="feed_forward",
    )(table, *inputs)


def down_kernel(blocks, table_ref, act_ref, *refs):
    out_ref, downs = refs[-1], refs[:-1]
    block = act_ref.shape[1] // blocks
    total = None
    for j in range(blocks):
        part = dot(act_ref[:, j * block : (j + 1) * block], downs[j][...])
        total = part if total is None else total + part
    out_ref[0, 0] = total.astype(LOW)


def down_terms_by_device(acts, table, downs, tok_rows):
    total, local = acts.shape
    c_count = table.shape[0]
    width = downs[0].shape[1]
    fixed = lambda shape: pl.BlockSpec(shape, lambda i, j, t: (0,) * len(shape))
    return pl.pallas_call(
        functools.partial(down_kernel, len(downs)),
        grid_spec=pltpu.PrefetchScalarGridSpec(
            num_scalar_prefetch=1,
            grid=(2, c_count),
            in_specs=[pl.BlockSpec((tok_rows, local), lambda i, j, t: (i * c_count + j, 0))]
            + [fixed(d.shape) for d in downs],
            out_specs=pl.BlockSpec((1, 1, tok_rows, width), lambda i, j, t: (t[j], i, 0, 0)),
        ),
        out_shape=jax.ShapeDtypeStruct((c_count, 2, tok_rows, width), LOW),
        compiler_params=pltpu.CompilerParams(vmem_limit_bytes=VMEM_LIMIT),
        cost_estimate=pl.CostEstimate(flops=0, bytes_accessed=8 << 20, transcendentals=0),
        name="down_terms",
    )(table, acts, *downs)


def inverse_rms(rows):
    return lax.rsqrt(jnp.mean(rows * rows, axis=-1, keepdims=True) + EPSILON)


def norm_back(grad_hat, hat_rows, inv_rms):
    return inv_rms * (grad_hat - hat_rows * jnp.mean(grad_hat * hat_rows, axis=-1, keepdims=True))


def per_device(
    tokens, positions, attn_gain, w_query, w_key, w_value, w_out,
    mlp_gain, w_gate, w_up, w_down, cotangent,
):
    f_count, c_count = lax.axis_size("fsdp"), lax.axis_size("ctx")
    f_index, c_index = lax.axis_index("fsdp"), lax.axis_index("ctx")
    devices = f_count * c_count
    top_bit = f_count // 2
    own_tokens, own_cot = tokens[0], cotangent[0]
    tok_rows, width = own_tokens.shape
    piece = w_query.shape[0]
    heads = HEADS // c_count
    q_width = heads * HEAD_DIM
    qkv_width = q_width + 2 * HEAD_DIM
    kv_share = max(1, c_count // KV_HEADS)
    ff_block = w_down.shape[0]
    c_order = ctx_order(c_count)
    f_order = xor_order(top_bit, 1)

    attn_scale, mlp_scale = attn_gain.astype(WIDE)[:, None], mlp_gain.astype(WIDE)[:, None]
    near_tokens = gather_near(own_tokens)
    shares = [
        w_query.reshape(piece, c_count, q_width),
        jnp.repeat(w_key.reshape(piece, KV_HEADS, HEAD_DIM), kv_share, axis=1),
        jnp.repeat(w_value.reshape(piece, KV_HEADS, HEAD_DIM), kv_share, axis=1),
    ]
    qkv_piece = (jnp.concatenate(shares, axis=2).astype(WIDE) * attn_scale[:, :, None]).astype(LOW)
    qkv_piece = qkv_piece.transpose(1, 0, 2)
    qkv_piece, w_gate_in, w_out = tie(qkv_piece, w_gate, w_out)
    qkv_piece = exchange_ctx(qkv_piece).reshape(1, c_count * piece, qkv_width)
    out_route = [(f_count * c + j, j * c_count + c) for c in range(c_count) for j in range(f_count)]
    out_piece = lax.ppermute(w_out, ("fsdp", "ctx"), out_route)
    small = positions
    for bit in [2 ** j for j in range(1, c_count.bit_length() - 1)] + [1]:
        small = jnp.concatenate([small, swap(small, "ctx", bit)], axis=0)
    int_places = small.reshape(-1)
    gate_up = columns_by_device(w_gate_in, w_up, mlp_scale, ff_block)

    qkv_piece, out_piece, near_tokens = tie(qkv_piece, out_piece, near_tokens)
    even_tokens = gather_far(own_tokens, near_tokens)
    qkv_piece = qkv_piece[0]
    qkv_parts = [qkv_piece] + [swap(qkv_piece, "fsdp", r) for r in range(1, f_count)]
    half_dim = HEAD_DIM // 2
    frequency = jnp.power(ROPE_BASE, -2.0 * jnp.arange(half_dim, dtype=WIDE) / HEAD_DIM)
    angles = int_places.astype(WIDE)[:, None] * frequency[None, :]
    cosine, sine = jnp.cos(angles), jnp.sin(angles)
    cosine = jnp.concatenate([cosine] * 4, axis=1)
    sine = jnp.concatenate([-sine, sine, -sine, sine], axis=1)

    out_piece, cosine, sine, even_tokens = tie(out_piece, cosine, sine, even_tokens)
    quad_tokens, other_tokens = gather_core(even_tokens)
    w_out_rows = lax.all_gather(out_piece, "fsdp", axis=0, tiled=True)

    def first_norm(rows):
        rows = rows.astype(WIDE)
        return (rows * inverse_rms(rows)).astype(LOW)

    normed_first = [first_norm(quad_tokens), first_norm(other_tokens)]

    qkv_parts, gate_up, own_cot, normed_first, w_down = tie(
        qkv_parts, gate_up, own_cot, normed_first, w_down
    )
    gate_up = lax.all_to_all(gate_up, ("fsdp", "ctx"), 0, 0, tiled=True)
    side_cot = swap(own_cot, "fsdp", top_bit)
    downs = [w_down] + [swap(w_down, "fsdp", r) for r in range(1, top_bit)]
    w_qkv = place([(r, 0, part) for r, part in enumerate(qkv_parts)], f_index, f_count)
    qkv = jnp.concatenate([dot(rows, w_qkv) for rows in normed_first], axis=0)
    mixed, lse, q_scaled, k_rot, v_low = attention_forward(qkv, cosine, sine, int_places, heads)

    mixed, side_cot, downs = tie(mixed, side_cot, downs)
    cots = lax.all_gather(jnp.stack([own_cot, side_cot], axis=0), "ctx", axis=1, tiled=True)
    middle = mixed.shape[0] // 2
    odd_out = scatter_core(dot(mixed[middle:], w_out_rows, out=LOW))
    even_out = dot(mixed[:middle], w_out_rows, out=LOW)
    state = scatter_far(even_out, odd_out)
    inputs = own_tokens.astype(WIDE)
    inv_first = inverse_rms(inputs)
    hat_first = inputs * inv_first
    state, hat_first, gate_up = tie(state, hat_first, gate_up)
    gate_ups = [gate_up.reshape(width, 2 * ff_block)]
    halves = [gate_ups[0][: width // 2], gate_ups[0][width // 2 :]]
    tops = [swap(halves[0], "fsdp", r) for r in range(1, top_bit)]
    hidden = inputs + scatter_end(scatter_near(state))
    inv_second = inverse_rms(hidden)
    hat_second = hidden * inv_second
    normed_own = hat_second.astype(LOW)

    near_norm = gather_near(normed_own)
    side_norm = swap(normed_own, "fsdp", top_bit)
    near_norm, side_norm, tops, halves = tie(near_norm, side_norm, tops, halves)
    lows = [swap(halves[1], "fsdp", r) for r in range(1, top_bit)]
    even_norm = gather_far(normed_own, near_norm)
    near_side = gather_near(side_norm)
    norm_pieces = list(gather_core(even_norm))
    near_side, norm_pieces, cots, lows = tie(near_side, norm_pieces, cots, lows)
    gate_ups += [jnp.concatenate(parts, axis=0) for parts in zip(tops, lows)]
    even_side = gather_far(side_norm, near_side)
    cots = cots.reshape(2, c_count, tok_rows, width)
    table = jnp.array(c_order, jnp.int32) ^ c_index

    *buffers, even_zero, odd_zero = feed_forward(0, *norm_pieces, cots, table, gate_ups, downs, [])
    even_side, buffers, even_zero, odd_zero = tie(even_side, buffers, even_zero, odd_zero)
    norm_pieces = gather_core(even_side)
    odd_zero = scatter_core(odd_zero)
    state_zero = scatter_far(even_zero, odd_zero)
    norm_pieces, state_zero = tie(norm_pieces, state_zero)
    *buffers, even_one, odd_one = feed_forward(1, *norm_pieces, cots, table, gate_ups, downs, buffers)
    all_norms, all_cots, all_acts, all_lows = buffers
    state_zero, odd_one = tie(state_zero, odd_one)
    odd_one = scatter_core(odd_one)
    state_zero = scatter_near(state_zero)
    state_zero, odd_one = tie(state_zero, odd_one)
    state_one = scatter_far(even_one, odd_one)

    act_of = lambda j: all_acts[:, j * ff_block : (j + 1) * ff_block]
    gate_up_away = [dot(all_norms, all_lows[j], ((0,), (0,)), LOW) for j in range(1, len(downs))]
    state_one, gate_up_away, all_lows = tie(state_one, gate_up_away, all_lows)
    state_one = scatter_near(state_one)
    cut = width // 2
    tops = [swap(part[:cut], "fsdp", r) for r, part in enumerate(gate_up_away, 1)]
    gate_up_own = dot(all_norms, all_lows[0], ((0,), (0,)))
    down_away = [dot(act_of(j), all_cots, ((0,), (0,)), LOW) for j in range(1, len(downs))]
    side_one = swap(scatter_end(state_one).astype(LOW), "fsdp", top_bit)
    side_one, tops, gate_up_away, gate_up_own, down_away = tie(
        side_one, tops, gate_up_away, gate_up_own, down_away
    )
    lows = [swap(part[cut:], "fsdp", r) for r, part in enumerate(gate_up_away, 1)]
    grad_normed = scatter_end(state_zero) + side_one.astype(WIDE)

    grad_hidden = own_cot.astype(WIDE) + norm_back(grad_normed, hat_second, inv_second)
    hidden_low = grad_hidden.astype(LOW)
    near_hidden = gather_near(hidden_low)
    down_terms = down_terms_by_device(all_acts, table, downs, tok_rows)
    near_hidden, down_terms, lows, down_away = tie(near_hidden, down_terms, lows, down_away)
    even_hidden = gather_far(hidden_low, near_hidden)
    out_rows = lax.psum_scatter(down_terms.reshape(-1, width), "ctx", scatter_dimension=0, tiled=True)
    out_rows = out_rows.reshape(2, tok_rows, width)
    received = [jnp.concatenate(parts, axis=0) for parts in zip(tops, lows)]
    gate_up_sum = sum([part.astype(WIDE) for part in received], gate_up_own).astype(LOW)
    even_hidden, gate_up_sum = tie(even_hidden, gate_up_sum)
    hidden_halves = gather_core(even_hidden)
    gate_up_sum = lax.all_to_all(
        gate_up_sum.reshape(devices, piece, 2 * ff_block), ("fsdp", "ctx"), 0, 0, tiled=True
    )
    grad_mixed = jnp.concatenate([dot(h, w_out_rows, ((1,), (1,)), LOW) for h in hidden_halves], axis=0)
    out_part = dot(mixed[:middle], hidden_halves[0], ((0,), (0,))) + dot(
        mixed[middle:], hidden_halves[1], ((0,), (0,))
    )
    out_part = out_part.astype(LOW).reshape(f_count, piece, width)

    grad_mixed, out_part = tie(grad_mixed, out_part)
    out_sum = halve_near(out_part, f_index)
    down_sum = dot(act_of(0), all_cots, ((0,), (0,)))
    grad_q, grad_kv = attention_backward(
        q_scaled, k_rot, v_low, grad_mixed, lse, cosine, sine, int_places, heads
    )
    grad_qkv = jnp.concatenate([grad_q, grad_kv], axis=1)
    grad_qkv, out_sum = tie(grad_qkv, out_sum)

    halves = [grad_qkv[middle:], grad_qkv[:middle]]
    odd = scatter_core(dot(halves[0], w_qkv, ((1,), (1,)), LOW))
    qkv_part = dot(normed_first[0], halves[1], ((0,), (0,))) + dot(normed_first[1], halves[0], ((0,), (0,)))
    qkv_part = qkv_part.astype(LOW).reshape(f_count, c_count * piece, qkv_width)
    even = dot(halves[1], w_qkv, ((1,), (1,)), LOW)
    odd, even, qkv_part = tie(odd, even, qkv_part)
    state = scatter_far(even, odd)
    qkv_sum = halve_near(qkv_part, f_index)
    out_sum = halve_far(out_sum, f_index, top_bit)
    state, qkv_sum, out_sum, down_away = tie(state, qkv_sum, out_sum, down_away)
    state = scatter_near(state)
    qkv_sum = halve_far(qkv_sum, f_index, top_bit)
    out_grad = lax.ppermute(out_sum, ("fsdp", "ctx"), [(d, s) for s, d in out_route]).astype(WIDE)
    for r, part in enumerate(down_away, 1):
        down_sum = down_sum + swap(part, "fsdp", r).astype(WIDE)
    down_grad = down_sum
    state, qkv_sum, out_rows = tie(state, qkv_sum, out_rows)
    qkv_sum = exchange_ctx(qkv_sum.reshape(c_count, piece, qkv_width))
    side_out = swap(out_rows[1], "fsdp", top_bit)
    grad_normed = scatter_end(state)
    input_grad = grad_hidden + norm_back(grad_normed, hat_first, inv_first)
    gate_grad, up_grad, mlp_gain_grad = assemble_columns(gate_up_sum, w_gate, w_up, mlp_scale)
    mlp_gain_grad = mlp_gain_grad[:, 0]
    output = hidden + out_rows[0].astype(WIDE) + side_out.astype(WIDE)

    qkv_sum = qkv_sum.astype(WIDE)
    query_grad = qkv_sum[:, :, :q_width].transpose(1, 0, 2).reshape(piece, -1)
    kv_sum = qkv_sum[:, :, q_width:].reshape(KV_HEADS, kv_share, piece, 2, HEAD_DIM).sum(axis=1)
    key_grad = kv_sum[:, :, 0].transpose(1, 0, 2).reshape(piece, -1)
    value_grad = kv_sum[:, :, 1].transpose(1, 0, 2).reshape(piece, -1)
    attn_gain_grad = (
        jnp.sum(query_grad * w_query.astype(WIDE), axis=1)
        + jnp.sum(key_grad * w_key.astype(WIDE), axis=1)
        + jnp.sum(value_grad * w_value.astype(WIDE), axis=1)
    )
    query_grad, key_grad, value_grad = (g * attn_scale for g in (query_grad, key_grad, value_grad))

    return (
        output.astype(LOW)[None],
        input_grad.astype(LOW)[None],
        attn_gain_grad,
        query_grad,
        key_grad,
        value_grad,
        out_grad,
        mlp_gain_grad,
        gate_grad,
        up_grad,
        down_grad,
    )


def solution(mesh):
    rows = P(("fsdp", "ctx"), None)
    vector = P(("fsdp", "ctx"))
    tokens = P("fsdp", "ctx", None)
    in_specs = (
        tokens, P("fsdp", "ctx"), vector, rows, rows, rows, rows, vector, rows, rows, rows, tokens,
    )
    out_specs = (
        tokens, tokens, vector, rows, rows, rows, rows, vector, rows, rows, rows,
    )
    return jax.shard_map(
        per_device, mesh=mesh, in_specs=in_specs, out_specs=out_specs, check_vma=False
    )
```

```python
import functools

import jax
import jax.numpy as jnp
from jax import lax
from jax.experimental import pallas as pl
from jax.experimental.pallas import tpu as pltpu
from jax.sharding import PartitionSpec as P

HEADS = 32
KV_HEADS = 8
HEAD_DIM = 64
EPSILON = 1e-05
ROPE_BASE = 500000.0
VMEM_LIMIT = 56 * 1024 * 1024
LOW = jnp.bfloat16
WIDE = jnp.float32


def dot(left, right, dims=((1,), (0,)), out=WIDE):
    return lax.dot_general(left, right, (dims, ((), ())), preferred_element_type=WIDE).astype(out)


def tie(*values):
    return lax.optimization_barrier(values)


def swap(block, axis, mask):
    count = lax.axis_size(axis)
    return lax.ppermute(block, axis, [(i, i ^ mask) for i in range(count)])


def pick(stack, index):
    return lax.dynamic_index_in_dim(stack, index, 0, keepdims=False)


def in_order(pieces, base):
    out = jnp.zeros((len(pieces),) + pieces[0].shape, pieces[0].dtype)
    for r, piece in enumerate(pieces):
        out = lax.dynamic_update_index_in_dim(out, piece, base ^ r, 0)
    return out


def ctx_order(count):
    order = [0]
    bit = 2
    while bit < count:
        order = order + [k ^ bit for k in order]
        bit *= 2
    return order + [k ^ 1 for k in order]


def gather_near(block):
    count = lax.axis_size("ctx")
    return (swap(block, "ctx", 2), swap(block, "ctx", 4)) if count == 8 else ()


def gather_far(block, near):
    count = lax.axis_size("ctx")
    if count == 8:
        near_x, near_y = near
        half = block.shape[0] // 2
        return block, near_x, near_y, swap(near_y[:half], "ctx", 2), swap(near_x[half:], "ctx", 4)
    even, bit = (block,), 2
    while bit < count:
        even = even + tuple(swap(part, "ctx", bit) for part in even)
        bit *= 2
    return even


def gather_core(even):
    quad = jnp.concatenate(even, axis=0)
    return quad, swap(quad, "ctx", 1)


def scatter_core(odd):
    return swap(odd, "ctx", 1)


def scatter_sum(even, odd):
    return (even.astype(WIDE) + odd.astype(WIDE)).astype(LOW)


def scatter_far(quad):
    count = lax.axis_size("ctx")
    if count != 8:
        return (quad.astype(WIDE),)
    rows = quad.shape[0] // 4
    half = rows // 2
    own, to_x, to_y, far = (quad[j * rows : (j + 1) * rows] for j in range(4))
    far_x, far_y = swap(far[half:], "ctx", 2), swap(far[:half], "ctx", 4)
    by_x, by_y = swap(to_x[half:], "ctx", 2), swap(to_y[:half], "ctx", 4)
    return own, to_x[:half], to_y[half:], by_x, by_y, far_x, far_y


def scatter_near(state):
    count = lax.axis_size("ctx")
    if count != 8:
        (quad,) = state
        bit = count // 2
        while bit >= 2:
            middle = quad.shape[0] // 2
            quad = quad[:middle] + swap(quad[middle:].astype(LOW), "ctx", bit).astype(WIDE)
            bit //= 2
        return (quad,)
    own, to_x, to_y, by_x, by_y, far_x, far_y = state
    last_x = swap((to_x.astype(WIDE) + far_y.astype(WIDE)).astype(LOW), "ctx", 2)
    last_y = swap((to_y.astype(WIDE) + far_x.astype(WIDE)).astype(LOW), "ctx", 4)
    return own, by_x, by_y, last_x, last_y


def scatter_end(state):
    if len(state) == 1:
        return state[0]
    own, by_x, by_y, last_x, last_y = state
    half = last_x.shape[0]
    top = own[:half].astype(WIDE) + last_x.astype(WIDE) + by_y.astype(WIDE)
    low = own[half:].astype(WIDE) + by_x.astype(WIDE) + last_y.astype(WIDE)
    return jnp.concatenate([top, low], axis=0)


def exchange_ctx(stack):
    return lax.all_to_all(stack, "ctx", 0, 0, tiled=True)


def double_fsdp(stacks, first, last):
    bit = first
    while bit >= last:
        sent = stacks[0] if len(stacks) == 1 else jnp.concatenate(stacks, axis=0)
        stacks = stacks + [swap(sent, "fsdp", bit)]
        bit //= 2
    return stacks


def xor_order(first, last):
    order, bit = [0], first
    while bit >= last:
        order = order + [k ^ bit for k in order]
        bit //= 2
    return order


def place_kernel(masks, rows, base_ref, *refs):
    out_ref = refs[-1]
    masks = iter(masks)
    for part in refs[:-1]:
        for j in range(part.shape[0]):
            start = pl.multiple_of((base_ref[0] ^ next(masks)) * rows, 16)
            out_ref[pl.ds(start, rows), :] = part[j]


def place(parts, masks, base):
    _, rows, columns = parts[0].shape
    total = len(masks) * rows
    whole = pl.BlockSpec(memory_space=pltpu.VMEM)
    return pl.pallas_call(
        functools.partial(place_kernel, masks, rows),
        in_specs=[pl.BlockSpec(memory_space=pltpu.SMEM)] + [whole] * len(parts),
        out_specs=whole,
        out_shape=jax.ShapeDtypeStruct((total, columns), parts[0].dtype),
        compiler_params=pltpu.CompilerParams(vmem_limit_bytes=VMEM_LIMIT),
        cost_estimate=pl.CostEstimate(flops=0, bytes_accessed=total * columns * 2, transcendentals=0),
        name="place",
    )(base.reshape(1), *parts)


def halve_fsdp(stack, base, first, last):
    bit = first
    while bit >= last:
        low = stack.shape[0] // 2
        side = (base // bit) % 2
        pair = stack.reshape((2, low) + stack.shape[1:])
        mine, theirs = pick(pair, side), pick(pair, 1 - side)
        stack = (mine.astype(WIDE) + swap(theirs, "fsdp", bit).astype(WIDE)).astype(LOW)
        bit //= 2
    return stack if stack.shape[0] > 1 else stack[0]


def halve_near(stack, base):
    pair = stack.reshape((stack.shape[0] // 2, 2) + stack.shape[1:]).swapaxes(0, 1)
    mine, theirs = pick(pair, base % 2), pick(pair, 1 - base % 2)
    return (mine.astype(WIDE) + swap(theirs, "fsdp", 1).astype(WIDE)).astype(LOW)


def halve_far(stack, base, first):
    return halve_fsdp(stack, base, first, 2)


def turned(block, cosine, sine):
    lane = lax.broadcasted_iota(jnp.int32, block.shape, 1)
    first = (lane % HEAD_DIM) < HEAD_DIM // 2
    width = block.shape[1]
    other = jnp.where(
        first, pltpu.roll(block, width - HEAD_DIM // 2, 1), pltpu.roll(block, HEAD_DIM // 2, 1)
    )
    return block * cosine + other * sine


def forward_kernel(
    heads, q_ref, kv_ref, cos_ref, sin_ref, cosk_ref, sink_ref, row_ref, col_ref,
    mixed_ref, lse_ref, qs_ref, kr_ref, vl_ref, vt_ref,
):
    @pl.when(pl.program_id(0) == 0)
    def _():
        keys = turned(kv_ref[...], cosk_ref[...], sink_ref[...])
        kr_ref[...] = keys[:, :HEAD_DIM].astype(LOW)
        values = kv_ref[...][:, HEAD_DIM:].astype(LOW)
        vl_ref[...] = values
        vt_ref[...] = values.astype(WIDE).T.astype(LOW)

    cosine, sine = cos_ref[...], sin_ref[...]
    keys = kr_ref[...]
    values_t = vt_ref[...]
    visible = col_ref[...] <= row_ref[...]
    scale = HEAD_DIM ** (-0.5)
    mixed, totals = [], []
    for pair in range(heads // 2):
        both = turned(q_ref[:, pair * 128 : pair * 128 + 128], cosine, sine)
        both = (both.astype(LOW).astype(WIDE) * scale).astype(LOW)
        qs_ref[:, pair * 128 : pair * 128 + 128] = both
        for side in range(2):
            query = both[:, side * HEAD_DIM : (side + 1) * HEAD_DIM]
            scores = jnp.where(visible, dot(keys, query, ((1,), (1,))), -1e30)
            top = jnp.max(scores, axis=0, keepdims=True)
            weights = jnp.exp(scores - top)
            total = jnp.sum(weights, axis=0, keepdims=True)
            out = dot(values_t, weights.astype(LOW)) / total
            mixed.append(out)
            totals.append(top + jnp.log(total))
    mixed_ref[...] = jnp.concatenate(mixed, axis=0).T.astype(LOW)
    pad = [jnp.zeros_like(totals[0])] * (8 - heads)
    lse_ref[...] = jnp.concatenate(totals + pad, axis=0)


def backward_kernel(
    heads, steps, q_ref, k_ref, v_ref, do_ref, lse_ref, cos_ref, sin_ref, cosk_ref, sink_ref,
    row_ref, col_ref, out_ref, kt_ref, dk_ref, dv_ref,
):
    @pl.when(pl.program_id(0) == 0)
    def _():
        kt_ref[...] = k_ref[...].astype(WIDE).T.astype(LOW)
        dk_ref[...] = jnp.zeros_like(dk_ref)
        dv_ref[...] = jnp.zeros_like(dv_ref)

    keys, values, keys_t = k_ref[...], v_ref[...], kt_ref[...]
    visible = col_ref[...] <= row_ref[...]
    scale = HEAD_DIM ** (-0.5)
    grads = []
    for head in range(heads):
        lanes = slice(head * HEAD_DIM, (head + 1) * HEAD_DIM)
        query, grad_out = q_ref[:, lanes], do_ref[:, lanes]
        scores = dot(keys, query, ((1,), (1,)))
        probs = jnp.where(visible, jnp.exp(scores - lse_ref[head : head + 1, :]), 0.0)
        grad_probs = dot(values, grad_out, ((1,), (1,)))
        product = probs * grad_probs
        delta = jnp.sum(product, axis=0, keepdims=True)
        grad_scores = (product - probs * delta).astype(LOW)
        dv_ref[...] += dot(probs.astype(LOW), grad_out)
        dk_ref[...] += dot(grad_scores, query)
        grads.append(dot(keys_t, grad_scores) * scale)
    grad_q = jnp.concatenate(grads, axis=0).T
    cosine, sine = cos_ref[...], sin_ref[...]
    block = grad_q.shape[0]
    rows = pl.ds(pl.multiple_of(pl.program_id(0) * block, block), block)
    for pair in range(heads // 2):
        lanes = slice(pair * 128, pair * 128 + 128)
        out_ref[rows, lanes] = turned(grad_q[:, lanes], cosine, -sine).astype(LOW)

    @pl.when(pl.program_id(0) == steps - 1)
    def _():
        both = jnp.concatenate([dk_ref[...], dv_ref[...]], axis=1)
        back = turned(both, cosk_ref[...], -sink_ref[...])
        lane = lax.broadcasted_iota(jnp.int32, both.shape, 1)
        out_ref[:, heads * HEAD_DIM :] = jnp.where(lane < HEAD_DIM, back, both).astype(LOW)


def attention_forward(qkv, cosine, sine, places, heads):
    length = qkv.shape[0]
    width = heads * HEAD_DIM
    block = min(256, length)
    whole = lambda shape: pl.BlockSpec(shape, lambda i: (0,) * len(shape))
    rows = lambda columns: pl.BlockSpec((block, columns), lambda i: (i, 0))
    return pl.pallas_call(
        functools.partial(forward_kernel, heads),
        grid=(length // block,),
        in_specs=[
            rows(width),
            pl.BlockSpec((length, 128), lambda i: (0, width // 128)),
            rows(128), rows(128), whole((length, 128)), whole((length, 128)),
            pl.BlockSpec((1, block), lambda i: (0, i)), whole((length, 1)),
        ],
        out_specs=[
            rows(width), pl.BlockSpec((8, block), lambda i: (0, i)), rows(width),
            whole((length, HEAD_DIM)), whole((length, HEAD_DIM)),
        ],
        out_shape=[
            jax.ShapeDtypeStruct((length, width), LOW),
            jax.ShapeDtypeStruct((8, length), WIDE),
            jax.ShapeDtypeStruct((length, width), LOW),
            jax.ShapeDtypeStruct((length, HEAD_DIM), LOW),
            jax.ShapeDtypeStruct((length, HEAD_DIM), LOW),
        ],
        scratch_shapes=[pltpu.VMEM((HEAD_DIM, length), LOW)],
        compiler_params=pltpu.CompilerParams(
            dimension_semantics=("arbitrary",), vmem_limit_bytes=VMEM_LIMIT
        ),
        cost_estimate=pl.CostEstimate(
            flops=0, bytes_accessed=8 * length * width, transcendentals=0
        ),
        name="attention_forward",
    )(qkv, qkv, cosine, sine, cosine, sine, places[None, :], places[:, None])


def attention_backward(q_scaled, k_rot, v_low, grad_mixed, lse, cosine, sine, places, heads):
    length = q_scaled.shape[0]
    width = heads * HEAD_DIM
    block = min(256, length)
    steps = length // block
    whole = lambda shape: pl.BlockSpec(shape, lambda i: (0,) * len(shape))
    rows = lambda columns: pl.BlockSpec((block, columns), lambda i: (i, 0))
    return pl.pallas_call(
        functools.partial(backward_kernel, heads, steps),
        grid=(steps,),
        in_specs=[
            rows(width), whole((length, HEAD_DIM)), whole((length, HEAD_DIM)), rows(width),
            pl.BlockSpec((8, block), lambda i: (0, i)),
            rows(128), rows(128), whole((length, 128)), whole((length, 128)),
            pl.BlockSpec((1, block), lambda i: (0, i)), whole((length, 1)),
        ],
        out_specs=whole((length, width + 128)),
        out_shape=jax.ShapeDtypeStruct((length, width + 128), LOW),
        scratch_shapes=[
            pltpu.VMEM((HEAD_DIM, length), LOW),
            pltpu.VMEM((length, HEAD_DIM), WIDE),
            pltpu.VMEM((length, HEAD_DIM), WIDE),
        ],
        compiler_params=pltpu.CompilerParams(
            dimension_semantics=("arbitrary",), vmem_limit_bytes=VMEM_LIMIT
        ),
        cost_estimate=pl.CostEstimate(
            flops=0, bytes_accessed=8 * length * width, transcendentals=0
        ),
        name="attention_backward",
    )(
        q_scaled, k_rot, v_low, grad_mixed, lse, cosine, sine, cosine, sine,
        places[None, :], places[:, None],
    )


def columns_kernel(block, gate_ref, up_ref, scale_ref, out_ref):
    scale = scale_ref[...]
    for j in range(out_ref.shape[0]):
        lanes = slice(j * block, (j + 1) * block)
        out_ref[j, :, :block] = (gate_ref[:, lanes].astype(WIDE) * scale).astype(LOW)
        out_ref[j, :, block:] = (up_ref[:, lanes].astype(WIDE) * scale).astype(LOW)


def columns_by_device(w_gate, w_up, scale, block):
    rows, ff_width = w_gate.shape
    devices = ff_width // block
    if block % 128:
        split = [(w.astype(WIDE) * scale).astype(LOW).reshape(rows, devices, block) for w in (w_gate, w_up)]
        return jnp.concatenate(split, axis=2).transpose(1, 0, 2)
    some = 8
    part = pl.BlockSpec((rows, some * block), lambda d: (0, d))
    return pl.pallas_call(
        functools.partial(columns_kernel, block),
        grid=(devices // some,),
        in_specs=[part, part, pl.BlockSpec((rows, 1), lambda d: (0, 0))],
        out_specs=pl.BlockSpec((some, rows, 2 * block), lambda d: (d, 0, 0)),
        out_shape=jax.ShapeDtypeStruct((devices, rows, 2 * block), LOW),
        cost_estimate=pl.CostEstimate(flops=0, bytes_accessed=2 << 20, transcendentals=0),
        name="columns_by_device",
    )(w_gate, w_up, scale)


def assemble_kernel(part_ref, gate_ref, up_ref, scale_ref, gate_out, up_out, gain_out):
    @pl.when(pl.program_id(0) == 0)
    def _():
        gain_out[...] = jnp.zeros_like(gain_out)

    scale = scale_ref[...]
    block = gate_ref.shape[1] // part_ref.shape[0]
    total = jnp.zeros_like(gain_out)
    for j in range(part_ref.shape[0]):
        lanes = slice(j * block, (j + 1) * block)
        gate = part_ref[j, :, :block].astype(WIDE)
        up = part_ref[j, :, block:].astype(WIDE)
        gate_out[:, lanes] = gate * scale
        up_out[:, lanes] = up * scale
        products = gate * gate_ref[:, lanes].astype(WIDE) + up * up_ref[:, lanes].astype(WIDE)
        total = total + jnp.sum(products, axis=1, keepdims=True)
    gain_out[...] += total


def assemble_columns(parts, w_gate, w_up, scale):
    devices, rows, both = parts.shape
    block = both // 2
    ff_width = w_gate.shape[1]
    if block % 128:
        sides = parts.reshape(devices, rows, 2, block).transpose(2, 1, 0, 3).reshape(2, rows, ff_width)
        sides = sides.astype(WIDE)
        products = sides[0] * w_gate.astype(WIDE) + sides[1] * w_up.astype(WIDE)
        return sides[0] * scale, sides[1] * scale, jnp.sum(products, axis=1, keepdims=True)
    some = 8
    columns = pl.BlockSpec((rows, some * block), lambda d: (0, d))
    one = pl.BlockSpec((rows, 1), lambda d: (0, 0))
    return pl.pallas_call(
        assemble_kernel,
        grid=(devices // some,),
        in_specs=[pl.BlockSpec((some, rows, both), lambda d: (d, 0, 0)), columns, columns, one],
        out_specs=[columns, columns, one],
        out_shape=[
            jax.ShapeDtypeStruct((rows, ff_width), WIDE),
            jax.ShapeDtypeStruct((rows, ff_width), WIDE),
            jax.ShapeDtypeStruct((rows, 1), WIDE),
        ],
        compiler_params=pltpu.CompilerParams(
            dimension_semantics=("arbitrary",), vmem_limit_bytes=VMEM_LIMIT
        ),
        cost_estimate=pl.CostEstimate(flops=0, bytes_accessed=8 << 20, transcendentals=0),
        name="assemble_columns",
    )(parts, w_gate, w_up, scale)


def feed_kernel(blocks, steps, per_step, table_ref, *refs):
    even_ref, odd_ref = refs[:2]
    cot_refs = refs[2 : 2 + per_step]
    weights = refs[2 + per_step : 2 + per_step + blocks]
    downs = refs[2 + per_step + blocks : 2 + per_step + 2 * blocks]
    norm_out, cot_out, act_out, low_out, even_out, odd_out = refs[-6:]
    step = pl.program_id(0)
    width = downs[0].shape[0]
    norm = jnp.where(step < steps // 2, even_ref[...], odd_ref[...])
    norm_out[...] = norm
    cot = jnp.concatenate([ref[0] for ref in cot_refs], axis=0)
    cot_out[...] = cot
    term = None
    for j in range(blocks):
        rows = dot(norm, weights[j][...])
        gate, up = rows[:, :width], rows[:, width:]
        grad_act = dot(cot, downs[j][...], ((1,), (1,)))
        sig = 1.0 / (1.0 + jnp.exp(-gate))
        gate_sig = gate * sig
        act_out[j] = (gate_sig * up).astype(LOW)
        grad_up = (grad_act * gate_sig).astype(LOW)
        grad_gate = (grad_act * up * (sig + gate_sig * (1.0 - sig))).astype(LOW)
        low_out[2 * j] = grad_gate
        low_out[2 * j + 1] = grad_up
        more = dot(jnp.concatenate([grad_gate, grad_up], axis=1), weights[j][...], ((1,), (1,)))
        term = more if term is None else term + more
    term = term.astype(LOW)

    @pl.when(step < steps // 2)
    def _():
        even_out[...] = term

    @pl.when(step >= steps // 2)
    def _():
        odd_out[...] = term


def feed_forward(which, even, odd, cots, table, weights, downs, earlier):
    half, width = even.shape
    c_count, tok_rows, _ = cots.shape
    blocks = len(weights)
    block = downs[0].shape[0]
    steps = 4
    rows = 2 * half // steps
    per_step = rows // tok_rows
    total = 4 * half
    first = which * steps
    even_at = lambda i, t: (jnp.minimum(i, steps // 2 - 1), 0)
    odd_at = lambda i, t: (jnp.maximum(i - steps // 2, 0), 0)
    cot_spec = lambda j: pl.BlockSpec(
        (1, tok_rows, width), lambda i, t, j=j: (t[i * per_step + j], 0, 0)
    )
    fixed = lambda shape: pl.BlockSpec(shape, lambda i, t: (0,) * len(shape))
    at = lambda i, t: (first + i, 0)
    out_shape = [
        jax.ShapeDtypeStruct((total, width), LOW),
        jax.ShapeDtypeStruct((total, width), LOW),
        jax.ShapeDtypeStruct((blocks, total, block), LOW),
        jax.ShapeDtypeStruct((2 * blocks, total, block), LOW),
        jax.ShapeDtypeStruct((half, width), LOW),
        jax.ShapeDtypeStruct((half, width), LOW),
    ]
    weights = list(weights) + list(downs)
    inputs = [even, odd] + [cots] * per_step + weights + list(earlier)
    in_specs = (
        [pl.BlockSpec((rows, width), even_at), pl.BlockSpec((rows, width), odd_at)]
        + [cot_spec(j) for j in range(per_step)]
        + [fixed(w.shape) for w in weights]
        + [pl.BlockSpec(memory_space=pl.ANY)] * len(earlier)
    )
    aliases = {1 + len(inputs) - len(earlier) + j: j for j in range(len(earlier))}
    return pl.pallas_call(
        functools.partial(feed_kernel, blocks, steps, per_step),
        grid_spec=pltpu.PrefetchScalarGridSpec(
            num_scalar_prefetch=1,
            grid=(steps,),
            in_specs=in_specs,
            out_specs=[
                pl.BlockSpec((rows, width), at),
                pl.BlockSpec((rows, width), at),
                pl.BlockSpec((blocks, rows, block), lambda i, t: (0, first + i, 0)),
                pl.BlockSpec((2 * blocks, rows, block), lambda i, t: (0, first + i, 0)),
                pl.BlockSpec((rows, width), even_at),
                pl.BlockSpec((rows, width), odd_at),
            ],
        ),
        out_shape=out_shape,
        input_output_aliases=aliases,
        compiler_params=pltpu.CompilerParams(
            dimension_semantics=("arbitrary",), vmem_limit_bytes=VMEM_LIMIT
        ),
        cost_estimate=pl.CostEstimate(flops=0, bytes_accessed=8 << 20, transcendentals=0),
        name="feed_forward",
    )(table, *inputs)


def down_kernel(blocks, table_ref, act_ref, *refs):
    out_ref, downs = refs[-1], refs[:-1]
    total = None
    for j in range(blocks):
        part = dot(act_ref[j], downs[j][...])
        total = part if total is None else total + part
    total = total.astype(LOW)
    chips, rows = out_ref.shape[0], out_ref.shape[3]
    for q in range(chips):
        out_ref[table_ref[0] ^ q, 0, 0] = total[q * rows : (q + 1) * rows]


def down_terms_by_device(acts, c_index, c_count, downs, tok_rows):
    blocks, total, block = acts.shape
    width = downs[0].shape[1]
    chips = c_count // 2
    fixed = lambda shape: pl.BlockSpec(shape, lambda i, j, t: (0,) * len(shape))
    place_of = jnp.stack([c_index // 2, c_index % 2]).astype(jnp.int32)
    out = pl.pallas_call(
        functools.partial(down_kernel, blocks),
        grid_spec=pltpu.PrefetchScalarGridSpec(
            num_scalar_prefetch=1,
            grid=(2, 2),
            in_specs=[pl.BlockSpec((blocks, chips * tok_rows, block), lambda i, j, t: (0, 2 * i + j, 0))]
            + [fixed(d.shape) for d in downs],
            out_specs=pl.BlockSpec(
                (chips, 1, 1, tok_rows, width), lambda i, j, t: (0, t[1] ^ j, i, 0, 0)
            ),
        ),
        out_shape=jax.ShapeDtypeStruct((chips, 2, 2, tok_rows, width), LOW),
        compiler_params=pltpu.CompilerParams(vmem_limit_bytes=VMEM_LIMIT),
        cost_estimate=pl.CostEstimate(flops=0, bytes_accessed=8 << 20, transcendentals=0),
        name="down_terms",
    )(place_of, acts, *downs)
    return out.reshape(c_count * 2 * tok_rows, width)


def inverse_rms(rows):
    return lax.rsqrt(jnp.mean(rows * rows, axis=-1, keepdims=True) + EPSILON)


def norm_back(grad_hat, hat_rows, inv_rms):
    return inv_rms * (grad_hat - hat_rows * jnp.mean(grad_hat * hat_rows, axis=-1, keepdims=True))


def per_device(
    tokens, positions, attn_gain, w_query, w_key, w_value, w_out,
    mlp_gain, w_gate, w_up, w_down, cotangent,
):
    f_count, c_count = lax.axis_size("fsdp"), lax.axis_size("ctx")
    f_index, c_index = lax.axis_index("fsdp"), lax.axis_index("ctx")
    devices = f_count * c_count
    top_bit = f_count // 2
    own_tokens, own_cot = tokens[0], cotangent[0]
    tok_rows, width = own_tokens.shape
    piece = w_query.shape[0]
    heads = HEADS // c_count
    q_width = heads * HEAD_DIM
    qkv_width = q_width + 2 * HEAD_DIM
    kv_share = max(1, c_count // KV_HEADS)
    ff_block = w_down.shape[0]
    c_order = ctx_order(c_count)
    f_order = xor_order(top_bit, 1)

    attn_scale, mlp_scale = attn_gain.astype(WIDE)[:, None], mlp_gain.astype(WIDE)[:, None]
    near_tokens = gather_near(own_tokens)
    shares = [
        w_query.reshape(piece, c_count, q_width),
        jnp.repeat(w_key.reshape(piece, KV_HEADS, HEAD_DIM), kv_share, axis=1),
        jnp.repeat(w_value.reshape(piece, KV_HEADS, HEAD_DIM), kv_share, axis=1),
    ]
    qkv_piece = (jnp.concatenate(shares, axis=2).astype(WIDE) * attn_scale[:, :, None]).astype(LOW)
    qkv_piece = qkv_piece.transpose(1, 0, 2)
    qkv_piece, w_out, w_down = tie(qkv_piece, w_out, w_down)
    qkv_piece = exchange_ctx(qkv_piece).reshape(1, c_count * piece, qkv_width)
    out_route = [(f_count * c + j, j * c_count + c) for c in range(c_count) for j in range(f_count)]
    out_piece = lax.ppermute(w_out, ("fsdp", "ctx"), out_route)
    small = positions
    for bit in [2 ** j for j in range(1, c_count.bit_length() - 1)] + [1]:
        small = jnp.concatenate([small, swap(small, "ctx", bit)], axis=0)
    int_places = small.reshape(-1)
    down_half = ff_block // 2
    down_tops = [swap(w_down[:down_half], "fsdp", r) for r in range(1, top_bit)]

    qkv_piece, out_piece, near_tokens, own_cot, w_gate_in = tie(
        qkv_piece, out_piece, near_tokens, own_cot, w_gate
    )
    even_tokens = gather_far(own_tokens, near_tokens)
    qkv_parts = double_fsdp([qkv_piece], top_bit, 2)
    own_cots = lax.all_gather(own_cot, "ctx", axis=0, tiled=True)
    columns = columns_by_device(w_gate_in, w_up, mlp_scale, ff_block)
    half_dim = HEAD_DIM // 2
    frequency = jnp.power(ROPE_BASE, -2.0 * jnp.arange(half_dim, dtype=WIDE) / HEAD_DIM)
    angles = int_places.astype(WIDE)[:, None] * frequency[None, :]
    cosine, sine = jnp.cos(angles), jnp.sin(angles)
    cosine = jnp.concatenate([cosine] * 4, axis=1)
    sine = jnp.concatenate([-sine, sine, -sine, sine], axis=1)

    qkv_parts, out_piece, cosine, sine, even_tokens, down_tops, columns, own_cot = tie(
        qkv_parts, out_piece, cosine, sine, even_tokens, down_tops, columns, own_cot
    )
    half = tok_rows // 2
    cot_top = swap(own_cot[:half], "fsdp", top_bit)
    quad_tokens, other_tokens = gather_core(even_tokens)
    qkv_parts = double_fsdp(qkv_parts, 1, 1)
    out_parts = double_fsdp([out_piece[None]], top_bit, 2)

    def first_norm(rows):
        rows = rows.astype(WIDE)
        return (rows * inverse_rms(rows)).astype(LOW)

    normed_first = [first_norm(quad_tokens), first_norm(other_tokens)]

    qkv_parts, out_parts, normed_first, columns, cot_top, own_cot = tie(
        qkv_parts, out_parts, normed_first, columns, cot_top, own_cot
    )
    exchange_all = lambda stack: lax.all_to_all(stack, ("fsdp", "ctx"), 0, 0, tiled=True)
    columns = exchange_all(columns)
    out_parts = double_fsdp(out_parts, 1, 1)
    w_qkv = place(qkv_parts, f_order, f_index)
    qkv = jnp.concatenate([dot(rows, w_qkv) for rows in normed_first], axis=0)
    mixed, lse, q_scaled, k_rot, v_low = attention_forward(qkv, cosine, sine, int_places, heads)

    mixed, out_parts, columns, own_cot = tie(mixed, out_parts, columns, own_cot)
    cut = width // 2
    own_columns = columns.reshape(width, 2 * ff_block)
    tops = [swap(own_columns[:cut], "fsdp", r) for r in range(1, top_bit)]
    cot_low = swap(own_cot[half:], "fsdp", top_bit)
    w_out_rows = place(out_parts, f_order, f_index)
    middle = mixed.shape[0] // 2
    odd_out = scatter_core(dot(mixed[middle:], w_out_rows, out=LOW))
    even_out = dot(mixed[:middle], w_out_rows, out=LOW)
    state = scatter_far(scatter_sum(even_out, odd_out))
    inputs = own_tokens.astype(WIDE)
    inv_first = inverse_rms(inputs)
    hat_first = inputs * inv_first
    all_first = jnp.concatenate(normed_first, axis=0)
    state, hat_first, all_first, own_columns, tops, cot_low = tie(
        state, hat_first, all_first, own_columns, tops, cot_low
    )
    side_cots = lax.all_gather(jnp.concatenate([cot_top, cot_low], axis=0), "ctx", axis=0, tiled=True)
    lows = [swap(own_columns[cut:], "fsdp", r) for r in range(1, top_bit)]
    hidden = inputs + scatter_end(scatter_near(state))
    inv_second = inverse_rms(hidden)
    hat_second = hidden * inv_second
    normed_own = hat_second.astype(LOW)

    near_norm = gather_near(normed_own)
    side_norm = swap(normed_own, "fsdp", top_bit)
    near_norm, side_norm, own_columns, w_down, lows = tie(near_norm, side_norm, own_columns, w_down, lows)
    columns = [own_columns] + [jnp.concatenate(parts, axis=0) for parts in zip(tops, lows)]
    down_lows = [swap(w_down[down_half:], "fsdp", r) for r in range(1, top_bit)]
    even_norm = gather_far(normed_own, near_norm)
    near_side = gather_near(side_norm)
    norm_pieces = list(gather_core(even_norm))
    near_side, norm_pieces, own_cots, down_lows = tie(near_side, norm_pieces, own_cots, down_lows)
    downs = [w_down] + [jnp.concatenate(parts, axis=0) for parts in zip(down_tops, down_lows)]
    even_side = gather_far(side_norm, near_side)
    table = jnp.array(c_order, jnp.int32) ^ c_index
    by_block = lambda rows: rows.reshape(c_count, tok_rows, width)

    weights = (table, columns, downs)
    *buffers, even_zero, odd_zero = feed_forward(0, *norm_pieces, by_block(own_cots), *weights, [])
    even_side, buffers, even_zero, odd_zero = tie(even_side, buffers, even_zero, odd_zero)
    side_norms = gather_core(even_side)
    quad_zero = scatter_sum(even_zero, scatter_core(odd_zero))
    side_norms, quad_zero, buffers, side_cots = tie(side_norms, quad_zero, buffers, side_cots)
    state_zero = scatter_far(quad_zero)
    *buffers, even_one, odd_one = feed_forward(1, *side_norms, by_block(side_cots), *weights, buffers)
    all_norms, all_cots, all_acts, all_lows = buffers
    state_zero, odd_one, even_one, all_norms = tie(state_zero, odd_one, even_one, all_norms)
    odd_one = scatter_core(odd_one)
    state_zero = scatter_near(state_zero)

    blocks = range(1, top_bit)
    gate_away = [dot(all_norms, all_lows[2 * j], ((0,), (0,)), LOW) for j in blocks]
    quad_one = scatter_sum(even_one, odd_one)
    quad_one, state_zero, gate_away, all_norms = tie(quad_one, state_zero, gate_away, all_norms)
    state_one = scatter_far(quad_one)
    gate_received = [swap(part, "fsdp", r) for r, part in enumerate(gate_away, 1)]
    up_away = [dot(all_norms, all_lows[2 * j + 1], ((0,), (0,)), LOW) for j in blocks]
    state_one, up_away, all_norms, all_acts, all_cots = tie(
        state_one, up_away, all_norms, all_acts, all_cots
    )
    state_one = scatter_near(state_one)
    down_away = [dot(all_acts[j], all_cots, ((0,), (0,)), LOW) for j in blocks]
    state_one, down_away, all_norms, all_acts = tie(state_one, down_away, all_norms, all_acts)
    side_one = swap(scatter_end(state_one).astype(LOW), "fsdp", top_bit)
    gate_own = dot(all_norms, all_lows[0], ((0,), (0,)), LOW)
    down_terms = down_terms_by_device(all_acts, c_index, c_count, downs, tok_rows)
    side_one, gate_own, all_norms, up_away, down_terms = tie(
        side_one, gate_own, all_norms, up_away, down_terms
    )
    grad_normed = scatter_end(state_zero) + side_one.astype(WIDE)

    grad_hidden = own_cot.astype(WIDE) + norm_back(grad_normed, hat_second, inv_second)
    hidden_low = grad_hidden.astype(LOW)
    near_hidden = gather_near(hidden_low)
    up_received = [swap(part, "fsdp", r) for r, part in enumerate(up_away, 1)]
    up_own = dot(all_norms, all_lows[1], ((0,), (0,)), LOW)
    near_hidden, up_own = tie(near_hidden, up_own)
    even_hidden = gather_far(hidden_low, near_hidden)
    even_hidden, up_received, gate_received, down_terms = tie(
        even_hidden, up_received, gate_received, down_terms
    )
    out_rows = lax.psum_scatter(down_terms, "ctx", scatter_dimension=0, tiled=True)
    out_rows = out_rows.reshape(2, tok_rows, width)
    hidden_halves = gather_core(even_hidden)

    def sum_by_device(own, parts):
        total = sum([part.astype(WIDE) for part in parts], own.astype(WIDE)).astype(LOW)
        return total.reshape(devices, piece, ff_block)

    both_sums = [sum_by_device(gate_own, gate_received), sum_by_device(up_own, up_received)]
    both_sums = exchange_all(jnp.concatenate(both_sums, axis=2))
    grad_mixed = jnp.concatenate([dot(h, w_out_rows, ((1,), (1,)), LOW) for h in hidden_halves], axis=0)
    out_part = dot(mixed[:middle], hidden_halves[0], ((0,), (0,))) + dot(
        mixed[middle:], hidden_halves[1], ((0,), (0,))
    )
    out_part = out_part.astype(LOW).reshape(f_count, piece, width)

    grad_mixed, out_part = tie(grad_mixed, out_part)
    out_sum = halve_near(out_part, f_index)
    grad_qkv = attention_backward(
        q_scaled, k_rot, v_low, grad_mixed, lse, cosine, sine, int_places, heads
    )

    grad_qkv, all_first = tie(grad_qkv, all_first)
    qkv_part = dot(all_first, grad_qkv, ((0,), (0,)), LOW)
    qkv_part = qkv_part.reshape(f_count, c_count * piece, qkv_width)
    grad_qkv, qkv_part = tie(grad_qkv, qkv_part)
    qkv_sum = halve_near(qkv_part, f_index)
    grad_qkv, both_sums, out_sum = tie(grad_qkv, both_sums, out_sum)
    odd = scatter_core(dot(grad_qkv[middle:], w_qkv, ((1,), (1,)), LOW))
    even = dot(grad_qkv[:middle], w_qkv, ((1,), (1,)), LOW)
    quad = scatter_sum(even, odd)
    out_sum = halve_far(out_sum, f_index, top_bit)
    qkv_sum, quad, down_away, out_sum = tie(qkv_sum, quad, down_away, out_sum)
    state = scatter_far(quad)
    qkv_sum = halve_far(qkv_sum, f_index, top_bit)
    out_grad = lax.ppermute(out_sum, ("fsdp", "ctx"), [(d, s) for s, d in out_route]).astype(WIDE)
    down_received = [swap(part, "fsdp", r) for r, part in enumerate(down_away, 1)]
    state, qkv_sum, out_grad, all_cots, out_rows = tie(state, qkv_sum, out_grad, all_cots, out_rows)
    state = scatter_near(state)
    qkv_sum = exchange_ctx(qkv_sum.reshape(c_count, piece, qkv_width))
    side_out = swap(out_rows[1], "fsdp", top_bit)
    down_grad = dot(all_acts[0], all_cots, ((0,), (0,)))
    for part in down_received:
        down_grad = down_grad + part.astype(WIDE)
    grad_normed = scatter_end(state)
    input_grad = grad_hidden + norm_back(grad_normed, hat_first, inv_first)
    gate_grad, up_grad, mlp_gain_grad = assemble_columns(both_sums, w_gate, w_up, mlp_scale)
    mlp_gain_grad = mlp_gain_grad[:, 0]
    output = hidden + out_rows[0].astype(WIDE) + side_out.astype(WIDE)

    qkv_sum = qkv_sum.astype(WIDE)
    query_grad = qkv_sum[:, :, :q_width].transpose(1, 0, 2).reshape(piece, -1)
    kv_sum = qkv_sum[:, :, q_width:].reshape(KV_HEADS, kv_share, piece, 2, HEAD_DIM).sum(axis=1)
    key_grad = kv_sum[:, :, 0].transpose(1, 0, 2).reshape(piece, -1)
    value_grad = kv_sum[:, :, 1].transpose(1, 0, 2).reshape(piece, -1)
    attn_gain_grad = (
        jnp.sum(query_grad * w_query.astype(WIDE), axis=1)
        + jnp.sum(key_grad * w_key.astype(WIDE), axis=1)
        + jnp.sum(value_grad * w_value.astype(WIDE), axis=1)
    )
    query_grad, key_grad, value_grad = (g * attn_scale for g in (query_grad, key_grad, value_grad))

    return (
        output.astype(LOW)[None],
        input_grad.astype(LOW)[None],
        attn_gain_grad,
        query_grad,
        key_grad,
        value_grad,
        out_grad,
        mlp_gain_grad,
        gate_grad,
        up_grad,
        down_grad,
    )


def solution(mesh):
    rows = P(("fsdp", "ctx"), None)
    vector = P(("fsdp", "ctx"))
    tokens = P("fsdp", "ctx", None)
    in_specs = (
        tokens, P("fsdp", "ctx"), vector, rows, rows, rows, rows, vector, rows, rows, rows, tokens,
    )
    out_specs = (
        tokens, tokens, vector, rows, rows, rows, rows, vector, rows, rows, rows,
    )
    return jax.shard_map(
        per_device, mesh=mesh, in_specs=in_specs, out_specs=out_specs, check_vma=False
    )
```

```python
import functools

import jax
import jax.numpy as jnp
from jax import lax
from jax.experimental import pallas as pl
from jax.experimental.pallas import tpu as pltpu
from jax.sharding import PartitionSpec as P

HEADS = 32
KV_HEADS = 8
HEAD_DIM = 64
EPSILON = 1e-05
ROPE_BASE = 500000.0
VMEM_LIMIT = 56 * 1024 * 1024

WHEN = {
    "out_route": (0, 1),
    "down_a": (0, 2),
    "down_b": (6, 9),
    "own_cots": (1, 9),
    "columns": (1, 2),
    "out_far": (2, 3),
    "cot_a": (2, 3),
    "out_near": (3, 99),
    "columns_all": (3, 4),
    "cot_b": (4, 6),
    "move_0": (5, 7),
    "move_1": (5, 6),
    "move_2": (6, 8),
    "move_3": (6, 8),
    "side_cots": (6, 11),
    "gate_away": (12, 13),
    "gate_move": (13, 18),
    "up_away": (13, 14),
    "down_away": (14, 15),
    "gate_own": (15, 16),
    "down_terms": (15, 16),
    "up_move": (16, 18),
    "up_own": (16, 17),
    "out_rows": (18, 23),
    "both_all": (18, 22),
    "down_move": (21, 24),
    "out_part": (18, 19),
    "out_halved": (19, 21),
    "out_sum": (21, 23),
    "out_grad": (23, 25),
    "side_out": (23, 25),
    "down_own": (20, 22),
    "assembled": (23, 24),
}
COST = {"forward": 0, "backward": 0, "feed": 0, "split_out": 1, "split_last": 2, "split_hidden": 2}
LOW = jnp.bfloat16
WIDE = jnp.float32


def dot(left, right, dims=((1,), (0,)), out=WIDE):
    return lax.dot_general(left, right, (dims, ((), ())), preferred_element_type=WIDE).astype(out)


def tie(*values):
    return lax.optimization_barrier(values)


class Steps:
    def __init__(self):
        self.waiting, self.flying, self.ended = {}, {}, {}

    def add(self, name, needs, operand, task):
        self.waiting[name] = (needs, operand, task)

    def result(self, name):
        if name in self.waiting:
            _, operand, task = self.waiting.pop(name)
            self.flying[name] = task(operand())
        return self.ended[name] if name in self.ended else self.flying[name]

    def barrier(self, step, *values):
        starting = [n for n in self.waiting if WHEN[n][0] <= step]
        later = [n for n in starting if any(need in self.waiting for need in self.waiting[n][0])]
        tasks = [(n, *self.waiting.pop(n)[1:]) for n in starting if n not in later]
        operands = [operand() for _, operand, _ in tasks]
        ending = [n for n in self.flying if WHEN[n][1] <= step and n not in self.ended]
        values, operands, results = tie(values, operands, [self.flying[n] for n in ending])
        self.ended.update(zip(ending, results))
        for (name, _, task), operand in zip(tasks, operands):
            self.flying[name] = task(operand)
        for name in later:
            self.result(name)
        return values


def swap(block, axis, mask):
    count = lax.axis_size(axis)
    return lax.ppermute(block, axis, [(i, i ^ mask) for i in range(count)])


def pick(stack, index):
    return lax.dynamic_index_in_dim(stack, index, 0, keepdims=False)


def in_order(pieces, base):
    out = jnp.zeros((len(pieces),) + pieces[0].shape, pieces[0].dtype)
    for r, piece in enumerate(pieces):
        out = lax.dynamic_update_index_in_dim(out, piece, base ^ r, 0)
    return out


def ctx_order(count):
    order = [0]
    bit = 2
    while bit < count:
        order = order + [k ^ bit for k in order]
        bit *= 2
    return order + [k ^ 1 for k in order]


def gather_near(block):
    count = lax.axis_size("ctx")
    return (swap(block, "ctx", 2), swap(block, "ctx", 4)) if count == 8 else ()


def gather_far(block, near):
    count = lax.axis_size("ctx")
    if count == 8:
        near_x, near_y = near
        half = block.shape[0] // 2
        return block, near_x, near_y, swap(near_y[:half], "ctx", 2), swap(near_x[half:], "ctx", 4)
    even, bit = (block,), 2
    while bit < count:
        even = even + tuple(swap(part, "ctx", bit) for part in even)
        bit *= 2
    return even


def swap_core(rows, parts):
    size = rows.shape[0] // parts
    pieces = [swap(rows[j * size : (j + 1) * size], "ctx", 1) for j in range(parts)]
    return pieces[0] if parts == 1 else jnp.concatenate(pieces, axis=0)


def gather_core(even, parts=1):
    quad = jnp.concatenate(even, axis=0)
    return quad, swap_core(quad, parts)


def scatter_core(odd, parts=1):
    return swap_core(odd, parts)


def scatter_sum(even, odd):
    return (even.astype(WIDE) + odd.astype(WIDE)).astype(LOW)


def scatter_far(quad):
    count = lax.axis_size("ctx")
    if count != 8:
        return (quad.astype(WIDE),)
    rows = quad.shape[0] // 4
    half = rows // 2
    own, to_x, to_y, far = (quad[j * rows : (j + 1) * rows] for j in range(4))
    far_x, far_y = swap(far[half:], "ctx", 2), swap(far[:half], "ctx", 4)
    by_x, by_y = swap(to_x[half:], "ctx", 2), swap(to_y[:half], "ctx", 4)
    return own, to_x[:half], to_y[half:], by_x, by_y, far_x, far_y


def scatter_near(state):
    count = lax.axis_size("ctx")
    if count != 8:
        (quad,) = state
        bit = count // 2
        while bit >= 2:
            middle = quad.shape[0] // 2
            quad = quad[:middle] + swap(quad[middle:].astype(LOW), "ctx", bit).astype(WIDE)
            bit //= 2
        return (quad,)
    own, to_x, to_y, by_x, by_y, far_x, far_y = state
    last_x = swap((to_x.astype(WIDE) + far_y.astype(WIDE)).astype(LOW), "ctx", 2)
    last_y = swap((to_y.astype(WIDE) + far_x.astype(WIDE)).astype(LOW), "ctx", 4)
    return own, by_x, by_y, last_x, last_y


def scatter_end(state):
    if len(state) == 1:
        return state[0]
    own, by_x, by_y, last_x, last_y = state
    half = last_x.shape[0]
    top = own[:half].astype(WIDE) + last_x.astype(WIDE) + by_y.astype(WIDE)
    low = own[half:].astype(WIDE) + by_x.astype(WIDE) + last_y.astype(WIDE)
    return jnp.concatenate([top, low], axis=0)


def exchange_ctx(stack):
    return lax.all_to_all(stack, "ctx", 0, 0, tiled=True)


def double_fsdp(stacks, first, last):
    bit = first
    while bit >= last:
        sent = stacks[0] if len(stacks) == 1 else jnp.concatenate(stacks, axis=0)
        stacks = stacks + [swap(sent, "fsdp", bit)]
        bit //= 2
    return stacks


def xor_order(first, last):
    order, bit = [0], first
    while bit >= last:
        order = order + [k ^ bit for k in order]
        bit //= 2
    return order


def place_kernel(masks, rows, base_ref, *refs):
    out_ref = refs[-1]
    masks = iter(masks)
    for part in refs[:-1]:
        for j in range(part.shape[0]):
            start = pl.multiple_of((base_ref[0] ^ next(masks)) * rows, 16)
            out_ref[pl.ds(start, rows), :] = part[j]


def place(parts, masks, base):
    _, rows, columns = parts[0].shape
    total = len(masks) * rows
    whole = pl.BlockSpec(memory_space=pltpu.VMEM)
    return pl.pallas_call(
        functools.partial(place_kernel, masks, rows),
        in_specs=[pl.BlockSpec(memory_space=pltpu.SMEM)] + [whole] * len(parts),
        out_specs=whole,
        out_shape=jax.ShapeDtypeStruct((total, columns), parts[0].dtype),
        compiler_params=pltpu.CompilerParams(vmem_limit_bytes=VMEM_LIMIT),
        cost_estimate=pl.CostEstimate(flops=0, bytes_accessed=total * columns * 2, transcendentals=0),
        name="place",
    )(base.reshape(1), *parts)


def halve_fsdp(stack, base, first, last):
    bit = first
    while bit >= last:
        low = stack.shape[0] // 2
        side = (base // bit) % 2
        pair = stack.reshape((2, low) + stack.shape[1:])
        mine, theirs = pick(pair, side), pick(pair, 1 - side)
        stack = (mine.astype(WIDE) + swap(theirs, "fsdp", bit).astype(WIDE)).astype(LOW)
        bit //= 2
    return stack if stack.shape[0] > 1 else stack[0]


def halve_near(stack, base):
    pair = stack.reshape((stack.shape[0] // 2, 2) + stack.shape[1:]).swapaxes(0, 1)
    mine, theirs = pick(pair, base % 2), pick(pair, 1 - base % 2)
    return (mine.astype(WIDE) + swap(theirs, "fsdp", 1).astype(WIDE)).astype(LOW)


def halve_far(stack, base, first):
    return halve_fsdp(stack, base, first, 2)


def turned(block, cosine, sine):
    lane = lax.broadcasted_iota(jnp.int32, block.shape, 1)
    first = (lane % HEAD_DIM) < HEAD_DIM // 2
    width = block.shape[1]
    other = jnp.where(
        first, pltpu.roll(block, width - HEAD_DIM // 2, 1), pltpu.roll(block, HEAD_DIM // 2, 1)
    )
    return block * cosine + other * sine


def forward_kernel(
    heads, q_ref, kv_ref, cos_ref, sin_ref, cosk_ref, sink_ref, row_ref, col_ref,
    mixed_ref, lse_ref, qs_ref, kr_ref, vl_ref, vt_ref,
):
    @pl.when(pl.program_id(0) == 0)
    def _():
        keys = turned(kv_ref[...], cosk_ref[...], sink_ref[...])
        kr_ref[...] = keys[:, :HEAD_DIM].astype(LOW)
        values = kv_ref[...][:, HEAD_DIM:].astype(LOW)
        vl_ref[...] = values
        vt_ref[...] = values.astype(WIDE).T.astype(LOW)

    cosine, sine = cos_ref[...], sin_ref[...]
    keys = kr_ref[...]
    values_t = vt_ref[...]
    visible = col_ref[...] <= row_ref[...]
    scale = HEAD_DIM ** (-0.5)
    mixed, totals = [], []
    for pair in range(heads // 2):
        both = turned(q_ref[:, pair * 128 : pair * 128 + 128], cosine, sine)
        both = (both.astype(LOW).astype(WIDE) * scale).astype(LOW)
        qs_ref[:, pair * 128 : pair * 128 + 128] = both
        for side in range(2):
            query = both[:, side * HEAD_DIM : (side + 1) * HEAD_DIM]
            scores = jnp.where(visible, dot(keys, query, ((1,), (1,))), -1e30)
            top = jnp.max(scores, axis=0, keepdims=True)
            weights = jnp.exp(scores - top)
            total = jnp.sum(weights, axis=0, keepdims=True)
            out = dot(values_t, weights.astype(LOW)) / total
            mixed.append(out)
            totals.append(top + jnp.log(total))
    mixed_ref[...] = jnp.concatenate(mixed, axis=0).T.astype(LOW)
    pad = [jnp.zeros_like(totals[0])] * (8 - heads)
    lse_ref[...] = jnp.concatenate(totals + pad, axis=0)


def backward_kernel(
    heads, steps, q_ref, k_ref, v_ref, do_ref, lse_ref, cos_ref, sin_ref, cosk_ref, sink_ref,
    row_ref, col_ref, out_ref, kt_ref, dk_ref, dv_ref,
):
    @pl.when(pl.program_id(0) == 0)
    def _():
        kt_ref[...] = k_ref[...].astype(WIDE).T.astype(LOW)
        dk_ref[...] = jnp.zeros_like(dk_ref)
        dv_ref[...] = jnp.zeros_like(dv_ref)

    keys, values, keys_t = k_ref[...], v_ref[...], kt_ref[...]
    visible = col_ref[...] <= row_ref[...]
    scale = HEAD_DIM ** (-0.5)
    grads = []
    for head in range(heads):
        lanes = slice(head * HEAD_DIM, (head + 1) * HEAD_DIM)
        query, grad_out = q_ref[:, lanes], do_ref[:, lanes]
        scores = dot(keys, query, ((1,), (1,)))
        probs = jnp.where(visible, jnp.exp(scores - lse_ref[head : head + 1, :]), 0.0)
        grad_probs = dot(values, grad_out, ((1,), (1,)))
        product = probs * grad_probs
        delta = jnp.sum(product, axis=0, keepdims=True)
        grad_scores = (product - probs * delta).astype(LOW)
        dv_ref[...] += dot(probs.astype(LOW), grad_out)
        dk_ref[...] += dot(grad_scores, query)
        grads.append(dot(keys_t, grad_scores) * scale)
    grad_q = jnp.concatenate(grads, axis=0).T
    cosine, sine = cos_ref[...], sin_ref[...]
    block = grad_q.shape[0]
    rows = pl.ds(pl.multiple_of(pl.program_id(0) * block, block), block)
    for pair in range(heads // 2):
        lanes = slice(pair * 128, pair * 128 + 128)
        out_ref[rows, lanes] = turned(grad_q[:, lanes], cosine, -sine).astype(LOW)

    @pl.when(pl.program_id(0) == steps - 1)
    def _():
        both = jnp.concatenate([dk_ref[...], dv_ref[...]], axis=1)
        back = turned(both, cosk_ref[...], -sink_ref[...])
        lane = lax.broadcasted_iota(jnp.int32, both.shape, 1)
        out_ref[:, heads * HEAD_DIM :] = jnp.where(lane < HEAD_DIM, back, both).astype(LOW)


def attention_forward(qkv, cosine, sine, places, heads):
    length = qkv.shape[0]
    width = heads * HEAD_DIM
    block = min(256, length)
    whole = lambda shape: pl.BlockSpec(shape, lambda i: (0,) * len(shape))
    rows = lambda columns: pl.BlockSpec((block, columns), lambda i: (i, 0))
    return pl.pallas_call(
        functools.partial(forward_kernel, heads),
        grid=(length // block,),
        in_specs=[
            rows(width),
            pl.BlockSpec((length, 128), lambda i: (0, width // 128)),
            rows(128), rows(128), whole((length, 128)), whole((length, 128)),
            pl.BlockSpec((1, block), lambda i: (0, i)), whole((length, 1)),
        ],
        out_specs=[
            rows(width), pl.BlockSpec((8, block), lambda i: (0, i)), rows(width),
            whole((length, HEAD_DIM)), whole((length, HEAD_DIM)),
        ],
        out_shape=[
            jax.ShapeDtypeStruct((length, width), LOW),
            jax.ShapeDtypeStruct((8, length), WIDE),
            jax.ShapeDtypeStruct((length, width), LOW),
            jax.ShapeDtypeStruct((length, HEAD_DIM), LOW),
            jax.ShapeDtypeStruct((length, HEAD_DIM), LOW),
        ],
        scratch_shapes=[pltpu.VMEM((HEAD_DIM, length), LOW)],
        compiler_params=pltpu.CompilerParams(
            dimension_semantics=("arbitrary",), vmem_limit_bytes=VMEM_LIMIT
        ),
        cost_estimate=pl.CostEstimate(
            flops=COST["forward"] * 10**9, bytes_accessed=8 * length * width, transcendentals=0
        ),
        name="attention_forward",
    )(qkv, qkv, cosine, sine, cosine, sine, places[None, :], places[:, None])


def attention_backward(q_scaled, k_rot, v_low, grad_mixed, lse, cosine, sine, places, heads):
    length = q_scaled.shape[0]
    width = heads * HEAD_DIM
    block = min(256, length)
    steps = length // block
    whole = lambda shape: pl.BlockSpec(shape, lambda i: (0,) * len(shape))
    rows = lambda columns: pl.BlockSpec((block, columns), lambda i: (i, 0))
    return pl.pallas_call(
        functools.partial(backward_kernel, heads, steps),
        grid=(steps,),
        in_specs=[
            rows(width), whole((length, HEAD_DIM)), whole((length, HEAD_DIM)), rows(width),
            pl.BlockSpec((8, block), lambda i: (0, i)),
            rows(128), rows(128), whole((length, 128)), whole((length, 128)),
            pl.BlockSpec((1, block), lambda i: (0, i)), whole((length, 1)),
        ],
        out_specs=whole((length, width + 128)),
        out_shape=jax.ShapeDtypeStruct((length, width + 128), LOW),
        scratch_shapes=[
            pltpu.VMEM((HEAD_DIM, length), LOW),
            pltpu.VMEM((length, HEAD_DIM), WIDE),
            pltpu.VMEM((length, HEAD_DIM), WIDE),
        ],
        compiler_params=pltpu.CompilerParams(
            dimension_semantics=("arbitrary",), vmem_limit_bytes=VMEM_LIMIT
        ),
        cost_estimate=pl.CostEstimate(
            flops=COST["backward"] * 10**9, bytes_accessed=8 * length * width, transcendentals=0
        ),
        name="attention_backward",
    )(
        q_scaled, k_rot, v_low, grad_mixed, lse, cosine, sine, cosine, sine,
        places[None, :], places[:, None],
    )


def columns_kernel(block, gate_ref, up_ref, scale_ref, out_ref):
    scale = scale_ref[...]
    for j in range(out_ref.shape[0]):
        lanes = slice(j * block, (j + 1) * block)
        out_ref[j, :, :block] = (gate_ref[:, lanes].astype(WIDE) * scale).astype(LOW)
        out_ref[j, :, block:] = (up_ref[:, lanes].astype(WIDE) * scale).astype(LOW)


def columns_by_device(w_gate, w_up, scale, block):
    rows, ff_width = w_gate.shape
    devices = ff_width // block
    if block % 128:
        split = [(w.astype(WIDE) * scale).astype(LOW).reshape(rows, devices, block) for w in (w_gate, w_up)]
        return jnp.concatenate(split, axis=2).transpose(1, 0, 2)
    some = 8
    part = pl.BlockSpec((rows, some * block), lambda d: (0, d))
    return pl.pallas_call(
        functools.partial(columns_kernel, block),
        grid=(devices // some,),
        in_specs=[part, part, pl.BlockSpec((rows, 1), lambda d: (0, 0))],
        out_specs=pl.BlockSpec((some, rows, 2 * block), lambda d: (d, 0, 0)),
        out_shape=jax.ShapeDtypeStruct((devices, rows, 2 * block), LOW),
        cost_estimate=pl.CostEstimate(flops=0, bytes_accessed=2 << 20, transcendentals=0),
        name="columns_by_device",
    )(w_gate, w_up, scale)


def assemble_kernel(part_ref, gate_ref, up_ref, scale_ref, gate_out, up_out, gain_out):
    @pl.when(pl.program_id(0) == 0)
    def _():
        gain_out[...] = jnp.zeros_like(gain_out)

    scale = scale_ref[...]
    block = gate_ref.shape[1] // part_ref.shape[0]
    total = jnp.zeros_like(gain_out)
    for j in range(part_ref.shape[0]):
        lanes = slice(j * block, (j + 1) * block)
        gate = part_ref[j, :, :block].astype(WIDE)
        up = part_ref[j, :, block:].astype(WIDE)
        gate_out[:, lanes] = gate * scale
        up_out[:, lanes] = up * scale
        products = gate * gate_ref[:, lanes].astype(WIDE) + up * up_ref[:, lanes].astype(WIDE)
        total = total + jnp.sum(products, axis=1, keepdims=True)
    gain_out[...] += total


def assemble_columns(parts, w_gate, w_up, scale):
    devices, rows, both = parts.shape
    block = both // 2
    ff_width = w_gate.shape[1]
    if block % 128:
        sides = parts.reshape(devices, rows, 2, block).transpose(2, 1, 0, 3).reshape(2, rows, ff_width)
        sides = sides.astype(WIDE)
        products = sides[0] * w_gate.astype(WIDE) + sides[1] * w_up.astype(WIDE)
        return sides[0] * scale, sides[1] * scale, jnp.sum(products, axis=1, keepdims=True)
    some = 8
    columns = pl.BlockSpec((rows, some * block), lambda d: (0, d))
    one = pl.BlockSpec((rows, 1), lambda d: (0, 0))
    return pl.pallas_call(
        assemble_kernel,
        grid=(devices // some,),
        in_specs=[pl.BlockSpec((some, rows, both), lambda d: (d, 0, 0)), columns, columns, one],
        out_specs=[columns, columns, one],
        out_shape=[
            jax.ShapeDtypeStruct((rows, ff_width), WIDE),
            jax.ShapeDtypeStruct((rows, ff_width), WIDE),
            jax.ShapeDtypeStruct((rows, 1), WIDE),
        ],
        compiler_params=pltpu.CompilerParams(
            dimension_semantics=("arbitrary",), vmem_limit_bytes=VMEM_LIMIT
        ),
        cost_estimate=pl.CostEstimate(flops=0, bytes_accessed=8 << 20, transcendentals=0),
        name="assemble_columns",
    )(parts, w_gate, w_up, scale)


def feed_kernel(blocks, steps, per_step, table_ref, *refs):
    even_ref, odd_ref = refs[:2]
    cot_refs = refs[2 : 2 + per_step]
    weights = refs[2 + per_step : 2 + per_step + blocks]
    downs = refs[2 + per_step + blocks : 2 + per_step + 2 * blocks]
    norm_out, cot_out, act_out, low_out, even_out, odd_out = refs[-6:]
    step = pl.program_id(0)
    width = downs[0].shape[0]
    norm = jnp.where(step < steps // 2, even_ref[...], odd_ref[...])
    norm_out[...] = norm
    cot = jnp.concatenate([ref[0] for ref in cot_refs], axis=0)
    cot_out[...] = cot
    term = None
    for j in range(blocks):
        rows = dot(norm, weights[j][...])
        gate, up = rows[:, :width], rows[:, width:]
        grad_act = dot(cot, downs[j][...], ((1,), (1,)))
        sig = 1.0 / (1.0 + jnp.exp(-gate))
        gate_sig = gate * sig
        act_out[j] = (gate_sig * up).astype(LOW)
        grad_up = (grad_act * gate_sig).astype(LOW)
        grad_gate = (grad_act * up * (sig + gate_sig * (1.0 - sig))).astype(LOW)
        low_out[2 * j] = grad_gate
        low_out[2 * j + 1] = grad_up
        more = dot(jnp.concatenate([grad_gate, grad_up], axis=1), weights[j][...], ((1,), (1,)))
        term = more if term is None else term + more
    term = term.astype(LOW)

    @pl.when(step < steps // 2)
    def _():
        even_out[...] = term

    @pl.when(step >= steps // 2)
    def _():
        odd_out[...] = term


def feed_forward(which, even, odd, cots, table, weights, downs, earlier):
    half, width = even.shape
    c_count, tok_rows, _ = cots.shape
    blocks = len(weights)
    block = downs[0].shape[0]
    steps = 4
    rows = 2 * half // steps
    per_step = rows // tok_rows
    total = 4 * half
    first = which * steps
    even_at = lambda i, t: (jnp.minimum(i, steps // 2 - 1), 0)
    odd_at = lambda i, t: (jnp.maximum(i - steps // 2, 0), 0)
    cot_spec = lambda j: pl.BlockSpec(
        (1, tok_rows, width), lambda i, t, j=j: (t[i * per_step + j], 0, 0)
    )
    fixed = lambda shape: pl.BlockSpec(shape, lambda i, t: (0,) * len(shape))
    at = lambda i, t: (first + i, 0)
    out_shape = [
        jax.ShapeDtypeStruct((total, width), LOW),
        jax.ShapeDtypeStruct((total, width), LOW),
        jax.ShapeDtypeStruct((blocks, total, block), LOW),
        jax.ShapeDtypeStruct((2 * blocks, total, block), LOW),
        jax.ShapeDtypeStruct((half, width), LOW),
        jax.ShapeDtypeStruct((half, width), LOW),
    ]
    weights = list(weights) + list(downs)
    inputs = [even, odd] + [cots] * per_step + weights + list(earlier)
    in_specs = (
        [pl.BlockSpec((rows, width), even_at), pl.BlockSpec((rows, width), odd_at)]
        + [cot_spec(j) for j in range(per_step)]
        + [fixed(w.shape) for w in weights]
        + [pl.BlockSpec(memory_space=pl.ANY)] * len(earlier)
    )
    aliases = {1 + len(inputs) - len(earlier) + j: j for j in range(len(earlier))}
    return pl.pallas_call(
        functools.partial(feed_kernel, blocks, steps, per_step),
        grid_spec=pltpu.PrefetchScalarGridSpec(
            num_scalar_prefetch=1,
            grid=(steps,),
            in_specs=in_specs,
            out_specs=[
                pl.BlockSpec((rows, width), at),
                pl.BlockSpec((rows, width), at),
                pl.BlockSpec((blocks, rows, block), lambda i, t: (0, first + i, 0)),
                pl.BlockSpec((2 * blocks, rows, block), lambda i, t: (0, first + i, 0)),
                pl.BlockSpec((rows, width), even_at),
                pl.BlockSpec((rows, width), odd_at),
            ],
        ),
        out_shape=out_shape,
        input_output_aliases=aliases,
        compiler_params=pltpu.CompilerParams(
            dimension_semantics=("arbitrary",), vmem_limit_bytes=VMEM_LIMIT
        ),
        cost_estimate=pl.CostEstimate(flops=COST["feed"] * 10**9, bytes_accessed=8 << 20, transcendentals=0),
        name="feed_forward",
    )(table, *inputs)


def down_kernel(blocks, table_ref, act_ref, *refs):
    out_ref, downs = refs[-1], refs[:-1]
    total = None
    for j in range(blocks):
        part = dot(act_ref[j], downs[j][...])
        total = part if total is None else total + part
    total = total.astype(LOW)
    chips, rows = out_ref.shape[0], out_ref.shape[3]
    for q in range(chips):
        out_ref[table_ref[0] ^ q, 0, 0] = total[q * rows : (q + 1) * rows]


def down_terms_by_device(acts, c_index, c_count, downs, tok_rows):
    blocks, total, block = acts.shape
    width = downs[0].shape[1]
    chips = c_count // 2
    fixed = lambda shape: pl.BlockSpec(shape, lambda i, j, t: (0,) * len(shape))
    place_of = jnp.stack([c_index // 2, c_index % 2]).astype(jnp.int32)
    out = pl.pallas_call(
        functools.partial(down_kernel, blocks),
        grid_spec=pltpu.PrefetchScalarGridSpec(
            num_scalar_prefetch=1,
            grid=(2, 2),
            in_specs=[pl.BlockSpec((blocks, chips * tok_rows, block), lambda i, j, t: (0, 2 * i + j, 0))]
            + [fixed(d.shape) for d in downs],
            out_specs=pl.BlockSpec(
                (chips, 1, 1, tok_rows, width), lambda i, j, t: (0, t[1] ^ j, i, 0, 0)
            ),
        ),
        out_shape=jax.ShapeDtypeStruct((chips, 2, 2, tok_rows, width), LOW),
        compiler_params=pltpu.CompilerParams(vmem_limit_bytes=VMEM_LIMIT),
        cost_estimate=pl.CostEstimate(flops=0, bytes_accessed=8 << 20, transcendentals=0),
        name="down_terms",
    )(place_of, acts, *downs)
    return out.reshape(c_count * 2 * tok_rows, width)


def inverse_rms(rows):
    return lax.rsqrt(jnp.mean(rows * rows, axis=-1, keepdims=True) + EPSILON)


def norm_back(grad_hat, hat_rows, inv_rms):
    return inv_rms * (grad_hat - hat_rows * jnp.mean(grad_hat * hat_rows, axis=-1, keepdims=True))


def per_device(
    tokens, positions, attn_gain, w_query, w_key, w_value, w_out,
    mlp_gain, w_gate, w_up, w_down, cotangent,
):
    f_count, c_count = lax.axis_size("fsdp"), lax.axis_size("ctx")
    f_index, c_index = lax.axis_index("fsdp"), lax.axis_index("ctx")
    devices = f_count * c_count
    top_bit = f_count // 2
    own_tokens, own_cot = tokens[0], cotangent[0]
    tok_rows, width = own_tokens.shape
    piece = w_query.shape[0]
    heads = HEADS // c_count
    q_width = heads * HEAD_DIM
    qkv_width = q_width + 2 * HEAD_DIM
    kv_share = max(1, c_count // KV_HEADS)
    ff_block = w_down.shape[0]
    c_order = ctx_order(c_count)
    f_order = xor_order(top_bit, 1)

    attn_scale, mlp_scale = attn_gain.astype(WIDE)[:, None], mlp_gain.astype(WIDE)[:, None]
    near_tokens = gather_near(own_tokens)
    shares = [
        w_query.reshape(piece, c_count, q_width),
        jnp.repeat(w_key.reshape(piece, KV_HEADS, HEAD_DIM), kv_share, axis=1),
        jnp.repeat(w_value.reshape(piece, KV_HEADS, HEAD_DIM), kv_share, axis=1),
    ]
    qkv_piece = (jnp.concatenate(shares, axis=2).astype(WIDE) * attn_scale[:, :, None]).astype(LOW)
    qkv_piece = qkv_piece.transpose(1, 0, 2)
    steps = Steps()
    add, result, barrier = steps.add, steps.result, steps.barrier
    blocks = range(1, top_bit)
    away = lambda rows: [swap(rows, "fsdp", r) for r in blocks]
    exchange_all = lambda stack: lax.all_to_all(stack, ("fsdp", "ctx"), 0, 0, tiled=True)
    joined = lambda lists: [jnp.concatenate(parts, axis=0) for parts in zip(*lists)]
    half, unit_half, quarter = tok_rows // 2, ff_block // 2, width // 4
    out_route = [(f_count * c + j, j * c_count + c) for c in range(c_count) for j in range(f_count)]
    back_route = [(d, s) for s, d in out_route]

    add("out_route", (), lambda: w_out, lambda w: lax.ppermute(w, ("fsdp", "ctx"), out_route)[None])
    add("out_far", ("out_route",), lambda: [result("out_route")], lambda s: double_fsdp(s, top_bit, 2))
    add("out_near", ("out_far",), lambda: result("out_far"), lambda s: double_fsdp(s, 1, 1))
    add("down_a", (), lambda: w_down[:unit_half], away)
    add("down_b", (), lambda: w_down[unit_half:], away)
    add("columns", (), lambda: (w_gate, w_up), lambda w: columns_by_device(*w, mlp_scale, ff_block))
    add(
        "columns_all", ("columns",), lambda: result("columns"),
        lambda stack: exchange_all(stack).reshape(width, 2 * ff_block),
    )
    for j in range(4):
        add(f"move_{j}", ("columns_all",), lambda: result("columns_all"), lambda c, j=j: away(c[j * quarter : (j + 1) * quarter]))
    gather_rows = lambda rows: lax.all_gather(rows, "ctx", axis=0, tiled=True)
    add("own_cots", (), lambda: own_cot, gather_rows)
    add("cot_a", (), lambda: own_cot[:half], lambda rows: swap(rows, "fsdp", top_bit))
    add("cot_b", (), lambda: own_cot[half:], lambda rows: swap(rows, "fsdp", top_bit))
    add(
        "side_cots", ("cot_a", "cot_b"), lambda: (result("cot_a"), result("cot_b")),
        lambda parts: gather_rows(jnp.concatenate(parts, axis=0)),
    )

    (qkv_piece,) = barrier(0, qkv_piece)
    qkv_piece = exchange_ctx(qkv_piece).reshape(1, c_count * piece, qkv_width)
    small = positions
    for bit in [2 ** j for j in range(1, c_count.bit_length() - 1)] + [1]:
        small = jnp.concatenate([small, swap(small, "ctx", bit)], axis=0)
    int_places = small.reshape(-1)
    qkv_piece, near_tokens = barrier(1, qkv_piece, near_tokens)
    even_tokens = gather_far(own_tokens, near_tokens)
    qkv_parts = double_fsdp([qkv_piece], top_bit, 2)
    half_dim = HEAD_DIM // 2
    frequency = jnp.power(ROPE_BASE, -2.0 * jnp.arange(half_dim, dtype=WIDE) / HEAD_DIM)
    angles = int_places.astype(WIDE)[:, None] * frequency[None, :]
    cosine, sine = jnp.cos(angles), jnp.sin(angles)
    cosine = jnp.concatenate([cosine] * 4, axis=1)
    sine = jnp.concatenate([-sine, sine, -sine, sine], axis=1)
    qkv_parts, cosine, sine, even_tokens = barrier(2, qkv_parts, cosine, sine, even_tokens)
    quad_tokens, other_tokens = gather_core(even_tokens)
    qkv_parts = double_fsdp(qkv_parts, 1, 1)

    def first_norm(rows):
        rows = rows.astype(WIDE)
        return (rows * inverse_rms(rows)).astype(LOW)

    normed_first = [first_norm(quad_tokens), first_norm(other_tokens)]

    qkv_parts, normed_first = barrier(3, qkv_parts, normed_first)
    w_qkv = place(qkv_parts, f_order, f_index)
    qkv = jnp.concatenate([dot(rows, w_qkv) for rows in normed_first], axis=0)
    mixed, lse, q_scaled, k_rot, v_low = attention_forward(qkv, cosine, sine, int_places, heads)
    (mixed,) = barrier(4, mixed)

    w_out_rows = place(result("out_near"), f_order, f_index)
    middle = mixed.shape[0] // 2
    odd_out = scatter_core(dot(mixed[middle:], w_out_rows, out=LOW), COST["split_out"])
    even_out = dot(mixed[:middle], w_out_rows, out=LOW)
    odd_out, even_out = barrier(5, odd_out, even_out)
    state = scatter_far(scatter_sum(even_out, odd_out))
    inputs = own_tokens.astype(WIDE)
    inv_first = inverse_rms(inputs)
    hat_first = inputs * inv_first
    all_first = jnp.concatenate(normed_first, axis=0)
    state, hat_first, all_first = barrier(6, state, hat_first, all_first)
    (state,) = barrier(7, scatter_near(state))
    hidden = inputs + scatter_end(state)
    inv_second = inverse_rms(hidden)
    hat_second = hidden * inv_second
    normed_own = hat_second.astype(LOW)

    near_norm = gather_near(normed_own)
    side_norm = swap(normed_own, "fsdp", top_bit)
    near_norm, side_norm = barrier(8, near_norm, side_norm)
    even_norm = gather_far(normed_own, near_norm)
    near_side = gather_near(side_norm)
    norm_pieces = list(gather_core(even_norm))
    (norm_pieces,) = barrier(9, norm_pieces)
    columns = [result("columns_all")] + joined([result(f"move_{j}") for j in range(4)])
    downs = [w_down] + joined([result("down_a"), result("down_b")])
    table = jnp.array(c_order, jnp.int32) ^ c_index
    by_block = lambda rows: rows.reshape(c_count, tok_rows, width)

    weights = (table, columns, downs)
    *buffers, even_zero, odd_zero = feed_forward(0, *norm_pieces, by_block(result("own_cots")), *weights, [])
    near_side, buffers, even_zero, odd_zero = barrier(10, near_side, buffers, even_zero, odd_zero)
    side_norms = gather_core(gather_far(side_norm, near_side))
    quad_zero = scatter_sum(even_zero, scatter_core(odd_zero))
    side_norms, quad_zero, buffers, side_cots = barrier(
        11, side_norms, quad_zero, buffers, result("side_cots")
    )
    state_zero = scatter_far(quad_zero)
    *buffers, even_one, odd_one = feed_forward(1, *side_norms, by_block(side_cots), *weights, buffers)
    all_norms, all_cots, all_acts, all_lows = buffers

    product = lambda left, right: dot(left, right, ((0,), (0,)), LOW)
    add(
        "gate_away", (), lambda: (all_norms, all_lows),
        lambda p: [product(p[0], p[1][2 * j]) for j in blocks],
    )
    add(
        "up_away", (), lambda: (all_norms, all_lows),
        lambda p: [product(p[0], p[1][2 * j + 1]) for j in blocks],
    )
    add("down_away", (), lambda: (all_acts, all_cots), lambda p: [product(p[0][j], p[1]) for j in blocks])
    add("gate_own", (), lambda: (all_norms, all_lows), lambda p: product(p[0], p[1][0]))
    add("up_own", (), lambda: (all_norms, all_lows), lambda p: product(p[0], p[1][1]))
    move_back = lambda parts: [swap(part, "fsdp", r) for r, part in enumerate(parts, 1)]
    add("gate_move", ("gate_away",), lambda: result("gate_away"), move_back)
    add("up_move", ("up_away",), lambda: result("up_away"), move_back)
    add("down_move", ("down_away",), lambda: result("down_away"), move_back)
    add(
        "down_terms", (), lambda: all_acts,
        lambda acts: down_terms_by_device(acts, c_index, c_count, downs, tok_rows),
    )
    add(
        "out_rows", ("down_terms",), lambda: result("down_terms"),
        lambda t: lax.psum_scatter(t, "ctx", scatter_dimension=0, tiled=True).reshape(2, tok_rows, width),
    )
    add("side_out", ("out_rows",), lambda: result("out_rows")[1], lambda rows: swap(rows, "fsdp", top_bit))

    def sum_by_device(own, parts):
        total = sum([part.astype(WIDE) for part in parts], own.astype(WIDE)).astype(LOW)
        return total.reshape(devices, piece, ff_block)

    add(
        "both_all", ("gate_own", "gate_move", "up_own", "up_move"), lambda: [result(n) for n in ("gate_own", "gate_move", "up_own", "up_move")],
        lambda p: exchange_all(
            jnp.concatenate([sum_by_device(p[0], p[1]), sum_by_device(p[2], p[3])], axis=2)
        ),
    )
    add(
        "down_own", (), lambda: (all_acts, all_cots),
        lambda p: dot(p[0][0], p[1], ((0,), (0,))),
    )
    add(
        "assembled",
        ("both_all",),
        lambda: result("both_all"),
        lambda parts: assemble_columns(parts, w_gate, w_up, mlp_scale),
    )
    state_zero, odd_one, even_one = barrier(12, state_zero, odd_one, even_one)
    odd_one = scatter_core(odd_one)
    state_zero = scatter_near(state_zero)
    quad_one = scatter_sum(even_one, odd_one)
    quad_one, state_zero = barrier(13, quad_one, state_zero)
    (state_one,) = barrier(14, scatter_far(quad_one))
    (state_one,) = barrier(15, scatter_near(state_one))
    side_one = swap(scatter_end(state_one).astype(LOW), "fsdp", top_bit)
    (side_one,) = barrier(16, side_one)
    grad_normed = scatter_end(state_zero) + side_one.astype(WIDE)

    grad_hidden = own_cot.astype(WIDE) + norm_back(grad_normed, hat_second, inv_second)
    hidden_low = grad_hidden.astype(LOW)
    (near_hidden,) = barrier(17, gather_near(hidden_low))
    (even_hidden,) = barrier(18, gather_far(hidden_low, near_hidden))
    hidden_halves = gather_core(even_hidden, COST["split_hidden"])
    grad_mixed = jnp.concatenate([dot(h, w_out_rows, ((1,), (1,)), LOW) for h in hidden_halves], axis=0)

    def out_product(p):
        total = dot(p[0][:middle], p[1][0], ((0,), (0,))) + dot(p[0][middle:], p[1][1], ((0,), (0,)))
        return total.astype(LOW).reshape(f_count, piece, width)

    add("out_part", (), lambda: (mixed, hidden_halves), out_product)
    add("out_halved", ("out_part",), lambda: result("out_part"), lambda p: halve_near(p, f_index))
    add("out_sum", ("out_halved",), lambda: result("out_halved"), lambda p: halve_far(p, f_index, top_bit))
    add("out_grad", ("out_sum",), lambda: result("out_sum"), lambda p: lax.ppermute(p, ("fsdp", "ctx"), back_route))

    (grad_mixed,) = barrier(19, grad_mixed)
    grad_qkv = attention_backward(
        q_scaled, k_rot, v_low, grad_mixed, lse, cosine, sine, int_places, heads
    )
    grad_qkv, all_first = barrier(20, grad_qkv, all_first)

    qkv_part = dot(all_first, grad_qkv, ((0,), (0,)), LOW)
    qkv_part = qkv_part.reshape(f_count, c_count * piece, qkv_width)
    grad_qkv, qkv_part = tie(grad_qkv, qkv_part)
    qkv_sum = halve_near(qkv_part, f_index)
    (grad_qkv,) = barrier(21, grad_qkv)
    odd = scatter_core(dot(grad_qkv[middle:], w_qkv, ((1,), (1,)), LOW), COST["split_last"])
    even = dot(grad_qkv[:middle], w_qkv, ((1,), (1,)), LOW)
    quad = scatter_sum(even, odd)
    qkv_sum, quad = barrier(22, qkv_sum, quad)
    state = scatter_far(quad)
    qkv_sum = halve_far(qkv_sum, f_index, top_bit)
    state, qkv_sum = barrier(23, state, qkv_sum)
    qkv_sum = exchange_ctx(qkv_sum.reshape(c_count, piece, qkv_width))
    (state,) = barrier(24, scatter_near(state))
    (qkv_sum,) = barrier(25, qkv_sum)
    grad_normed = scatter_end(state)
    input_grad = grad_hidden + norm_back(grad_normed, hat_first, inv_first)
    gate_grad, up_grad, mlp_gain_grad = result("assembled")
    mlp_gain_grad = mlp_gain_grad[:, 0]
    out_grad = result("out_grad").astype(WIDE)
    down_grad = result("down_own")
    for part in result("down_move"):
        down_grad = down_grad + part.astype(WIDE)
    side_out, out_rows = result("side_out"), result("out_rows")
    output = hidden + out_rows[0].astype(WIDE) + side_out.astype(WIDE)

    qkv_sum = qkv_sum.astype(WIDE)
    query_grad = qkv_sum[:, :, :q_width].transpose(1, 0, 2).reshape(piece, -1)
    kv_sum = qkv_sum[:, :, q_width:].reshape(KV_HEADS, kv_share, piece, 2, HEAD_DIM).sum(axis=1)
    key_grad = kv_sum[:, :, 0].transpose(1, 0, 2).reshape(piece, -1)
    value_grad = kv_sum[:, :, 1].transpose(1, 0, 2).reshape(piece, -1)
    attn_gain_grad = (
        jnp.sum(query_grad * w_query.astype(WIDE), axis=1)
        + jnp.sum(key_grad * w_key.astype(WIDE), axis=1)
        + jnp.sum(value_grad * w_value.astype(WIDE), axis=1)
    )
    query_grad, key_grad, value_grad = (g * attn_scale for g in (query_grad, key_grad, value_grad))

    return (
        output.astype(LOW)[None],
        input_grad.astype(LOW)[None],
        attn_gain_grad,
        query_grad,
        key_grad,
        value_grad,
        out_grad,
        mlp_gain_grad,
        gate_grad,
        up_grad,
        down_grad,
    )


def solution(mesh):
    rows = P(("fsdp", "ctx"), None)
    vector = P(("fsdp", "ctx"))
    tokens = P("fsdp", "ctx", None)
    in_specs = (
        tokens, P("fsdp", "ctx"), vector, rows, rows, rows, rows, vector, rows, rows, rows, tokens,
    )
    out_specs = (
        tokens, tokens, vector, rows, rows, rows, rows, vector, rows, rows, rows,
    )
    return jax.shard_map(
        per_device, mesh=mesh, in_specs=in_specs, out_specs=out_specs, check_vma=False
    )
```

```python
import functools

import jax
import jax.numpy as jnp
from jax import lax
from jax.experimental import pallas as pl
from jax.experimental.pallas import tpu as pltpu
from jax.sharding import PartitionSpec as P

HEADS = 32
KV_HEADS = 8
HEAD_DIM = 64
EPSILON = 1e-05
ROPE_BASE = 500000.0
VMEM_LIMIT = 56 * 1024 * 1024

WHEN = {
    "out_route": (0, 1),
    "down_a": (0, 2),
    "down_b": (6, 9),
    "own_cots": (1, 9),
    "columns": (1, 2),
    "out_far": (2, 3),
    "cot_a": (2, 3),
    "out_near": (3, 99),
    "columns_all": (3, 4),
    "cot_b": (4, 6),
    "move_0": (5, 7),
    "move_1": (5, 6),
    "move_2": (6, 8),
    "move_3": (6, 8),
    "side_cots": (6, 11),
    "gate_away": (12, 13),
    "gate_move": (13, 18),
    "up_away": (13, 14),
    "down_away": (14, 15),
    "gate_own": (15, 16),
    "down_terms": (15, 16),
    "up_move": (16, 18),
    "up_own": (16, 17),
    "out_rows": (18, 23),
    "both_all": (18, 22),
    "out_part": (18, 19),
    "out_halved": (19, 20),
    "out_sum": (20, 22),
    "out_grad": (23, 25),
    "side_out": (23, 25),
    "down_own": (20, 22),
    "assembled": (23, 24),
    "down_move_a": (21, 24),
    "down_move_b": (21, 24),
}
COST = {"forward": 0, "backward": 0, "feed": 0, "split_out": 1, "split_last": 2, "split_hidden": 2}
LOW = jnp.bfloat16
WIDE = jnp.float32


def dot(left, right, dims=((1,), (0,)), out=WIDE):
    return lax.dot_general(left, right, (dims, ((), ())), preferred_element_type=WIDE).astype(out)


def tie(*values):
    return lax.optimization_barrier(values)


class Steps:
    def __init__(self):
        self.waiting, self.flying, self.ended = {}, {}, {}

    def add(self, name, needs, operand, task):
        self.waiting[name] = (needs, operand, task)

    def result(self, name):
        if name in self.waiting:
            _, operand, task = self.waiting.pop(name)
            self.flying[name] = task(operand())
        return self.ended[name] if name in self.ended else self.flying[name]

    def barrier(self, step, *values):
        starting = [n for n in self.waiting if WHEN[n][0] <= step]
        later = [n for n in starting if any(need in self.waiting for need in self.waiting[n][0])]
        tasks = [(n, *self.waiting.pop(n)[1:]) for n in starting if n not in later]
        operands = [operand() for _, operand, _ in tasks]
        ending = [n for n in self.flying if WHEN[n][1] <= step and n not in self.ended]
        values, operands, results = tie(values, operands, [self.flying[n] for n in ending])
        self.ended.update(zip(ending, results))
        for (name, _, task), operand in zip(tasks, operands):
            self.flying[name] = task(operand)
        for name in later:
            self.result(name)
        return values


def swap(block, axis, mask):
    count = lax.axis_size(axis)
    return lax.ppermute(block, axis, [(i, i ^ mask) for i in range(count)])


def pick(stack, index):
    return lax.dynamic_index_in_dim(stack, index, 0, keepdims=False)


def in_order(pieces, base):
    out = jnp.zeros((len(pieces),) + pieces[0].shape, pieces[0].dtype)
    for r, piece in enumerate(pieces):
        out = lax.dynamic_update_index_in_dim(out, piece, base ^ r, 0)
    return out


def ctx_order(count):
    order = [0]
    bit = 2
    while bit < count:
        order = order + [k ^ bit for k in order]
        bit *= 2
    return order + [k ^ 1 for k in order]


def gather_near(block):
    count = lax.axis_size("ctx")
    return (swap(block, "ctx", 2), swap(block, "ctx", 4)) if count == 8 else ()


def gather_far(block, near):
    count = lax.axis_size("ctx")
    if count == 8:
        near_x, near_y = near
        half = block.shape[0] // 2
        return block, near_x, near_y, swap(near_y[:half], "ctx", 2), swap(near_x[half:], "ctx", 4)
    even, bit = (block,), 2
    while bit < count:
        even = even + tuple(swap(part, "ctx", bit) for part in even)
        bit *= 2
    return even


def swap_core(rows, parts):
    size = rows.shape[0] // parts
    pieces = [swap(rows[j * size : (j + 1) * size], "ctx", 1) for j in range(parts)]
    return pieces[0] if parts == 1 else jnp.concatenate(pieces, axis=0)


def gather_core(even, parts=1):
    quad = jnp.concatenate(even, axis=0)
    return quad, swap_core(quad, parts)


def scatter_core(odd, parts=1):
    return swap_core(odd, parts)


def scatter_sum(even, odd):
    return (even.astype(WIDE) + odd.astype(WIDE)).astype(LOW)


def scatter_far(quad):
    count = lax.axis_size("ctx")
    if count != 8:
        return (quad.astype(WIDE),)
    rows = quad.shape[0] // 4
    half = rows // 2
    own, to_x, to_y, far = (quad[j * rows : (j + 1) * rows] for j in range(4))
    far_x, far_y = swap(far[half:], "ctx", 2), swap(far[:half], "ctx", 4)
    by_x, by_y = swap(to_x[half:], "ctx", 2), swap(to_y[:half], "ctx", 4)
    return own, to_x[:half], to_y[half:], by_x, by_y, far_x, far_y


def scatter_near(state):
    count = lax.axis_size("ctx")
    if count != 8:
        (quad,) = state
        bit = count // 2
        while bit >= 2:
            middle = quad.shape[0] // 2
            quad = quad[:middle] + swap(quad[middle:].astype(LOW), "ctx", bit).astype(WIDE)
            bit //= 2
        return (quad,)
    own, to_x, to_y, by_x, by_y, far_x, far_y = state
    last_x = swap((to_x.astype(WIDE) + far_y.astype(WIDE)).astype(LOW), "ctx", 2)
    last_y = swap((to_y.astype(WIDE) + far_x.astype(WIDE)).astype(LOW), "ctx", 4)
    return own, by_x, by_y, last_x, last_y


def scatter_end(state):
    if len(state) == 1:
        return state[0]
    own, by_x, by_y, last_x, last_y = state
    half = last_x.shape[0]
    top = own[:half].astype(WIDE) + last_x.astype(WIDE) + by_y.astype(WIDE)
    low = own[half:].astype(WIDE) + by_x.astype(WIDE) + last_y.astype(WIDE)
    return jnp.concatenate([top, low], axis=0)


def exchange_ctx(stack):
    return lax.all_to_all(stack, "ctx", 0, 0, tiled=True)


def double_fsdp(stacks, first, last):
    bit = first
    while bit >= last:
        sent = stacks[0] if len(stacks) == 1 else jnp.concatenate(stacks, axis=0)
        stacks = stacks + [swap(sent, "fsdp", bit)]
        bit //= 2
    return stacks


def xor_order(first, last):
    order, bit = [0], first
    while bit >= last:
        order = order + [k ^ bit for k in order]
        bit //= 2
    return order


def place_kernel(masks, rows, base_ref, *refs):
    out_ref = refs[-1]
    masks = iter(masks)
    for part in refs[:-1]:
        for j in range(part.shape[0]):
            start = pl.multiple_of((base_ref[0] ^ next(masks)) * rows, 16)
            out_ref[pl.ds(start, rows), :] = part[j]


def place(parts, masks, base):
    _, rows, columns = parts[0].shape
    total = len(masks) * rows
    whole = pl.BlockSpec(memory_space=pltpu.VMEM)
    return pl.pallas_call(
        functools.partial(place_kernel, masks, rows),
        in_specs=[pl.BlockSpec(memory_space=pltpu.SMEM)] + [whole] * len(parts),
        out_specs=whole,
        out_shape=jax.ShapeDtypeStruct((total, columns), parts[0].dtype),
        compiler_params=pltpu.CompilerParams(vmem_limit_bytes=VMEM_LIMIT),
        cost_estimate=pl.CostEstimate(flops=0, bytes_accessed=total * columns * 2, transcendentals=0),
        name="place",
    )(base.reshape(1), *parts)


def halve_fsdp(stack, base, first, last):
    bit = first
    while bit >= last:
        low = stack.shape[0] // 2
        side = (base // bit) % 2
        pair = stack.reshape((2, low) + stack.shape[1:])
        mine, theirs = pick(pair, side), pick(pair, 1 - side)
        stack = (mine.astype(WIDE) + swap(theirs, "fsdp", bit).astype(WIDE)).astype(LOW)
        bit //= 2
    return stack if stack.shape[0] > 1 else stack[0]


def halve_near(stack, base):
    pair = stack.reshape((stack.shape[0] // 2, 2) + stack.shape[1:]).swapaxes(0, 1)
    mine, theirs = pick(pair, base % 2), pick(pair, 1 - base % 2)
    return (mine.astype(WIDE) + swap(theirs, "fsdp", 1).astype(WIDE)).astype(LOW)


def halve_far(stack, base, first):
    return halve_fsdp(stack, base, first, 2)


def turned(block, cosine, sine):
    lane = lax.broadcasted_iota(jnp.int32, block.shape, 1)
    first = (lane % HEAD_DIM) < HEAD_DIM // 2
    width = block.shape[1]
    other = jnp.where(
        first, pltpu.roll(block, width - HEAD_DIM // 2, 1), pltpu.roll(block, HEAD_DIM // 2, 1)
    )
    return block * cosine + other * sine


def forward_kernel(
    heads, q_ref, kv_ref, cos_ref, sin_ref, cosk_ref, sink_ref, row_ref, col_ref,
    mixed_ref, lse_ref, qs_ref, kr_ref, vl_ref, vt_ref,
):
    @pl.when(pl.program_id(0) == 0)
    def _():
        keys = turned(kv_ref[...], cosk_ref[...], sink_ref[...])
        kr_ref[...] = keys[:, :HEAD_DIM].astype(LOW)
        values = kv_ref[...][:, HEAD_DIM:].astype(LOW)
        vl_ref[...] = values
        vt_ref[...] = values.astype(WIDE).T.astype(LOW)

    cosine, sine = cos_ref[...], sin_ref[...]
    keys = kr_ref[...]
    values_t = vt_ref[...]
    visible = col_ref[...] <= row_ref[...]
    scale = HEAD_DIM ** (-0.5)
    mixed, totals = [], []
    for pair in range(heads // 2):
        both = turned(q_ref[:, pair * 128 : pair * 128 + 128], cosine, sine)
        both = (both.astype(LOW).astype(WIDE) * scale).astype(LOW)
        qs_ref[:, pair * 128 : pair * 128 + 128] = both
        for side in range(2):
            query = both[:, side * HEAD_DIM : (side + 1) * HEAD_DIM]
            scores = jnp.where(visible, dot(keys, query, ((1,), (1,))), -1e30)
            top = jnp.max(scores, axis=0, keepdims=True)
            weights = jnp.exp(scores - top)
            total = jnp.sum(weights, axis=0, keepdims=True)
            out = dot(values_t, weights.astype(LOW)) / total
            mixed.append(out)
            totals.append(top + jnp.log(total))
    mixed_ref[...] = jnp.concatenate(mixed, axis=0).T.astype(LOW)
    pad = [jnp.zeros_like(totals[0])] * (8 - heads)
    lse_ref[...] = jnp.concatenate(totals + pad, axis=0)


def backward_kernel(
    heads, steps, q_ref, k_ref, v_ref, do_ref, lse_ref, cos_ref, sin_ref, cosk_ref, sink_ref,
    row_ref, col_ref, out_ref, kt_ref, dk_ref, dv_ref,
):
    @pl.when(pl.program_id(0) == 0)
    def _():
        kt_ref[...] = k_ref[...].astype(WIDE).T.astype(LOW)
        dk_ref[...] = jnp.zeros_like(dk_ref)
        dv_ref[...] = jnp.zeros_like(dv_ref)

    keys, values, keys_t = k_ref[...], v_ref[...], kt_ref[...]
    visible = col_ref[...] <= row_ref[...]
    scale = HEAD_DIM ** (-0.5)
    grads = []
    for head in range(heads):
        lanes = slice(head * HEAD_DIM, (head + 1) * HEAD_DIM)
        query, grad_out = q_ref[:, lanes], do_ref[:, lanes]
        scores = dot(keys, query, ((1,), (1,)))
        probs = jnp.where(visible, jnp.exp(scores - lse_ref[head : head + 1, :]), 0.0)
        grad_probs = dot(values, grad_out, ((1,), (1,)))
        product = probs * grad_probs
        delta = jnp.sum(product, axis=0, keepdims=True)
        grad_scores = (product - probs * delta).astype(LOW)
        dv_ref[...] += dot(probs.astype(LOW), grad_out)
        dk_ref[...] += dot(grad_scores, query)
        grads.append(dot(keys_t, grad_scores) * scale)
    grad_q = jnp.concatenate(grads, axis=0).T
    cosine, sine = cos_ref[...], sin_ref[...]
    block = grad_q.shape[0]
    rows = pl.ds(pl.multiple_of(pl.program_id(0) * block, block), block)
    for pair in range(heads // 2):
        lanes = slice(pair * 128, pair * 128 + 128)
        out_ref[rows, lanes] = turned(grad_q[:, lanes], cosine, -sine).astype(LOW)

    @pl.when(pl.program_id(0) == steps - 1)
    def _():
        both = jnp.concatenate([dk_ref[...], dv_ref[...]], axis=1)
        back = turned(both, cosk_ref[...], -sink_ref[...])
        lane = lax.broadcasted_iota(jnp.int32, both.shape, 1)
        out_ref[:, heads * HEAD_DIM :] = jnp.where(lane < HEAD_DIM, back, both).astype(LOW)


def attention_forward(qkv, cosine, sine, places, heads):
    length = qkv.shape[0]
    width = heads * HEAD_DIM
    block = min(256, length)
    whole = lambda shape: pl.BlockSpec(shape, lambda i: (0,) * len(shape))
    rows = lambda columns: pl.BlockSpec((block, columns), lambda i: (i, 0))
    return pl.pallas_call(
        functools.partial(forward_kernel, heads),
        grid=(length // block,),
        in_specs=[
            rows(width),
            pl.BlockSpec((length, 128), lambda i: (0, width // 128)),
            rows(128), rows(128), whole((length, 128)), whole((length, 128)),
            pl.BlockSpec((1, block), lambda i: (0, i)), whole((length, 1)),
        ],
        out_specs=[
            rows(width), pl.BlockSpec((8, block), lambda i: (0, i)), rows(width),
            whole((length, HEAD_DIM)), whole((length, HEAD_DIM)),
        ],
        out_shape=[
            jax.ShapeDtypeStruct((length, width), LOW),
            jax.ShapeDtypeStruct((8, length), WIDE),
            jax.ShapeDtypeStruct((length, width), LOW),
            jax.ShapeDtypeStruct((length, HEAD_DIM), LOW),
            jax.ShapeDtypeStruct((length, HEAD_DIM), LOW),
        ],
        scratch_shapes=[pltpu.VMEM((HEAD_DIM, length), LOW)],
        compiler_params=pltpu.CompilerParams(
            dimension_semantics=("arbitrary",), vmem_limit_bytes=VMEM_LIMIT
        ),
        cost_estimate=pl.CostEstimate(
            flops=COST["forward"] * 10**9, bytes_accessed=8 * length * width, transcendentals=0
        ),
        name="attention_forward",
    )(qkv, qkv, cosine, sine, cosine, sine, places[None, :], places[:, None])


def attention_backward(q_scaled, k_rot, v_low, grad_mixed, lse, cosine, sine, places, heads):
    length = q_scaled.shape[0]
    width = heads * HEAD_DIM
    block = min(256, length)
    steps = length // block
    whole = lambda shape: pl.BlockSpec(shape, lambda i: (0,) * len(shape))
    rows = lambda columns: pl.BlockSpec((block, columns), lambda i: (i, 0))
    return pl.pallas_call(
        functools.partial(backward_kernel, heads, steps),
        grid=(steps,),
        in_specs=[
            rows(width), whole((length, HEAD_DIM)), whole((length, HEAD_DIM)), rows(width),
            pl.BlockSpec((8, block), lambda i: (0, i)),
            rows(128), rows(128), whole((length, 128)), whole((length, 128)),
            pl.BlockSpec((1, block), lambda i: (0, i)), whole((length, 1)),
        ],
        out_specs=whole((length, width + 128)),
        out_shape=jax.ShapeDtypeStruct((length, width + 128), LOW),
        scratch_shapes=[
            pltpu.VMEM((HEAD_DIM, length), LOW),
            pltpu.VMEM((length, HEAD_DIM), WIDE),
            pltpu.VMEM((length, HEAD_DIM), WIDE),
        ],
        compiler_params=pltpu.CompilerParams(
            dimension_semantics=("arbitrary",), vmem_limit_bytes=VMEM_LIMIT
        ),
        cost_estimate=pl.CostEstimate(
            flops=COST["backward"] * 10**9, bytes_accessed=8 * length * width, transcendentals=0
        ),
        name="attention_backward",
    )(
        q_scaled, k_rot, v_low, grad_mixed, lse, cosine, sine, cosine, sine,
        places[None, :], places[:, None],
    )


def columns_kernel(block, gate_ref, up_ref, scale_ref, out_ref):
    scale = scale_ref[...]
    for j in range(out_ref.shape[0]):
        lanes = slice(j * block, (j + 1) * block)
        out_ref[j, :, :block] = (gate_ref[:, lanes].astype(WIDE) * scale).astype(LOW)
        out_ref[j, :, block:] = (up_ref[:, lanes].astype(WIDE) * scale).astype(LOW)


def columns_by_device(w_gate, w_up, scale, block):
    rows, ff_width = w_gate.shape
    devices = ff_width // block
    if block % 128:
        split = [(w.astype(WIDE) * scale).astype(LOW).reshape(rows, devices, block) for w in (w_gate, w_up)]
        return jnp.concatenate(split, axis=2).transpose(1, 0, 2)
    some = 8
    part = pl.BlockSpec((rows, some * block), lambda d: (0, d))
    return pl.pallas_call(
        functools.partial(columns_kernel, block),
        grid=(devices // some,),
        in_specs=[part, part, pl.BlockSpec((rows, 1), lambda d: (0, 0))],
        out_specs=pl.BlockSpec((some, rows, 2 * block), lambda d: (d, 0, 0)),
        out_shape=jax.ShapeDtypeStruct((devices, rows, 2 * block), LOW),
        cost_estimate=pl.CostEstimate(flops=0, bytes_accessed=2 << 20, transcendentals=0),
        name="columns_by_device",
    )(w_gate, w_up, scale)


def assemble_kernel(part_ref, gate_ref, up_ref, scale_ref, gate_out, up_out, gain_out):
    @pl.when(pl.program_id(0) == 0)
    def _():
        gain_out[...] = jnp.zeros_like(gain_out)

    scale = scale_ref[...]
    block = gate_ref.shape[1] // part_ref.shape[0]
    total = jnp.zeros_like(gain_out)
    for j in range(part_ref.shape[0]):
        lanes = slice(j * block, (j + 1) * block)
        gate = part_ref[j, :, :block].astype(WIDE)
        up = part_ref[j, :, block:].astype(WIDE)
        gate_out[:, lanes] = gate * scale
        up_out[:, lanes] = up * scale
        products = gate * gate_ref[:, lanes].astype(WIDE) + up * up_ref[:, lanes].astype(WIDE)
        total = total + jnp.sum(products, axis=1, keepdims=True)
    gain_out[...] += total


def assemble_columns(parts, w_gate, w_up, scale):
    devices, rows, both = parts.shape
    block = both // 2
    ff_width = w_gate.shape[1]
    if block % 128:
        sides = parts.reshape(devices, rows, 2, block).transpose(2, 1, 0, 3).reshape(2, rows, ff_width)
        sides = sides.astype(WIDE)
        products = sides[0] * w_gate.astype(WIDE) + sides[1] * w_up.astype(WIDE)
        return sides[0] * scale, sides[1] * scale, jnp.sum(products, axis=1, keepdims=True)
    some = 8
    columns = pl.BlockSpec((rows, some * block), lambda d: (0, d))
    one = pl.BlockSpec((rows, 1), lambda d: (0, 0))
    return pl.pallas_call(
        assemble_kernel,
        grid=(devices // some,),
        in_specs=[pl.BlockSpec((some, rows, both), lambda d: (d, 0, 0)), columns, columns, one],
        out_specs=[columns, columns, one],
        out_shape=[
            jax.ShapeDtypeStruct((rows, ff_width), WIDE),
            jax.ShapeDtypeStruct((rows, ff_width), WIDE),
            jax.ShapeDtypeStruct((rows, 1), WIDE),
        ],
        compiler_params=pltpu.CompilerParams(
            dimension_semantics=("arbitrary",), vmem_limit_bytes=VMEM_LIMIT
        ),
        cost_estimate=pl.CostEstimate(flops=0, bytes_accessed=8 << 20, transcendentals=0),
        name="assemble_columns",
    )(parts, w_gate, w_up, scale)


def feed_kernel(blocks, steps, per_step, table_ref, *refs):
    even_ref, odd_ref = refs[:2]
    cot_refs = refs[2 : 2 + per_step]
    weights = refs[2 + per_step : 2 + per_step + blocks]
    downs = refs[2 + per_step + blocks : 2 + per_step + 2 * blocks]
    norm_out, cot_out, act_out, low_out, even_out, odd_out = refs[-6:]
    step = pl.program_id(0)
    width = downs[0].shape[0]
    norm = jnp.where(step < steps // 2, even_ref[...], odd_ref[...])
    norm_out[...] = norm
    cot = jnp.concatenate([ref[0] for ref in cot_refs], axis=0)
    cot_out[...] = cot
    term = None
    for j in range(blocks):
        rows = dot(norm, weights[j][...])
        gate, up = rows[:, :width], rows[:, width:]
        grad_act = dot(cot, downs[j][...], ((1,), (1,)))
        sig = 1.0 / (1.0 + jnp.exp(-gate))
        gate_sig = gate * sig
        act_out[j] = (gate_sig * up).astype(LOW)
        grad_up = (grad_act * gate_sig).astype(LOW)
        grad_gate = (grad_act * up * (sig + gate_sig * (1.0 - sig))).astype(LOW)
        low_out[2 * j] = grad_gate
        low_out[2 * j + 1] = grad_up
        more = dot(jnp.concatenate([grad_gate, grad_up], axis=1), weights[j][...], ((1,), (1,)))
        term = more if term is None else term + more
    term = term.astype(LOW)

    @pl.when(step < steps // 2)
    def _():
        even_out[...] = term

    @pl.when(step >= steps // 2)
    def _():
        odd_out[...] = term


def feed_forward(which, even, odd, cots, table, weights, downs, earlier):
    half, width = even.shape
    c_count, tok_rows, _ = cots.shape
    blocks = len(weights)
    block = downs[0].shape[0]
    steps = 4
    rows = 2 * half // steps
    per_step = rows // tok_rows
    total = 4 * half
    first = which * steps
    even_at = lambda i, t: (jnp.minimum(i, steps // 2 - 1), 0)
    odd_at = lambda i, t: (jnp.maximum(i - steps // 2, 0), 0)
    cot_spec = lambda j: pl.BlockSpec(
        (1, tok_rows, width), lambda i, t, j=j: (t[i * per_step + j], 0, 0)
    )
    fixed = lambda shape: pl.BlockSpec(shape, lambda i, t: (0,) * len(shape))
    at = lambda i, t: (first + i, 0)
    out_shape = [
        jax.ShapeDtypeStruct((total, width), LOW),
        jax.ShapeDtypeStruct((total, width), LOW),
        jax.ShapeDtypeStruct((blocks, total, block), LOW),
        jax.ShapeDtypeStruct((2 * blocks, total, block), LOW),
        jax.ShapeDtypeStruct((half, width), LOW),
        jax.ShapeDtypeStruct((half, width), LOW),
    ]
    weights = list(weights) + list(downs)
    inputs = [even, odd] + [cots] * per_step + weights + list(earlier)
    in_specs = (
        [pl.BlockSpec((rows, width), even_at), pl.BlockSpec((rows, width), odd_at)]
        + [cot_spec(j) for j in range(per_step)]
        + [fixed(w.shape) for w in weights]
        + [pl.BlockSpec(memory_space=pl.ANY)] * len(earlier)
    )
    aliases = {1 + len(inputs) - len(earlier) + j: j for j in range(len(earlier))}
    return pl.pallas_call(
        functools.partial(feed_kernel, blocks, steps, per_step),
        grid_spec=pltpu.PrefetchScalarGridSpec(
            num_scalar_prefetch=1,
            grid=(steps,),
            in_specs=in_specs,
            out_specs=[
                pl.BlockSpec((rows, width), at),
                pl.BlockSpec((rows, width), at),
                pl.BlockSpec((blocks, rows, block), lambda i, t: (0, first + i, 0)),
                pl.BlockSpec((2 * blocks, rows, block), lambda i, t: (0, first + i, 0)),
                pl.BlockSpec((rows, width), even_at),
                pl.BlockSpec((rows, width), odd_at),
            ],
        ),
        out_shape=out_shape,
        input_output_aliases=aliases,
        compiler_params=pltpu.CompilerParams(
            dimension_semantics=("arbitrary",), vmem_limit_bytes=VMEM_LIMIT
        ),
        cost_estimate=pl.CostEstimate(flops=COST["feed"] * 10**9, bytes_accessed=8 << 20, transcendentals=0),
        name="feed_forward",
    )(table, *inputs)


def down_kernel(blocks, table_ref, act_ref, *refs):
    out_ref, downs = refs[-1], refs[:-1]
    total = None
    for j in range(blocks):
        part = dot(act_ref[j], downs[j][...])
        total = part if total is None else total + part
    total = total.astype(LOW)
    chips, rows = out_ref.shape[0], out_ref.shape[3]
    for q in range(chips):
        out_ref[table_ref[0] ^ q, 0, 0] = total[q * rows : (q + 1) * rows]


def down_terms_by_device(acts, c_index, c_count, downs, tok_rows):
    blocks, total, block = acts.shape
    width = downs[0].shape[1]
    chips = c_count // 2
    fixed = lambda shape: pl.BlockSpec(shape, lambda i, j, t: (0,) * len(shape))
    place_of = jnp.stack([c_index // 2, c_index % 2]).astype(jnp.int32)
    out = pl.pallas_call(
        functools.partial(down_kernel, blocks),
        grid_spec=pltpu.PrefetchScalarGridSpec(
            num_scalar_prefetch=1,
            grid=(2, 2),
            in_specs=[pl.BlockSpec((blocks, chips * tok_rows, block), lambda i, j, t: (0, 2 * i + j, 0))]
            + [fixed(d.shape) for d in downs],
            out_specs=pl.BlockSpec(
                (chips, 1, 1, tok_rows, width), lambda i, j, t: (0, t[1] ^ j, i, 0, 0)
            ),
        ),
        out_shape=jax.ShapeDtypeStruct((chips, 2, 2, tok_rows, width), LOW),
        compiler_params=pltpu.CompilerParams(vmem_limit_bytes=VMEM_LIMIT),
        cost_estimate=pl.CostEstimate(flops=0, bytes_accessed=8 << 20, transcendentals=0),
        name="down_terms",
    )(place_of, acts, *downs)
    return out.reshape(c_count * 2 * tok_rows, width)


def inverse_rms(rows):
    return lax.rsqrt(jnp.mean(rows * rows, axis=-1, keepdims=True) + EPSILON)


def norm_back(grad_hat, hat_rows, inv_rms):
    return inv_rms * (grad_hat - hat_rows * jnp.mean(grad_hat * hat_rows, axis=-1, keepdims=True))


def per_device(
    tokens, positions, attn_gain, w_query, w_key, w_value, w_out,
    mlp_gain, w_gate, w_up, w_down, cotangent,
):
    f_count, c_count = lax.axis_size("fsdp"), lax.axis_size("ctx")
    f_index, c_index = lax.axis_index("fsdp"), lax.axis_index("ctx")
    devices = f_count * c_count
    top_bit = f_count // 2
    own_tokens, own_cot = tokens[0], cotangent[0]
    tok_rows, width = own_tokens.shape
    piece = w_query.shape[0]
    heads = HEADS // c_count
    q_width = heads * HEAD_DIM
    qkv_width = q_width + 2 * HEAD_DIM
    kv_share = max(1, c_count // KV_HEADS)
    ff_block = w_down.shape[0]
    c_order = ctx_order(c_count)
    f_order = xor_order(top_bit, 1)

    attn_scale, mlp_scale = attn_gain.astype(WIDE)[:, None], mlp_gain.astype(WIDE)[:, None]
    near_tokens = gather_near(own_tokens)
    shares = [
        w_query.reshape(piece, c_count, q_width),
        jnp.repeat(w_key.reshape(piece, KV_HEADS, HEAD_DIM), kv_share, axis=1),
        jnp.repeat(w_value.reshape(piece, KV_HEADS, HEAD_DIM), kv_share, axis=1),
    ]
    qkv_piece = (jnp.concatenate(shares, axis=2).astype(WIDE) * attn_scale[:, :, None]).astype(LOW)
    qkv_piece = qkv_piece.transpose(1, 0, 2)
    steps = Steps()
    add, result, barrier = steps.add, steps.result, steps.barrier
    blocks = range(1, top_bit)
    away = lambda rows: [swap(rows, "fsdp", r) for r in blocks]
    exchange_all = lambda stack: lax.all_to_all(stack, ("fsdp", "ctx"), 0, 0, tiled=True)
    joined = lambda lists: [jnp.concatenate(parts, axis=0) for parts in zip(*lists)]
    half, unit_half, quarter = tok_rows // 2, ff_block // 2, width // 4
    out_route = [(f_count * c + j, j * c_count + c) for c in range(c_count) for j in range(f_count)]
    back_route = [(d, s) for s, d in out_route]

    add("out_route", (), lambda: w_out, lambda w: lax.ppermute(w, ("fsdp", "ctx"), out_route)[None])
    add("out_far", ("out_route",), lambda: [result("out_route")], lambda s: double_fsdp(s, top_bit, 2))
    add("out_near", ("out_far",), lambda: result("out_far"), lambda s: double_fsdp(s, 1, 1))
    add("down_a", (), lambda: w_down[:unit_half], away)
    add("down_b", (), lambda: w_down[unit_half:], away)
    add("columns", (), lambda: (w_gate, w_up), lambda w: columns_by_device(*w, mlp_scale, ff_block))
    add(
        "columns_all", ("columns",), lambda: result("columns"),
        lambda stack: exchange_all(stack).reshape(width, 2 * ff_block),
    )
    for j in range(4):
        add(f"move_{j}", ("columns_all",), lambda: result("columns_all"), lambda c, j=j: away(c[j * quarter : (j + 1) * quarter]))
    gather_rows = lambda rows: lax.all_gather(rows, "ctx", axis=0, tiled=True)
    add("own_cots", (), lambda: own_cot, gather_rows)
    add("cot_a", (), lambda: own_cot[:half], lambda rows: swap(rows, "fsdp", top_bit))
    add("cot_b", (), lambda: own_cot[half:], lambda rows: swap(rows, "fsdp", top_bit))
    add(
        "side_cots", ("cot_a", "cot_b"), lambda: (result("cot_a"), result("cot_b")),
        lambda parts: gather_rows(jnp.concatenate(parts, axis=0)),
    )

    (qkv_piece,) = barrier(0, qkv_piece)
    qkv_piece = exchange_ctx(qkv_piece).reshape(1, c_count * piece, qkv_width)
    small = positions
    for bit in [2 ** j for j in range(1, c_count.bit_length() - 1)] + [1]:
        small = jnp.concatenate([small, swap(small, "ctx", bit)], axis=0)
    int_places = small.reshape(-1)
    qkv_piece, near_tokens = barrier(1, qkv_piece, near_tokens)
    even_tokens = gather_far(own_tokens, near_tokens)
    qkv_parts = double_fsdp([qkv_piece], top_bit, 2)
    half_dim = HEAD_DIM // 2
    frequency = jnp.power(ROPE_BASE, -2.0 * jnp.arange(half_dim, dtype=WIDE) / HEAD_DIM)
    angles = int_places.astype(WIDE)[:, None] * frequency[None, :]
    cosine, sine = jnp.cos(angles), jnp.sin(angles)
    cosine = jnp.concatenate([cosine] * 4, axis=1)
    sine = jnp.concatenate([-sine, sine, -sine, sine], axis=1)
    qkv_parts, cosine, sine, even_tokens = barrier(2, qkv_parts, cosine, sine, even_tokens)
    quad_tokens, other_tokens = gather_core(even_tokens)
    qkv_parts = double_fsdp(qkv_parts, 1, 1)

    def first_norm(rows):
        rows = rows.astype(WIDE)
        return (rows * inverse_rms(rows)).astype(LOW)

    normed_first = [first_norm(quad_tokens), first_norm(other_tokens)]

    qkv_parts, normed_first = barrier(3, qkv_parts, normed_first)
    w_qkv = place(qkv_parts, f_order, f_index)
    qkv = jnp.concatenate([dot(rows, w_qkv) for rows in normed_first], axis=0)
    mixed, lse, q_scaled, k_rot, v_low = attention_forward(qkv, cosine, sine, int_places, heads)
    (mixed,) = barrier(4, mixed)

    w_out_rows = place(result("out_near"), f_order, f_index)
    middle = mixed.shape[0] // 2
    odd_out = scatter_core(dot(mixed[middle:], w_out_rows, out=LOW), COST["split_out"])
    even_out = dot(mixed[:middle], w_out_rows, out=LOW)
    odd_out, even_out = barrier(5, odd_out, even_out)
    state = scatter_far(scatter_sum(even_out, odd_out))
    inputs = own_tokens.astype(WIDE)
    inv_first = inverse_rms(inputs)
    hat_first = inputs * inv_first
    all_first = jnp.concatenate(normed_first, axis=0)
    state, hat_first, all_first = barrier(6, state, hat_first, all_first)
    (state,) = barrier(7, scatter_near(state))
    hidden = inputs + scatter_end(state)
    inv_second = inverse_rms(hidden)
    hat_second = hidden * inv_second
    normed_own = hat_second.astype(LOW)

    near_norm = gather_near(normed_own)
    side_norm = swap(normed_own, "fsdp", top_bit)
    near_norm, side_norm = barrier(8, near_norm, side_norm)
    even_norm = gather_far(normed_own, near_norm)
    near_side = gather_near(side_norm)
    norm_pieces = list(gather_core(even_norm))
    (norm_pieces,) = barrier(9, norm_pieces)
    columns = [result("columns_all")] + joined([result(f"move_{j}") for j in range(4)])
    downs = [w_down] + joined([result("down_a"), result("down_b")])
    table = jnp.array(c_order, jnp.int32) ^ c_index
    by_block = lambda rows: rows.reshape(c_count, tok_rows, width)

    weights = (table, columns, downs)
    *buffers, even_zero, odd_zero = feed_forward(0, *norm_pieces, by_block(result("own_cots")), *weights, [])
    near_side, buffers, even_zero, odd_zero = barrier(10, near_side, buffers, even_zero, odd_zero)
    side_norms = gather_core(gather_far(side_norm, near_side))
    quad_zero = scatter_sum(even_zero, scatter_core(odd_zero))
    side_norms, quad_zero, buffers, side_cots = barrier(
        11, side_norms, quad_zero, buffers, result("side_cots")
    )
    state_zero = scatter_far(quad_zero)
    *buffers, even_one, odd_one = feed_forward(1, *side_norms, by_block(side_cots), *weights, buffers)
    all_norms, all_cots, all_acts, all_lows = buffers

    product = lambda left, right: dot(left, right, ((0,), (0,)), LOW)
    add(
        "gate_away", (), lambda: (all_norms, all_lows),
        lambda p: [product(p[0], p[1][2 * j]) for j in blocks],
    )
    add(
        "up_away", (), lambda: (all_norms, all_lows),
        lambda p: [product(p[0], p[1][2 * j + 1]) for j in blocks],
    )
    add("down_away", (), lambda: (all_acts, all_cots), lambda p: [product(p[0][j], p[1]) for j in blocks])
    add("gate_own", (), lambda: (all_norms, all_lows), lambda p: product(p[0], p[1][0]))
    add("up_own", (), lambda: (all_norms, all_lows), lambda p: product(p[0], p[1][1]))
    move_back = lambda parts: [swap(part, "fsdp", r) for r, part in enumerate(parts, 1)]
    add("gate_move", ("gate_away",), lambda: result("gate_away"), move_back)
    add("up_move", ("up_away",), lambda: result("up_away"), move_back)
    add("down_move_a", ("down_away",), lambda: [p[:unit_half] for p in result("down_away")], move_back)
    add("down_move_b", ("down_away",), lambda: [p[unit_half:] for p in result("down_away")], move_back)
    add(
        "down_terms", (), lambda: all_acts,
        lambda acts: down_terms_by_device(acts, c_index, c_count, downs, tok_rows),
    )
    add(
        "out_rows", ("down_terms",), lambda: result("down_terms"),
        lambda t: lax.psum_scatter(t, "ctx", scatter_dimension=0, tiled=True).reshape(2, tok_rows, width),
    )
    add("side_out", ("out_rows",), lambda: result("out_rows")[1], lambda rows: swap(rows, "fsdp", top_bit))

    def sum_by_device(own, parts):
        total = sum([part.astype(WIDE) for part in parts], own.astype(WIDE)).astype(LOW)
        return total.reshape(devices, piece, ff_block)

    add(
        "both_all", ("gate_own", "gate_move", "up_own", "up_move"), lambda: [result(n) for n in ("gate_own", "gate_move", "up_own", "up_move")],
        lambda p: exchange_all(
            jnp.concatenate([sum_by_device(p[0], p[1]), sum_by_device(p[2], p[3])], axis=2)
        ),
    )
    add(
        "down_own", (), lambda: (all_acts, all_cots),
        lambda p: dot(p[0][0], p[1], ((0,), (0,))),
    )
    add(
        "assembled",
        ("both_all",),
        lambda: result("both_all"),
        lambda parts: assemble_columns(parts, w_gate, w_up, mlp_scale),
    )
    state_zero, odd_one, even_one = barrier(12, state_zero, odd_one, even_one)
    odd_one = scatter_core(odd_one)
    state_zero = scatter_near(state_zero)
    quad_one = scatter_sum(even_one, odd_one)
    quad_one, state_zero = barrier(13, quad_one, state_zero)
    (state_one,) = barrier(14, scatter_far(quad_one))
    (state_one,) = barrier(15, scatter_near(state_one))
    side_one = swap(scatter_end(state_one).astype(LOW), "fsdp", top_bit)
    (side_one,) = barrier(16, side_one)
    grad_normed = scatter_end(state_zero) + side_one.astype(WIDE)

    grad_hidden = own_cot.astype(WIDE) + norm_back(grad_normed, hat_second, inv_second)
    hidden_low = grad_hidden.astype(LOW)
    (near_hidden,) = barrier(17, gather_near(hidden_low))
    (even_hidden,) = barrier(18, gather_far(hidden_low, near_hidden))
    hidden_halves = gather_core(even_hidden, COST["split_hidden"])
    grad_mixed = jnp.concatenate([dot(h, w_out_rows, ((1,), (1,)), LOW) for h in hidden_halves], axis=0)

    def out_product(p):
        total = dot(p[0][:middle], p[1][0], ((0,), (0,))) + dot(p[0][middle:], p[1][1], ((0,), (0,)))
        return total.astype(LOW).reshape(f_count, piece, width)

    add("out_part", (), lambda: (mixed, hidden_halves), out_product)
    add("out_halved", ("out_part",), lambda: result("out_part"), lambda p: halve_near(p, f_index))
    add("out_sum", ("out_halved",), lambda: result("out_halved"), lambda p: halve_far(p, f_index, top_bit))
    add("out_grad", ("out_sum",), lambda: result("out_sum"), lambda p: lax.ppermute(p, ("fsdp", "ctx"), back_route))

    (grad_mixed,) = barrier(19, grad_mixed)
    grad_qkv = attention_backward(
        q_scaled, k_rot, v_low, grad_mixed, lse, cosine, sine, int_places, heads
    )
    grad_qkv, all_first = barrier(20, grad_qkv, all_first)

    qkv_part = dot(all_first, grad_qkv, ((0,), (0,)), LOW)
    qkv_part = qkv_part.reshape(f_count, c_count * piece, qkv_width)
    grad_qkv, qkv_part = tie(grad_qkv, qkv_part)
    qkv_sum = halve_near(qkv_part, f_index)
    (grad_qkv,) = barrier(21, grad_qkv)
    odd = scatter_core(dot(grad_qkv[middle:], w_qkv, ((1,), (1,)), LOW), COST["split_last"])
    even = dot(grad_qkv[:middle], w_qkv, ((1,), (1,)), LOW)
    quad = scatter_sum(even, odd)
    qkv_sum, quad = barrier(22, qkv_sum, quad)
    state = scatter_far(quad)
    qkv_sum = halve_far(qkv_sum, f_index, top_bit)
    state, qkv_sum = barrier(23, state, qkv_sum)
    qkv_sum = exchange_ctx(qkv_sum.reshape(c_count, piece, qkv_width))
    (state,) = barrier(24, scatter_near(state))
    (qkv_sum,) = barrier(25, qkv_sum)
    grad_normed = scatter_end(state)
    input_grad = grad_hidden + norm_back(grad_normed, hat_first, inv_first)
    gate_grad, up_grad, mlp_gain_grad = result("assembled")
    mlp_gain_grad = mlp_gain_grad[:, 0]
    out_grad = result("out_grad").astype(WIDE)
    down_grad = result("down_own")
    for part in joined([result("down_move_a"), result("down_move_b")]):
        down_grad = down_grad + part.astype(WIDE)
    side_out, out_rows = result("side_out"), result("out_rows")
    output = hidden + out_rows[0].astype(WIDE) + side_out.astype(WIDE)

    qkv_sum = qkv_sum.astype(WIDE)
    query_grad = qkv_sum[:, :, :q_width].transpose(1, 0, 2).reshape(piece, -1)
    kv_sum = qkv_sum[:, :, q_width:].reshape(KV_HEADS, kv_share, piece, 2, HEAD_DIM).sum(axis=1)
    key_grad = kv_sum[:, :, 0].transpose(1, 0, 2).reshape(piece, -1)
    value_grad = kv_sum[:, :, 1].transpose(1, 0, 2).reshape(piece, -1)
    attn_gain_grad = (
        jnp.sum(query_grad * w_query.astype(WIDE), axis=1)
        + jnp.sum(key_grad * w_key.astype(WIDE), axis=1)
        + jnp.sum(value_grad * w_value.astype(WIDE), axis=1)
    )
    query_grad, key_grad, value_grad = (g * attn_scale for g in (query_grad, key_grad, value_grad))

    return (
        output.astype(LOW)[None],
        input_grad.astype(LOW)[None],
        attn_gain_grad,
        query_grad,
        key_grad,
        value_grad,
        out_grad,
        mlp_gain_grad,
        gate_grad,
        up_grad,
        down_grad,
    )


def solution(mesh):
    rows = P(("fsdp", "ctx"), None)
    vector = P(("fsdp", "ctx"))
    tokens = P("fsdp", "ctx", None)
    in_specs = (
        tokens, P("fsdp", "ctx"), vector, rows, rows, rows, rows, vector, rows, rows, rows, tokens,
    )
    out_specs = (
        tokens, tokens, vector, rows, rows, rows, rows, vector, rows, rows, rows,
    )
    return jax.shard_map(
        per_device, mesh=mesh, in_specs=in_specs, out_specs=out_specs, check_vma=False
    )
```

```python
import functools

import jax
import jax.numpy as jnp
from jax import lax
from jax.experimental import pallas as pl
from jax.experimental.pallas import tpu as pltpu
from jax.sharding import PartitionSpec as P

HEADS = 32
KV_HEADS = 8
HEAD_DIM = 64
EPSILON = 1e-05
ROPE_BASE = 500000.0
VMEM_LIMIT = 56 * 1024 * 1024

WHEN = {
    "out_route": (0, 1),
    "down_a": (0, 2),
    "down_b": (6, 9),
    "own_cots": (1, 9),
    "columns": (1, 2),
    "out_far": (2, 3),
    "cot_a": (2, 3),
    "out_near": (3, 99),
    "columns_all": (3, 4),
    "cot_b": (4, 6),
    "move_0": (5, 7),
    "move_1": (5, 6),
    "move_2": (6, 8),
    "move_3": (6, 8),
    "side_cots": (6, 11),
    "gate_away": (13, 14),
    "gate_move": (14, 18),
    "up_away": (14, 15),
    "down_away": (14, 15),
    "gate_own": (15, 16),
    "down_terms": (15, 16),
    "up_move": (16, 18),
    "up_own": (16, 17),
    "out_rows": (18, 23),
    "both_all": (18, 22),
    "out_part": (18, 19),
    "out_halved": (19, 20),
    "out_sum": (20, 22),
    "out_grad": (23, 25),
    "side_out": (23, 25),
    "down_own": (20, 22),
    "assembled": (23, 24),
    "down_move_a": (21, 24),
    "down_move_b": (21, 24),
}
COST = {"forward": 0, "backward": 0, "feed": 0, "split_out": 1, "split_last": 2, "split_hidden": 2}
LOW = jnp.bfloat16
WIDE = jnp.float32


def dot(left, right, dims=((1,), (0,)), out=WIDE):
    return lax.dot_general(left, right, (dims, ((), ())), preferred_element_type=WIDE).astype(out)


def tie(*values):
    return lax.optimization_barrier(values)


class Steps:
    def __init__(self):
        self.waiting, self.flying, self.ended = {}, {}, {}

    def add(self, name, needs, operand, task):
        self.waiting[name] = (needs, operand, task)

    def result(self, name):
        if name in self.waiting:
            _, operand, task = self.waiting.pop(name)
            self.flying[name] = task(operand())
        return self.ended[name] if name in self.ended else self.flying[name]

    def barrier(self, step, *values):
        starting = [n for n in self.waiting if WHEN[n][0] <= step]
        later = [n for n in starting if any(need in self.waiting for need in self.waiting[n][0])]
        tasks = [(n, *self.waiting.pop(n)[1:]) for n in starting if n not in later]
        operands = [operand() for _, operand, _ in tasks]
        ending = [n for n in self.flying if WHEN[n][1] <= step and n not in self.ended]
        values, operands, results = tie(values, operands, [self.flying[n] for n in ending])
        self.ended.update(zip(ending, results))
        for (name, _, task), operand in zip(tasks, operands):
            self.flying[name] = task(operand)
        for name in later:
            self.result(name)
        return values


def swap(block, axis, mask):
    count = lax.axis_size(axis)
    return lax.ppermute(block, axis, [(i, i ^ mask) for i in range(count)])


def pick(stack, index):
    return lax.dynamic_index_in_dim(stack, index, 0, keepdims=False)


def in_order(pieces, base):
    out = jnp.zeros((len(pieces),) + pieces[0].shape, pieces[0].dtype)
    for r, piece in enumerate(pieces):
        out = lax.dynamic_update_index_in_dim(out, piece, base ^ r, 0)
    return out


def ctx_order(count):
    order = [0]
    bit = 2
    while bit < count:
        order = order + [k ^ bit for k in order]
        bit *= 2
    return order + [k ^ 1 for k in order]


def gather_near(block):
    count = lax.axis_size("ctx")
    return (swap(block, "ctx", 2), swap(block, "ctx", 4)) if count == 8 else ()


def gather_far(block, near):
    count = lax.axis_size("ctx")
    if count == 8:
        near_x, near_y = near
        half = block.shape[0] // 2
        return block, near_x, near_y, swap(near_y[:half], "ctx", 2), swap(near_x[half:], "ctx", 4)
    even, bit = (block,), 2
    while bit < count:
        even = even + tuple(swap(part, "ctx", bit) for part in even)
        bit *= 2
    return even


def swap_core(rows, parts):
    size = rows.shape[0] // parts
    pieces = [swap(rows[j * size : (j + 1) * size], "ctx", 1) for j in range(parts)]
    return pieces[0] if parts == 1 else jnp.concatenate(pieces, axis=0)


def gather_core(even, parts=1):
    quad = jnp.concatenate(even, axis=0)
    return quad, swap_core(quad, parts)


def scatter_core(odd, parts=1):
    return swap_core(odd, parts)


def scatter_sum(even, odd):
    return (even.astype(WIDE) + odd.astype(WIDE)).astype(LOW)


def scatter_far(quad):
    count = lax.axis_size("ctx")
    if count != 8:
        return (quad.astype(WIDE),)
    rows = quad.shape[0] // 4
    half = rows // 2
    own, to_x, to_y, far = (quad[j * rows : (j + 1) * rows] for j in range(4))
    far_x, far_y = swap(far[half:], "ctx", 2), swap(far[:half], "ctx", 4)
    by_x, by_y = swap(to_x[half:], "ctx", 2), swap(to_y[:half], "ctx", 4)
    return own, to_x[:half], to_y[half:], by_x, by_y, far_x, far_y


def scatter_near(state):
    count = lax.axis_size("ctx")
    if count != 8:
        (quad,) = state
        bit = count // 2
        while bit >= 2:
            middle = quad.shape[0] // 2
            quad = quad[:middle] + swap(quad[middle:].astype(LOW), "ctx", bit).astype(WIDE)
            bit //= 2
        return (quad,)
    own, to_x, to_y, by_x, by_y, far_x, far_y = state
    last_x = swap((to_x.astype(WIDE) + far_y.astype(WIDE)).astype(LOW), "ctx", 2)
    last_y = swap((to_y.astype(WIDE) + far_x.astype(WIDE)).astype(LOW), "ctx", 4)
    return own, by_x, by_y, last_x, last_y


def scatter_end(state):
    if len(state) == 1:
        return state[0]
    own, by_x, by_y, last_x, last_y = state
    half = last_x.shape[0]
    top = own[:half].astype(WIDE) + last_x.astype(WIDE) + by_y.astype(WIDE)
    low = own[half:].astype(WIDE) + by_x.astype(WIDE) + last_y.astype(WIDE)
    return jnp.concatenate([top, low], axis=0)


def exchange_ctx(stack):
    return lax.all_to_all(stack, "ctx", 0, 0, tiled=True)


def double_fsdp(stacks, first, last):
    bit = first
    while bit >= last:
        sent = stacks[0] if len(stacks) == 1 else jnp.concatenate(stacks, axis=0)
        stacks = stacks + [swap(sent, "fsdp", bit)]
        bit //= 2
    return stacks


def xor_order(first, last):
    order, bit = [0], first
    while bit >= last:
        order = order + [k ^ bit for k in order]
        bit //= 2
    return order


def place_kernel(masks, rows, base_ref, *refs):
    out_ref = refs[-1]
    masks = iter(masks)
    for part in refs[:-1]:
        for j in range(part.shape[0]):
            start = pl.multiple_of((base_ref[0] ^ next(masks)) * rows, 16)
            out_ref[pl.ds(start, rows), :] = part[j]


def place(parts, masks, base):
    _, rows, columns = parts[0].shape
    total = len(masks) * rows
    whole = pl.BlockSpec(memory_space=pltpu.VMEM)
    return pl.pallas_call(
        functools.partial(place_kernel, masks, rows),
        in_specs=[pl.BlockSpec(memory_space=pltpu.SMEM)] + [whole] * len(parts),
        out_specs=whole,
        out_shape=jax.ShapeDtypeStruct((total, columns), parts[0].dtype),
        compiler_params=pltpu.CompilerParams(vmem_limit_bytes=VMEM_LIMIT),
        cost_estimate=pl.CostEstimate(flops=0, bytes_accessed=total * columns * 2, transcendentals=0),
        name="place",
    )(base.reshape(1), *parts)


def halve_fsdp(stack, base, first, last):
    bit = first
    while bit >= last:
        low = stack.shape[0] // 2
        side = (base // bit) % 2
        pair = stack.reshape((2, low) + stack.shape[1:])
        mine, theirs = pick(pair, side), pick(pair, 1 - side)
        stack = (mine.astype(WIDE) + swap(theirs, "fsdp", bit).astype(WIDE)).astype(LOW)
        bit //= 2
    return stack if stack.shape[0] > 1 else stack[0]


def halve_near(stack, base):
    pair = stack.reshape((stack.shape[0] // 2, 2) + stack.shape[1:]).swapaxes(0, 1)
    mine, theirs = pick(pair, base % 2), pick(pair, 1 - base % 2)
    return (mine.astype(WIDE) + swap(theirs, "fsdp", 1).astype(WIDE)).astype(LOW)


def halve_far(stack, base, first):
    return halve_fsdp(stack, base, first, 2)


def turned(block, cosine, sine):
    lane = lax.broadcasted_iota(jnp.int32, block.shape, 1)
    first = (lane % HEAD_DIM) < HEAD_DIM // 2
    width = block.shape[1]
    other = jnp.where(
        first, pltpu.roll(block, width - HEAD_DIM // 2, 1), pltpu.roll(block, HEAD_DIM // 2, 1)
    )
    return block * cosine + other * sine


def forward_kernel(
    heads, q_ref, kv_ref, cos_ref, sin_ref, cosk_ref, sink_ref, row_ref, col_ref,
    mixed_ref, lse_ref, qs_ref, kr_ref, vl_ref, vt_ref,
):
    @pl.when(pl.program_id(0) == 0)
    def _():
        keys = turned(kv_ref[...], cosk_ref[...], sink_ref[...])
        kr_ref[...] = keys[:, :HEAD_DIM].astype(LOW)
        values = kv_ref[...][:, HEAD_DIM:].astype(LOW)
        vl_ref[...] = values
        vt_ref[...] = values.astype(WIDE).T.astype(LOW)

    cosine, sine = cos_ref[...], sin_ref[...]
    keys = kr_ref[...]
    values_t = vt_ref[...]
    visible = col_ref[...] <= row_ref[...]
    scale = HEAD_DIM ** (-0.5)
    mixed, totals = [], []
    for pair in range(heads // 2):
        both = turned(q_ref[:, pair * 128 : pair * 128 + 128], cosine, sine)
        both = (both.astype(LOW).astype(WIDE) * scale).astype(LOW)
        qs_ref[:, pair * 128 : pair * 128 + 128] = both
        for side in range(2):
            query = both[:, side * HEAD_DIM : (side + 1) * HEAD_DIM]
            scores = jnp.where(visible, dot(keys, query, ((1,), (1,))), -1e30)
            top = jnp.max(scores, axis=0, keepdims=True)
            weights = jnp.exp(scores - top)
            total = jnp.sum(weights, axis=0, keepdims=True)
            out = dot(values_t, weights.astype(LOW)) / total
            mixed.append(out)
            totals.append(top + jnp.log(total))
    mixed_ref[...] = jnp.concatenate(mixed, axis=0).T.astype(LOW)
    pad = [jnp.zeros_like(totals[0])] * (8 - heads)
    lse_ref[...] = jnp.concatenate(totals + pad, axis=0)


def backward_kernel(
    heads, steps, q_ref, k_ref, v_ref, do_ref, lse_ref, cos_ref, sin_ref, cosk_ref, sink_ref,
    row_ref, col_ref, out_ref, kt_ref, dk_ref, dv_ref,
):
    @pl.when(pl.program_id(0) == 0)
    def _():
        kt_ref[...] = k_ref[...].astype(WIDE).T.astype(LOW)
        dk_ref[...] = jnp.zeros_like(dk_ref)
        dv_ref[...] = jnp.zeros_like(dv_ref)

    keys, values, keys_t = k_ref[...], v_ref[...], kt_ref[...]
    visible = col_ref[...] <= row_ref[...]
    scale = HEAD_DIM ** (-0.5)
    grads = []
    for head in range(heads):
        lanes = slice(head * HEAD_DIM, (head + 1) * HEAD_DIM)
        query, grad_out = q_ref[:, lanes], do_ref[:, lanes]
        scores = dot(keys, query, ((1,), (1,)))
        probs = jnp.where(visible, jnp.exp(scores - lse_ref[head : head + 1, :]), 0.0)
        grad_probs = dot(values, grad_out, ((1,), (1,)))
        product = probs * grad_probs
        delta = jnp.sum(product, axis=0, keepdims=True)
        grad_scores = (product - probs * delta).astype(LOW)
        dv_ref[...] += dot(probs.astype(LOW), grad_out)
        dk_ref[...] += dot(grad_scores, query)
        grads.append(dot(keys_t, grad_scores) * scale)
    grad_q = jnp.concatenate(grads, axis=0).T
    cosine, sine = cos_ref[...], sin_ref[...]
    block = grad_q.shape[0]
    rows = pl.ds(pl.multiple_of(pl.program_id(0) * block, block), block)
    for pair in range(heads // 2):
        lanes = slice(pair * 128, pair * 128 + 128)
        out_ref[rows, lanes] = turned(grad_q[:, lanes], cosine, -sine).astype(LOW)

    @pl.when(pl.program_id(0) == steps - 1)
    def _():
        both = jnp.concatenate([dk_ref[...], dv_ref[...]], axis=1)
        back = turned(both, cosk_ref[...], -sink_ref[...])
        lane = lax.broadcasted_iota(jnp.int32, both.shape, 1)
        out_ref[:, heads * HEAD_DIM :] = jnp.where(lane < HEAD_DIM, back, both).astype(LOW)


def attention_forward(qkv, cosine, sine, places, heads):
    length = qkv.shape[0]
    width = heads * HEAD_DIM
    block = min(256, length)
    whole = lambda shape: pl.BlockSpec(shape, lambda i: (0,) * len(shape))
    rows = lambda columns: pl.BlockSpec((block, columns), lambda i: (i, 0))
    return pl.pallas_call(
        functools.partial(forward_kernel, heads),
        grid=(length // block,),
        in_specs=[
            rows(width),
            pl.BlockSpec((length, 128), lambda i: (0, width // 128)),
            rows(128), rows(128), whole((length, 128)), whole((length, 128)),
            pl.BlockSpec((1, block), lambda i: (0, i)), whole((length, 1)),
        ],
        out_specs=[
            rows(width), pl.BlockSpec((8, block), lambda i: (0, i)), rows(width),
            whole((length, HEAD_DIM)), whole((length, HEAD_DIM)),
        ],
        out_shape=[
            jax.ShapeDtypeStruct((length, width), LOW),
            jax.ShapeDtypeStruct((8, length), WIDE),
            jax.ShapeDtypeStruct((length, width), LOW),
            jax.ShapeDtypeStruct((length, HEAD_DIM), LOW),
            jax.ShapeDtypeStruct((length, HEAD_DIM), LOW),
        ],
        scratch_shapes=[pltpu.VMEM((HEAD_DIM, length), LOW)],
        compiler_params=pltpu.CompilerParams(
            dimension_semantics=("arbitrary",), vmem_limit_bytes=VMEM_LIMIT
        ),
        cost_estimate=pl.CostEstimate(
            flops=COST["forward"] * 10**9, bytes_accessed=8 * length * width, transcendentals=0
        ),
        name="attention_forward",
    )(qkv, qkv, cosine, sine, cosine, sine, places[None, :], places[:, None])


def attention_backward(q_scaled, k_rot, v_low, grad_mixed, lse, cosine, sine, places, heads):
    length = q_scaled.shape[0]
    width = heads * HEAD_DIM
    block = min(256, length)
    steps = length // block
    whole = lambda shape: pl.BlockSpec(shape, lambda i: (0,) * len(shape))
    rows = lambda columns: pl.BlockSpec((block, columns), lambda i: (i, 0))
    return pl.pallas_call(
        functools.partial(backward_kernel, heads, steps),
        grid=(steps,),
        in_specs=[
            rows(width), whole((length, HEAD_DIM)), whole((length, HEAD_DIM)), rows(width),
            pl.BlockSpec((8, block), lambda i: (0, i)),
            rows(128), rows(128), whole((length, 128)), whole((length, 128)),
            pl.BlockSpec((1, block), lambda i: (0, i)), whole((length, 1)),
        ],
        out_specs=whole((length, width + 128)),
        out_shape=jax.ShapeDtypeStruct((length, width + 128), LOW),
        scratch_shapes=[
            pltpu.VMEM((HEAD_DIM, length), LOW),
            pltpu.VMEM((length, HEAD_DIM), WIDE),
            pltpu.VMEM((length, HEAD_DIM), WIDE),
        ],
        compiler_params=pltpu.CompilerParams(
            dimension_semantics=("arbitrary",), vmem_limit_bytes=VMEM_LIMIT
        ),
        cost_estimate=pl.CostEstimate(
            flops=COST["backward"] * 10**9, bytes_accessed=8 * length * width, transcendentals=0
        ),
        name="attention_backward",
    )(
        q_scaled, k_rot, v_low, grad_mixed, lse, cosine, sine, cosine, sine,
        places[None, :], places[:, None],
    )


def columns_kernel(block, gate_ref, up_ref, scale_ref, out_ref):
    scale = scale_ref[...]
    for j in range(out_ref.shape[0]):
        lanes = slice(j * block, (j + 1) * block)
        out_ref[j, :, :block] = (gate_ref[:, lanes].astype(WIDE) * scale).astype(LOW)
        out_ref[j, :, block:] = (up_ref[:, lanes].astype(WIDE) * scale).astype(LOW)


def columns_by_device(w_gate, w_up, scale, block):
    rows, ff_width = w_gate.shape
    devices = ff_width // block
    if block % 128:
        split = [(w.astype(WIDE) * scale).astype(LOW).reshape(rows, devices, block) for w in (w_gate, w_up)]
        return jnp.concatenate(split, axis=2).transpose(1, 0, 2)
    some = 8
    part = pl.BlockSpec((rows, some * block), lambda d: (0, d))
    return pl.pallas_call(
        functools.partial(columns_kernel, block),
        grid=(devices // some,),
        in_specs=[part, part, pl.BlockSpec((rows, 1), lambda d: (0, 0))],
        out_specs=pl.BlockSpec((some, rows, 2 * block), lambda d: (d, 0, 0)),
        out_shape=jax.ShapeDtypeStruct((devices, rows, 2 * block), LOW),
        cost_estimate=pl.CostEstimate(flops=0, bytes_accessed=2 << 20, transcendentals=0),
        name="columns_by_device",
    )(w_gate, w_up, scale)


def assemble_kernel(part_ref, gate_ref, up_ref, scale_ref, gate_out, up_out, gain_out):
    @pl.when(pl.program_id(0) == 0)
    def _():
        gain_out[...] = jnp.zeros_like(gain_out)

    scale = scale_ref[...]
    block = gate_ref.shape[1] // part_ref.shape[0]
    total = jnp.zeros_like(gain_out)
    for j in range(part_ref.shape[0]):
        lanes = slice(j * block, (j + 1) * block)
        gate = part_ref[j, :, :block].astype(WIDE)
        up = part_ref[j, :, block:].astype(WIDE)
        gate_out[:, lanes] = gate * scale
        up_out[:, lanes] = up * scale
        products = gate * gate_ref[:, lanes].astype(WIDE) + up * up_ref[:, lanes].astype(WIDE)
        total = total + jnp.sum(products, axis=1, keepdims=True)
    gain_out[...] += total


def assemble_columns(parts, w_gate, w_up, scale):
    devices, rows, both = parts.shape
    block = both // 2
    ff_width = w_gate.shape[1]
    if block % 128:
        sides = parts.reshape(devices, rows, 2, block).transpose(2, 1, 0, 3).reshape(2, rows, ff_width)
        sides = sides.astype(WIDE)
        products = sides[0] * w_gate.astype(WIDE) + sides[1] * w_up.astype(WIDE)
        return sides[0] * scale, sides[1] * scale, jnp.sum(products, axis=1, keepdims=True)
    some = 8
    columns = pl.BlockSpec((rows, some * block), lambda d: (0, d))
    one = pl.BlockSpec((rows, 1), lambda d: (0, 0))
    return pl.pallas_call(
        assemble_kernel,
        grid=(devices // some,),
        in_specs=[pl.BlockSpec((some, rows, both), lambda d: (d, 0, 0)), columns, columns, one],
        out_specs=[columns, columns, one],
        out_shape=[
            jax.ShapeDtypeStruct((rows, ff_width), WIDE),
            jax.ShapeDtypeStruct((rows, ff_width), WIDE),
            jax.ShapeDtypeStruct((rows, 1), WIDE),
        ],
        compiler_params=pltpu.CompilerParams(
            dimension_semantics=("arbitrary",), vmem_limit_bytes=VMEM_LIMIT
        ),
        cost_estimate=pl.CostEstimate(flops=0, bytes_accessed=8 << 20, transcendentals=0),
        name="assemble_columns",
    )(parts, w_gate, w_up, scale)


def feed_kernel(blocks, steps, per_step, table_ref, *refs):
    even_ref, odd_ref = refs[:2]
    cot_refs = refs[2 : 2 + per_step]
    weights = refs[2 + per_step : 2 + per_step + blocks]
    downs = refs[2 + per_step + blocks : 2 + per_step + 2 * blocks]
    norm_out, cot_out, act_out, low_out, even_out, odd_out = refs[-6:]
    step = pl.program_id(0)
    width = downs[0].shape[0]
    norm = jnp.where(step < steps // 2, even_ref[...], odd_ref[...])
    norm_out[...] = norm
    cot = jnp.concatenate([ref[0] for ref in cot_refs], axis=0)
    cot_out[...] = cot
    term = None
    for j in range(blocks):
        rows = dot(norm, weights[j][...])
        gate, up = rows[:, :width], rows[:, width:]
        grad_act = dot(cot, downs[j][...], ((1,), (1,)))
        sig = 1.0 / (1.0 + jnp.exp(-gate))
        gate_sig = gate * sig
        act_out[j] = (gate_sig * up).astype(LOW)
        grad_up = (grad_act * gate_sig).astype(LOW)
        grad_gate = (grad_act * up * (sig + gate_sig * (1.0 - sig))).astype(LOW)
        low_out[2 * j] = grad_gate
        low_out[2 * j + 1] = grad_up
        more = dot(jnp.concatenate([grad_gate, grad_up], axis=1), weights[j][...], ((1,), (1,)))
        term = more if term is None else term + more
    term = term.astype(LOW)

    @pl.when(step < steps // 2)
    def _():
        even_out[...] = term

    @pl.when(step >= steps // 2)
    def _():
        odd_out[...] = term


def feed_forward(which, even, odd, cots, table, weights, downs, earlier):
    half, width = even.shape
    c_count, tok_rows, _ = cots.shape
    blocks = len(weights)
    block = downs[0].shape[0]
    steps = 4
    rows = 2 * half // steps
    per_step = rows // tok_rows
    total = 4 * half
    first = which * steps
    even_at = lambda i, t: (jnp.minimum(i, steps // 2 - 1), 0)
    odd_at = lambda i, t: (jnp.maximum(i - steps // 2, 0), 0)
    cot_spec = lambda j: pl.BlockSpec(
        (1, tok_rows, width), lambda i, t, j=j: (t[i * per_step + j], 0, 0)
    )
    fixed = lambda shape: pl.BlockSpec(shape, lambda i, t: (0,) * len(shape))
    at = lambda i, t: (first + i, 0)
    out_shape = [
        jax.ShapeDtypeStruct((total, width), LOW),
        jax.ShapeDtypeStruct((total, width), LOW),
        jax.ShapeDtypeStruct((blocks, total, block), LOW),
        jax.ShapeDtypeStruct((2 * blocks, total, block), LOW),
        jax.ShapeDtypeStruct((half, width), LOW),
        jax.ShapeDtypeStruct((half, width), LOW),
    ]
    weights = list(weights) + list(downs)
    inputs = [even, odd] + [cots] * per_step + weights + list(earlier)
    in_specs = (
        [pl.BlockSpec((rows, width), even_at), pl.BlockSpec((rows, width), odd_at)]
        + [cot_spec(j) for j in range(per_step)]
        + [fixed(w.shape) for w in weights]
        + [pl.BlockSpec(memory_space=pl.ANY)] * len(earlier)
    )
    aliases = {1 + len(inputs) - len(earlier) + j: j for j in range(len(earlier))}
    return pl.pallas_call(
        functools.partial(feed_kernel, blocks, steps, per_step),
        grid_spec=pltpu.PrefetchScalarGridSpec(
            num_scalar_prefetch=1,
            grid=(steps,),
            in_specs=in_specs,
            out_specs=[
                pl.BlockSpec((rows, width), at),
                pl.BlockSpec((rows, width), at),
                pl.BlockSpec((blocks, rows, block), lambda i, t: (0, first + i, 0)),
                pl.BlockSpec((2 * blocks, rows, block), lambda i, t: (0, first + i, 0)),
                pl.BlockSpec((rows, width), even_at),
                pl.BlockSpec((rows, width), odd_at),
            ],
        ),
        out_shape=out_shape,
        input_output_aliases=aliases,
        compiler_params=pltpu.CompilerParams(
            dimension_semantics=("arbitrary",), vmem_limit_bytes=VMEM_LIMIT
        ),
        cost_estimate=pl.CostEstimate(flops=COST["feed"] * 10**9, bytes_accessed=8 << 20, transcendentals=0),
        name="feed_forward",
    )(table, *inputs)


def down_kernel(blocks, table_ref, act_ref, *refs):
    out_ref, downs = refs[-1], refs[:-1]
    total = None
    for j in range(blocks):
        part = dot(act_ref[j], downs[j][...])
        total = part if total is None else total + part
    total = total.astype(LOW)
    chips, rows = out_ref.shape[0], out_ref.shape[3]
    for q in range(chips):
        out_ref[table_ref[0] ^ q, 0, 0] = total[q * rows : (q + 1) * rows]


def down_terms_by_device(acts, c_index, c_count, downs, tok_rows):
    blocks, total, block = acts.shape
    width = downs[0].shape[1]
    chips = c_count // 2
    fixed = lambda shape: pl.BlockSpec(shape, lambda i, j, t: (0,) * len(shape))
    place_of = jnp.stack([c_index // 2, c_index % 2]).astype(jnp.int32)
    out = pl.pallas_call(
        functools.partial(down_kernel, blocks),
        grid_spec=pltpu.PrefetchScalarGridSpec(
            num_scalar_prefetch=1,
            grid=(2, 2),
            in_specs=[pl.BlockSpec((blocks, chips * tok_rows, block), lambda i, j, t: (0, 2 * i + j, 0))]
            + [fixed(d.shape) for d in downs],
            out_specs=pl.BlockSpec(
                (chips, 1, 1, tok_rows, width), lambda i, j, t: (0, t[1] ^ j, i, 0, 0)
            ),
        ),
        out_shape=jax.ShapeDtypeStruct((chips, 2, 2, tok_rows, width), LOW),
        compiler_params=pltpu.CompilerParams(vmem_limit_bytes=VMEM_LIMIT),
        cost_estimate=pl.CostEstimate(flops=0, bytes_accessed=8 << 20, transcendentals=0),
        name="down_terms",
    )(place_of, acts, *downs)
    return out.reshape(c_count * 2 * tok_rows, width)


def inverse_rms(rows):
    return lax.rsqrt(jnp.mean(rows * rows, axis=-1, keepdims=True) + EPSILON)


def norm_back(grad_hat, hat_rows, inv_rms):
    return inv_rms * (grad_hat - hat_rows * jnp.mean(grad_hat * hat_rows, axis=-1, keepdims=True))


def per_device(
    tokens, positions, attn_gain, w_query, w_key, w_value, w_out,
    mlp_gain, w_gate, w_up, w_down, cotangent,
):
    f_count, c_count = lax.axis_size("fsdp"), lax.axis_size("ctx")
    f_index, c_index = lax.axis_index("fsdp"), lax.axis_index("ctx")
    devices = f_count * c_count
    top_bit = f_count // 2
    own_tokens, own_cot = tokens[0], cotangent[0]
    tok_rows, width = own_tokens.shape
    piece = w_query.shape[0]
    heads = HEADS // c_count
    q_width = heads * HEAD_DIM
    qkv_width = q_width + 2 * HEAD_DIM
    kv_share = max(1, c_count // KV_HEADS)
    ff_block = w_down.shape[0]
    c_order = ctx_order(c_count)
    f_order = xor_order(top_bit, 1)

    attn_scale, mlp_scale = attn_gain.astype(WIDE)[:, None], mlp_gain.astype(WIDE)[:, None]
    near_tokens = gather_near(own_tokens)
    shares = [
        w_query.reshape(piece, c_count, q_width),
        jnp.repeat(w_key.reshape(piece, KV_HEADS, HEAD_DIM), kv_share, axis=1),
        jnp.repeat(w_value.reshape(piece, KV_HEADS, HEAD_DIM), kv_share, axis=1),
    ]
    qkv_piece = (jnp.concatenate(shares, axis=2).astype(WIDE) * attn_scale[:, :, None]).astype(LOW)
    qkv_piece = qkv_piece.transpose(1, 0, 2)
    steps = Steps()
    add, result, barrier = steps.add, steps.result, steps.barrier
    blocks = range(1, top_bit)
    away = lambda rows: [swap(rows, "fsdp", r) for r in blocks]
    exchange_all = lambda stack: lax.all_to_all(stack, ("fsdp", "ctx"), 0, 0, tiled=True)
    joined = lambda lists: [jnp.concatenate(parts, axis=0) for parts in zip(*lists)]
    half, unit_half, quarter = tok_rows // 2, ff_block // 2, width // 4
    out_route = [(f_count * c + j, j * c_count + c) for c in range(c_count) for j in range(f_count)]
    back_route = [(d, s) for s, d in out_route]

    add("out_route", (), lambda: w_out, lambda w: lax.ppermute(w, ("fsdp", "ctx"), out_route)[None])
    add("out_far", ("out_route",), lambda: [result("out_route")], lambda s: double_fsdp(s, top_bit, 2))
    add("out_near", ("out_far",), lambda: result("out_far"), lambda s: double_fsdp(s, 1, 1))
    add("down_a", (), lambda: w_down[:unit_half], away)
    add("down_b", (), lambda: w_down[unit_half:], away)
    add("columns", (), lambda: (w_gate, w_up), lambda w: columns_by_device(*w, mlp_scale, ff_block))
    add(
        "columns_all", ("columns",), lambda: result("columns"),
        lambda stack: exchange_all(stack).reshape(width, 2 * ff_block),
    )
    for j in range(4):
        add(f"move_{j}", ("columns_all",), lambda: result("columns_all"), lambda c, j=j: away(c[j * quarter : (j + 1) * quarter]))
    gather_rows = lambda rows: lax.all_gather(rows, "ctx", axis=0, tiled=True)
    add("own_cots", (), lambda: own_cot, gather_rows)
    add("cot_a", (), lambda: own_cot[:half], lambda rows: swap(rows, "fsdp", top_bit))
    add("cot_b", (), lambda: own_cot[half:], lambda rows: swap(rows, "fsdp", top_bit))
    add(
        "side_cots", ("cot_a", "cot_b"), lambda: (result("cot_a"), result("cot_b")),
        lambda parts: gather_rows(jnp.concatenate(parts, axis=0)),
    )

    (qkv_piece,) = barrier(0, qkv_piece)
    qkv_piece = exchange_ctx(qkv_piece).reshape(1, c_count * piece, qkv_width)
    small = positions
    for bit in [2 ** j for j in range(1, c_count.bit_length() - 1)] + [1]:
        small = jnp.concatenate([small, swap(small, "ctx", bit)], axis=0)
    int_places = small.reshape(-1)
    qkv_piece, near_tokens = barrier(1, qkv_piece, near_tokens)
    even_tokens = gather_far(own_tokens, near_tokens)
    qkv_parts = double_fsdp([qkv_piece], top_bit, 2)
    half_dim = HEAD_DIM // 2
    frequency = jnp.power(ROPE_BASE, -2.0 * jnp.arange(half_dim, dtype=WIDE) / HEAD_DIM)
    angles = int_places.astype(WIDE)[:, None] * frequency[None, :]
    cosine, sine = jnp.cos(angles), jnp.sin(angles)
    cosine = jnp.concatenate([cosine] * 4, axis=1)
    sine = jnp.concatenate([-sine, sine, -sine, sine], axis=1)
    qkv_parts, cosine, sine, even_tokens = barrier(2, qkv_parts, cosine, sine, even_tokens)
    quad_tokens, other_tokens = gather_core(even_tokens)
    qkv_parts = double_fsdp(qkv_parts, 1, 1)

    def first_norm(rows):
        rows = rows.astype(WIDE)
        return (rows * inverse_rms(rows)).astype(LOW)

    normed_first = [first_norm(quad_tokens), first_norm(other_tokens)]

    qkv_parts, normed_first = barrier(3, qkv_parts, normed_first)
    w_qkv = place(qkv_parts, f_order, f_index)
    qkv = jnp.concatenate([dot(rows, w_qkv) for rows in normed_first], axis=0)
    mixed, lse, q_scaled, k_rot, v_low = attention_forward(qkv, cosine, sine, int_places, heads)
    (mixed,) = barrier(4, mixed)

    w_out_rows = place(result("out_near"), f_order, f_index)
    middle = mixed.shape[0] // 2
    odd_out = scatter_core(dot(mixed[middle:], w_out_rows, out=LOW), COST["split_out"])
    even_out = dot(mixed[:middle], w_out_rows, out=LOW)
    odd_out, even_out = barrier(5, odd_out, even_out)
    state = scatter_far(scatter_sum(even_out, odd_out))
    inputs = own_tokens.astype(WIDE)
    inv_first = inverse_rms(inputs)
    hat_first = inputs * inv_first
    all_first = jnp.concatenate(normed_first, axis=0)
    state, hat_first, all_first = barrier(6, state, hat_first, all_first)
    (state,) = barrier(7, scatter_near(state))
    hidden = inputs + scatter_end(state)
    inv_second = inverse_rms(hidden)
    hat_second = hidden * inv_second
    normed_own = hat_second.astype(LOW)

    near_norm = gather_near(normed_own)
    side_norm = swap(normed_own, "fsdp", top_bit)
    near_norm, side_norm = barrier(8, near_norm, side_norm)
    even_norm = gather_far(normed_own, near_norm)
    near_side = gather_near(side_norm)
    norm_pieces = list(gather_core(even_norm))
    (norm_pieces,) = barrier(9, norm_pieces)
    columns = [result("columns_all")] + joined([result(f"move_{j}") for j in range(4)])
    downs = [w_down] + joined([result("down_a"), result("down_b")])
    table = jnp.array(c_order, jnp.int32) ^ c_index
    by_block = lambda rows: rows.reshape(c_count, tok_rows, width)

    weights = (table, columns, downs)
    *buffers, even_zero, odd_zero = feed_forward(0, *norm_pieces, by_block(result("own_cots")), *weights, [])
    near_side, buffers, even_zero, odd_zero = barrier(10, near_side, buffers, even_zero, odd_zero)
    side_norms = gather_core(gather_far(side_norm, near_side))
    quad_zero = scatter_sum(even_zero, scatter_core(odd_zero))
    side_norms, quad_zero, buffers, side_cots = barrier(
        11, side_norms, quad_zero, buffers, result("side_cots")
    )
    state_zero = scatter_far(quad_zero)
    *buffers, even_one, odd_one = feed_forward(1, *side_norms, by_block(side_cots), *weights, buffers)
    all_norms, all_cots, all_acts, all_lows = buffers

    product = lambda left, right: dot(left, right, ((0,), (0,)), LOW)
    add(
        "gate_away", (), lambda: (all_norms, all_lows),
        lambda p: [product(p[0], p[1][2 * j]) for j in blocks],
    )
    add(
        "up_away", (), lambda: (all_norms, all_lows),
        lambda p: [product(p[0], p[1][2 * j + 1]) for j in blocks],
    )
    add("down_away", (), lambda: (all_acts, all_cots), lambda p: [product(p[0][j], p[1]) for j in blocks])
    add("gate_own", (), lambda: (all_norms, all_lows), lambda p: product(p[0], p[1][0]))
    add("up_own", (), lambda: (all_norms, all_lows), lambda p: product(p[0], p[1][1]))
    move_back = lambda parts: [swap(part, "fsdp", r) for r, part in enumerate(parts, 1)]
    add("gate_move", ("gate_away",), lambda: result("gate_away"), move_back)
    add("up_move", ("up_away",), lambda: result("up_away"), move_back)
    add("down_move_a", ("down_away",), lambda: [p[:unit_half] for p in result("down_away")], move_back)
    add("down_move_b", ("down_away",), lambda: [p[unit_half:] for p in result("down_away")], move_back)
    add(
        "down_terms", (), lambda: all_acts,
        lambda acts: down_terms_by_device(acts, c_index, c_count, downs, tok_rows),
    )
    add(
        "out_rows", ("down_terms",), lambda: result("down_terms"),
        lambda t: lax.psum_scatter(t, "ctx", scatter_dimension=0, tiled=True).reshape(2, tok_rows, width),
    )
    add("side_out", ("out_rows",), lambda: result("out_rows")[1], lambda rows: swap(rows, "fsdp", top_bit))

    def sum_by_device(own, parts):
        total = sum([part.astype(WIDE) for part in parts], own.astype(WIDE)).astype(LOW)
        return total.reshape(devices, piece, ff_block)

    add(
        "both_all", ("gate_own", "gate_move", "up_own", "up_move"), lambda: [result(n) for n in ("gate_own", "gate_move", "up_own", "up_move")],
        lambda p: exchange_all(
            jnp.concatenate([sum_by_device(p[0], p[1]), sum_by_device(p[2], p[3])], axis=2)
        ),
    )
    add(
        "down_own", (), lambda: (all_acts, all_cots),
        lambda p: dot(p[0][0], p[1], ((0,), (0,))),
    )
    add(
        "assembled",
        ("both_all",),
        lambda: result("both_all"),
        lambda parts: assemble_columns(parts, w_gate, w_up, mlp_scale),
    )
    state_zero, odd_one, even_one = barrier(12, state_zero, odd_one, even_one)
    odd_one = scatter_core(odd_one)
    state_zero = scatter_near(state_zero)
    quad_one = scatter_sum(even_one, odd_one)
    quad_one, state_zero = barrier(13, quad_one, state_zero)
    (state_one,) = barrier(14, scatter_far(quad_one))
    (state_one,) = barrier(15, scatter_near(state_one))
    side_one = swap(scatter_end(state_one).astype(LOW), "fsdp", top_bit)
    (side_one,) = barrier(16, side_one)
    grad_normed = scatter_end(state_zero) + side_one.astype(WIDE)

    grad_hidden = own_cot.astype(WIDE) + norm_back(grad_normed, hat_second, inv_second)
    hidden_low = grad_hidden.astype(LOW)
    (near_hidden,) = barrier(17, gather_near(hidden_low))
    (even_hidden,) = barrier(18, gather_far(hidden_low, near_hidden))
    hidden_halves = gather_core(even_hidden, COST["split_hidden"])
    grad_mixed = jnp.concatenate([dot(h, w_out_rows, ((1,), (1,)), LOW) for h in hidden_halves], axis=0)

    def out_product(p):
        total = dot(p[0][:middle], p[1][0], ((0,), (0,))) + dot(p[0][middle:], p[1][1], ((0,), (0,)))
        return total.astype(LOW).reshape(f_count, piece, width)

    add("out_part", (), lambda: (mixed, hidden_halves), out_product)
    add("out_halved", ("out_part",), lambda: result("out_part"), lambda p: halve_near(p, f_index))
    add("out_sum", ("out_halved",), lambda: result("out_halved"), lambda p: halve_far(p, f_index, top_bit))
    add("out_grad", ("out_sum",), lambda: result("out_sum"), lambda p: lax.ppermute(p, ("fsdp", "ctx"), back_route))

    (grad_mixed,) = barrier(19, grad_mixed)
    grad_qkv = attention_backward(
        q_scaled, k_rot, v_low, grad_mixed, lse, cosine, sine, int_places, heads
    )
    grad_qkv, all_first = barrier(20, grad_qkv, all_first)

    qkv_part = dot(all_first, grad_qkv, ((0,), (0,)), LOW)
    qkv_part = qkv_part.reshape(f_count, c_count * piece, qkv_width)
    grad_qkv, qkv_part = tie(grad_qkv, qkv_part)
    qkv_sum = halve_near(qkv_part, f_index)
    (grad_qkv,) = barrier(21, grad_qkv)
    odd = scatter_core(dot(grad_qkv[middle:], w_qkv, ((1,), (1,)), LOW), COST["split_last"])
    even = dot(grad_qkv[:middle], w_qkv, ((1,), (1,)), LOW)
    quad = scatter_sum(even, odd)
    qkv_sum, quad = barrier(22, qkv_sum, quad)
    state = scatter_far(quad)
    qkv_sum = halve_far(qkv_sum, f_index, top_bit)
    state, qkv_sum = barrier(23, state, qkv_sum)
    qkv_sum = exchange_ctx(qkv_sum.reshape(c_count, piece, qkv_width))
    (state,) = barrier(24, scatter_near(state))
    (qkv_sum,) = barrier(25, qkv_sum)
    grad_normed = scatter_end(state)
    input_grad = grad_hidden + norm_back(grad_normed, hat_first, inv_first)
    gate_grad, up_grad, mlp_gain_grad = result("assembled")
    mlp_gain_grad = mlp_gain_grad[:, 0]
    out_grad = result("out_grad").astype(WIDE)
    down_grad = result("down_own")
    for part in joined([result("down_move_a"), result("down_move_b")]):
        down_grad = down_grad + part.astype(WIDE)
    side_out, out_rows = result("side_out"), result("out_rows")
    output = hidden + out_rows[0].astype(WIDE) + side_out.astype(WIDE)

    qkv_sum = qkv_sum.astype(WIDE)
    query_grad = qkv_sum[:, :, :q_width].transpose(1, 0, 2).reshape(piece, -1)
    kv_sum = qkv_sum[:, :, q_width:].reshape(KV_HEADS, kv_share, piece, 2, HEAD_DIM).sum(axis=1)
    key_grad = kv_sum[:, :, 0].transpose(1, 0, 2).reshape(piece, -1)
    value_grad = kv_sum[:, :, 1].transpose(1, 0, 2).reshape(piece, -1)
    attn_gain_grad = (
        jnp.sum(query_grad * w_query.astype(WIDE), axis=1)
        + jnp.sum(key_grad * w_key.astype(WIDE), axis=1)
        + jnp.sum(value_grad * w_value.astype(WIDE), axis=1)
    )
    query_grad, key_grad, value_grad = (g * attn_scale for g in (query_grad, key_grad, value_grad))

    return (
        output.astype(LOW)[None],
        input_grad.astype(LOW)[None],
        attn_gain_grad,
        query_grad,
        key_grad,
        value_grad,
        out_grad,
        mlp_gain_grad,
        gate_grad,
        up_grad,
        down_grad,
    )


def solution(mesh):
    rows = P(("fsdp", "ctx"), None)
    vector = P(("fsdp", "ctx"))
    tokens = P("fsdp", "ctx", None)
    in_specs = (
        tokens, P("fsdp", "ctx"), vector, rows, rows, rows, rows, vector, rows, rows, rows, tokens,
    )
    out_specs = (
        tokens, tokens, vector, rows, rows, rows, rows, vector, rows, rows, rows,
    )
    return jax.shard_map(
        per_device, mesh=mesh, in_specs=in_specs, out_specs=out_specs, check_vma=False
    )
```
